128 devices in a mesh: lat: 16 (over z, x_hi, core), lon: 8 (over y, x_lo).
Axes of the slice: x: 4 (x_hi: 2, x_lo: 2; x = x_hi * 2 + x_lo), y: 4, z: 4, core: 2. Of those that a mesh axis runs over, the one named last changes fastest.
Arguments:
- winds: float32 [2, 16, 1440, 2880], P(None, None, 'lat', 'lon'), may hold values from -6 to 6
- theta: float32 [16, 1440, 2880], P(None, 'lat', 'lon'), may hold values from -6 to 6
- thick: float32 [16, 1440, 2880], P(None, 'lat', 'lon'), may hold values from 0.5 to 1.5
- polar_rows: int32 [480], replicated, may hold values from 0 to 1439, as said below
- cutoffs: int32 [480], replicated, may hold values from 1 to 719, as said below
Outputs:
- new_winds: float32 [2, 16, 1440, 2880], P(None, None, 'lat', 'lon')
- new_theta: float32 [16, 1440, 2880], P(None, 'lat', 'lon')
- new_thick: float32 [16, 1440, 2880], P(None, 'lat', 'lon')
The draws below stay inside these ranges and needn't reach their ends.
Inputs may be any that keep to these rules, and one draw needn't show every extreme that they name: `polar_rows`: each row is listed once, in an order drawn from the seed. The listed rows are a run of rows from row 0 up together with a run of rows ending at row 1439; each run has between 180 and 300 rows, so no row of the middle half of the latitudes is listed. `cutoffs`: rows 0 and 1439 have cutoff 1, and the listed row of each run that lies farthest from its pole has cutoff 720 - 1. Any other listed row that lies d rows from its nearest pole (d = 0 at the pole) has a cutoff between min(d + 1, 719) and min(2 (d + 1), 719).
All inputs are finite; a program needn't handle non-finite values.
Results may differ from the reference program's by a relative error of at most 0.000071.
Values sent between devices are 32-bit elements; how exact they have to be, the bound alone decides.
A program may use at most 192 MiB of HBM per device.

```python
import jax
import jax.numpy as jnp
from jax import lax

NLON = 2880
LEV = 16
NLAT = 1440
KW = 720
NPOLE = 240
NF = 480


def polar_layout(key):
    north = jax.random.randint(key, (), NPOLE - NPOLE // 4, NPOLE + NPOLE // 4 + 1).astype(jnp.int32)
    place = jnp.arange(NF, dtype=jnp.int32)
    rows = jnp.where(place < north, place, NLAT - NF + place).astype(jnp.int32)
    order = jax.random.permutation(jax.random.fold_in(key, 5), NF)
    return (rows[order].astype(jnp.int32), north)


def draw_polar_rows(key, part):
    rows, north = polar_layout(key)
    return rows


def draw_cutoffs(key, part):
    rows, north = polar_layout(key)
    key = jax.random.fold_in(key, 23)
    depth = jnp.minimum(rows, NLAT - 1 - rows)
    lower = jnp.minimum(depth + 1, KW - 1)
    upper = jnp.minimum(2 * (depth + 1), KW - 1)
    drawn = jax.random.randint(key, (NF,), lower, upper + 1).astype(jnp.int32)
    deepest = (rows == north - 1) | (rows == NLAT - NF + north)
    drawn = jnp.where(deepest, KW - 1, drawn)
    drawn = jnp.where(depth == 0, 1, drawn)
    return drawn.astype(jnp.int32)


def steps_of(stream_key, shape, split, low, top_value):
    level, own = 1.0, jax.random.fold_in(stream_key, 6)
    for axis_at, blocks in split:
        steps = jnp.exp(jax.random.uniform(jax.random.fold_in(own, axis_at), (blocks,), jnp.float32, low / len(split), top_value / len(split)))
        level = level * jnp.repeat(steps, shape[axis_at] // blocks).reshape([-1 if axis == axis_at else 1 for axis in range(len(shape))])
    return level


def gaussian(rng, shape, width, reach, split=(), held_as=jnp.bfloat16):
    entries = jax.random.normal(rng, shape, jnp.float32) * width
    if len(split) > 0:
        entries = steps_of(rng, shape, split, -0.22, 0.18) * entries
    return jnp.clip(entries, min=-reach, max=reach).astype(held_as)


def setup_inputs(seed: int = 0) -> dict:
    key_of = jax.random.split(jax.random.key(seed), 6)
    return {
        "winds": gaussian(key_of[0], (2, LEV, NLAT, NLON), 1.0, 6.0, ((2, 16), (3, 8)), jnp.float32),
        "theta": gaussian(key_of[1], (LEV, NLAT, NLON), 1.0, 6.0, ((1, 16), (2, 8)), jnp.float32),
        "thick": jnp.clip(0.5 + 1.0 * jax.random.uniform(key_of[2], (LEV, NLAT, NLON), jnp.float32) ** steps_of(key_of[2], (LEV, NLAT, NLON), ((1, 16), (2, 8)), -0.2, 0.2), 0.5, 1.5),
        "polar_rows": draw_polar_rows(jax.random.fold_in(key_of[5], 71), 0),
        "cutoffs": draw_cutoffs(jax.random.fold_in(key_of[5], 71), 0),
    }


def truncate_row(field, keep, listed):
    spec = jnp.fft.rfft(field, axis=1)
    spec = jnp.where(keep, spec, jnp.zeros_like(spec))
    back = jnp.fft.irfft(spec, n=NLON, axis=1).astype(field.dtype)
    return jnp.where(listed[:, None], back, field)


def diff_lon(field):
    return (jnp.roll(field, -1, axis=1) - jnp.roll(field, 1, axis=1)) * 0.5


def diff_lat(field):
    padded = jnp.pad(field, ((1, 1), (0, 0)))
    return (padded[2:] - padded[:-2]) * 0.5


def reference(winds, theta, thick, polar_rows, cutoffs):
    cut_full = jnp.full((NLAT,), -1, jnp.int32).at[polar_rows].set(cutoffs)
    listed = cut_full >= 0
    wave = jnp.arange(NLON // 2 + 1, dtype=jnp.int32)
    keep = wave[None, :] <= cut_full[:, None]
    centre = (jnp.arange(NLAT, dtype=jnp.int32).astype(winds.dtype) + 0.5) * (jnp.pi / NLAT)
    coslat = jnp.sin(centre)[:, None]
    sinlat = (-jnp.cos(centre))[:, None]

    def level(fields):
        uu, vv, tt, hh = [truncate_row(f, keep, listed) for f in fields]
        new_h = hh - 0.05 * diff_lon(uu * hh) / coslat - 0.2 * diff_lat(vv * hh * coslat) / coslat
        new_t = tt - 0.05 * uu * diff_lon(tt) / coslat - 0.2 * vv * diff_lat(tt)
        new_u = uu - 0.05 * uu * diff_lon(uu) / coslat - 0.2 * vv * diff_lat(uu) - 0.1 * diff_lon(hh) / coslat + 0.3 * sinlat * vv
        new_v = vv - 0.05 * uu * diff_lon(vv) / coslat - 0.2 * vv * diff_lat(vv) - 0.3 * diff_lat(hh) - 0.3 * sinlat * uu
        return new_u, new_v, new_t, new_h

    outs = lax.map(level, (winds[0], winds[1], theta, thick))
    return jnp.stack([outs[0], outs[1]]), outs[2], outs[3]
```

```python
import functools

import jax
import jax.numpy as jnp
import numpy as np
from jax import lax
from jax.experimental import pallas as pl
from jax.experimental.pallas import tpu as pltpu
from jax.sharding import PartitionSpec as P

NLON = 2880
NLAT = 1440
LEV = 16
ROWS = 90
COLS = 360
PR = 96
PC = 384
NP = 8
FIELDS = 64
NCH = 4
CF = 2
NOFF = 0
SHIFT = 6
MESH = pl.DeviceIdType.MESH
F32 = jnp.float32
BF16 = jnp.bfloat16


def split(table):
    hi = table.astype(np.float32).astype(BF16)
    lo = (table - hi.astype(np.float64)).astype(np.float32).astype(BF16)
    return np.asarray(hi), np.asarray(lo)


@functools.lru_cache(maxsize=None)
def value_tables():
    q = np.arange(PC)
    q = np.where(q == PC - 1, -1, q)
    forward = np.zeros((4, 2 * PC, PC))
    inverse = np.zeros((4, PC, 2 * PC))
    waves = np.full((4, PC), 1e9)
    m = np.arange(90)
    for g in range(4):
        parts = [(0, 0, 0), (4, 1, 0)] if g == 0 else [(g, 0, 1), (8 - g, 0, -1)]
        for slot, (r, half, sign) in enumerate(parts):
            k = 8 * m + r
            angle = 2.0 * np.pi * ((k[:, None] * q[None, :]) % NLON) / NLON
            cos, sin = np.cos(angle), np.sin(angle)
            re = slice(slot * 180, slot * 180 + 90)
            im = slice(slot * 180 + 90, slot * 180 + 180)
            waves[g, re] = k
            waves[g, im] = k
            weight = np.where(k == 0, 1.0, 2.0)[:, None] / NLON
            own = np.zeros((PC, 2 * PC))
            if sign == 0:
                own[re, half * PC : (half + 1) * PC] = cos
                own[im, half * PC : (half + 1) * PC] = -sin
            else:
                own[re, :PC] = cos
                own[im, :PC] = -sin
                own[re, PC:] = sign * sin
                own[im, PC:] = sign * cos
            scaled = own.copy()
            scaled[re] *= weight
            scaled[im] *= weight
            inverse[g] += scaled
            keep = np.concatenate([np.arange(PC) < COLS] * 2)
            forward[g] += (own * keep[None, :]).T
    used = np.concatenate([(np.arange(PC) <= COLS) | (np.arange(PC) == PC - 1)] * 2)
    inverse = inverse * used[None, None, :]
    return split(forward) + split(inverse) + (waves.astype(np.float32),)


@functools.lru_cache(maxsize=None)
def packed_tables():
    lane = np.arange(PC)
    wave = (lane + 1) // 2
    is_cos = (lane == 0) | (lane % 2 == 1)
    q = np.arange(PC)
    q = np.where(q == PC - 1, -1, q)
    used = (np.arange(PC) <= COLS) | (np.arange(PC) == PC - 1)
    forward = np.zeros((NP, 2, PC, PC))
    inverse = np.zeros((NP, 2, PC, PC))
    for p in range(NP):
        n = COLS * p + q
        angle = 2.0 * np.pi * ((wave[:, None] * n[None, :]) % NLON) / NLON
        base = np.where(is_cos[:, None], np.cos(angle), np.sin(angle))
        weight = np.where(wave == 0, 1.0, 2.0)[:, None] / NLON
        back = base * weight * used[None, :]
        ahead = (base * (np.arange(PC) < COLS)[None, :]).T
        forward[p, 0], forward[p, 1] = ahead, ahead[:, ::-1]
        inverse[p, 0], inverse[p, 1] = back, back[::-1]
    waves = np.stack([wave, wave[::-1]]).astype(np.float32)
    return split(forward) + split(inverse) + (waves,)


def dot3(x, hi, lo):
    x_hi = x.astype(BF16)
    x_lo = (x - x_hi.astype(F32)).astype(BF16)
    total = jnp.dot(x_hi, lo, preferred_element_type=F32)
    total += jnp.dot(x_lo, hi, preferred_element_type=F32)
    return total + jnp.dot(x_hi, hi, preferred_element_type=F32)


def filter_kernel(
    w_ref, t_ref, h_ref, lim_ref, own_ref, wv_ref, wp_ref,
    thi_ref, tlo_ref, uhi_ref, ulo_ref, fhi_ref, flo_ref, ghi_ref, glo_ref,
    filt_ref, side_ref, edge_ref,
    thi, tlo, uhi, ulo, fhi, flo, ghi, glo,
    recv, ret, srecv, stage, xs, obuf, yb, zb, cols, rawedge, fedge, sedge,
    tab_sem, stage_sem, fsend, frecv, rsend, rrecv, ssend, srecv_sem, asend, arecv,
    hsend, hrecv, lsend, lrecv, esem, osem,
):
    lat = lax.axis_index("lat")
    lon = lax.axis_index("lon")
    north = lat < 8
    depth = jnp.where(north, lat, 15 - lat)
    partner = jnp.where(north, jnp.where(lat < 4, lat + 4, lat - 4), jnp.where(lat >= 12, lat - 4, lat + 4))
    is_packed = depth == 0
    is_value = (depth >= 1) & (depth <= 3)
    is_off = (depth >= 5) & (depth <= 7)
    served = jnp.where(is_off, partner, lat)
    fields_of = ((w_ref, 0, 4), (t_ref, 4, 2), (h_ref, 6, 2))

    bar = pltpu.get_barrier_semaphore()
    for i in range(1, NP):
        pl.semaphore_signal(bar, inc=1, device_id=(lat, lax.rem(lon + i, NP)), device_id_type=MESH)
    for i in (1, 15):
        pl.semaphore_signal(bar, inc=1, device_id=(lax.rem(lat + i, 16), lon), device_id_type=MESH)
    n_signals = 9
    if NOFF:
        for i in range(NP):
            pl.semaphore_signal(bar, inc=1, device_id=(partner, lax.rem(lon + i, NP)), device_id_type=MESH)
        n_signals += 8

    tables = ((thi_ref, thi), (tlo_ref, tlo), (uhi_ref, uhi), (ulo_ref, ulo))
    packs = ((fhi_ref, fhi), (flo_ref, flo), (ghi_ref, ghi), (glo_ref, glo))

    @pl.when(is_value | is_off)
    def _():
        for i, (src, dst) in enumerate(tables):
            pltpu.make_async_copy(src, dst, tab_sem.at[i]).start()

    @pl.when(is_packed)
    def _():
        for i, (src, dst) in enumerate(packs):
            pltpu.make_async_copy(src.at[lon], dst, tab_sem.at[i]).start()

    def stage_copy(g, slot):
        src, lo, _ = fields_of[0 if g < 4 else 1 if g < 6 else 2]
        return pltpu.make_async_copy(src.at[pl.ds((g - lo) * 8, 8)], stage.at[slot], stage_sem.at[slot])

    stage_copy(0, 0).start()
    xs[...] = jnp.zeros_like(xs)
    yb[...] = jnp.zeros_like(yb)
    cols[...] = jnp.zeros_like(cols)

    pl.semaphore_wait(bar, n_signals)

    def variants(fn):
        @pl.when((served != 3) & (served != 12))
        def _():
            fn(0, ROWS, PR)

        @pl.when(served == 3)
        def _():
            fn(0, 32, 32)

        @pl.when(served == 12)
        def _():
            fn(56, ROWS - 56, PR - 56)

    @pl.when(is_value)
    def _():
        def per_rows(r0, rn, _):
            def per_copy(n, carry):
                c = n // NP
                p = lax.rem(lon + n, NP)
                target = jnp.where(c < NOFF, partner, lat)
                local = (c >= NOFF) & (p == lon)
                for arr, lo, cnt in fields_of:
                    mine = (p >= lo) & (p < lo + cnt)
                    src = arr.at[pl.ds((p - lo) * 8 + c * CF, CF), r0 : r0 + rn]
                    dst = recv.at[c, lon, :, r0 : r0 + rn]

                    @pl.when(mine & jnp.logical_not(local))
                    def _():
                        pltpu.make_async_remote_copy(
                            src_ref=src, dst_ref=dst, send_sem=fsend.at[c, p],
                            recv_sem=frecv.at[c, lon], device_id=(target, p), device_id_type=MESH,
                        ).start()

                    @pl.when(mine & local)
                    def _():
                        pltpu.make_async_copy(src, dst, frecv.at[c, lon]).start()

                return carry

            lax.fori_loop(0, NCH * NP, per_copy, 0)

        variants(per_rows)

    @pl.when(is_packed)
    def _():
        for i, (src, dst) in enumerate(packs):
            pltpu.make_async_copy(src.at[lon], dst, tab_sem.at[i]).wait()

    lane = lax.broadcasted_iota(jnp.int32, (ROWS, 128), 1)

    def strips_to(g, dst_lon, slot):
        return pltpu.make_async_remote_copy(
            src_ref=ret.at[pl.ds(g * 8, 8), 0:48], dst_ref=srecv.at[pl.ds(slot * 8, 8)],
            send_sem=ssend.at[g], recv_sem=srecv_sem.at[slot],
            device_id=(lat, dst_lon), device_id_type=MESH,
        )

    for g in range(NP):
        slot = g % 2
        if g + 1 < NP:
            stage_copy(g + 1, 1 - slot).start()
        stage_copy(g, slot).wait()

        def columns(f, carry, g=g, slot=slot):
            at = g * 8 + f
            block = stage[slot, f]
            cur = cols[0:ROWS, :]
            cur = jnp.where(lane == at, block[:, 0:1], cur)
            cur = jnp.where(lane == at + FIELDS, block[:, COLS - 1 : COLS], cur)
            cols[0:ROWS, :] = cur
            return carry

        lax.fori_loop(0, 8, columns, 0)
        for f in range(8):
            rawedge[0, g * 8 + f : g * 8 + f + 1, 0:COLS] = stage[slot, f, 0:1, :]
            rawedge[1, g * 8 + f : g * 8 + f + 1, 0:COLS] = stage[slot, f, ROWS - 1 : ROWS, :]

        @pl.when(is_packed)
        def _(g=g, slot=slot):
            @pl.when(north)
            def _():
                xs[:, SHIFT : SHIFT + ROWS, 0:COLS] = stage[slot]

            @pl.when(jnp.logical_not(north))
            def _():
                xs[:, 0:ROWS, 0:COLS] = stage[slot]

            low = dot3(xs[:, 0:48, :].reshape(8 * 48, PC), fhi[0], flo[0]).reshape(8, 48, PC)
            high = dot3(xs[:, 48:96, :].reshape(8 * 48, PC), fhi[1], flo[1]).reshape(8, 48, PC)
            keep_low = wp_ref[0:1, :] <= lim_ref[0:48, 0:1]
            keep_high = wp_ref[1:2, :] <= lim_ref[48:96, 0:1]
            low = jnp.where(keep_low[None], low, 0.0)
            high = jnp.where(keep_high[None], high, 0.0)
            for t in range(6):
                ret[g * 8 : g * 8 + 8, 8 * t : 8 * t + 8, :] = (
                    low[:, 8 * t : 8 * t + 8, :] + high[:, 40 - 8 * t : 48 - 8 * t, :]
                )

            @pl.when(lon != g)
            def _():
                strips_to(g, g, lon).start()

            @pl.when(lon == g)
            def _():
                pltpu.make_async_copy(
                    ret.at[pl.ds(g * 8, 8), 0:48], srecv.at[pl.ds(g * 8, 8)], srecv_sem.at[g]
                ).start()

    def side_copy(i):
        step = 1 if i == 0 else NP - 1
        return pltpu.make_async_remote_copy(
            src_ref=cols, dst_ref=side_ref.at[i], send_sem=hsend.at[i], recv_sem=hrecv.at[i],
            device_id=(lat, lax.rem(lon + step, NP)), device_id_type=MESH,
        )

    side_copy(0).start()
    side_copy(1).start()

    @pl.when(is_packed)
    def _():
        def wait_part(s, carry):
            pltpu.make_async_copy(
                srecv.at[pl.ds(s * 8, 8)], srecv.at[pl.ds(s * 8, 8)], srecv_sem.at[s]
            ).wait()
            return carry

        lax.fori_loop(0, NP, wait_part, 0)

        def add(f, carry):
            total = srecv[f]
            for s in range(1, NP):
                total = total + srecv[s * 8 + f]
            ret[lon * 8 + f, 48:96, :] = total
            return carry

        lax.fori_loop(0, 8, add, 0)

        def sum_to(p):
            return pltpu.make_async_remote_copy(
                src_ref=ret.at[pl.ds(lon * 8, 8), 48:96], dst_ref=ret.at[pl.ds(lon * 8, 8), 48:96],
                send_sem=asend.at[p], recv_sem=arecv.at[lon],
                device_id=(lat, p), device_id_type=MESH,
            )

        def send(i, carry):
            sum_to(lax.rem(lon + i, NP)).start()
            return carry

        lax.fori_loop(1, NP, send, 0)

        def out_copy(g, slot):
            return pltpu.make_async_copy(obuf.at[slot], filt_ref.at[pl.ds(g * 8, 8)], osem.at[slot])

        def back(i, carry):
            g = lax.rem(lon + i, NP)
            slot = lax.rem(i, 2)

            @pl.when(i > 0)
            def _():
                pltpu.make_async_copy(
                    ret.at[pl.ds(g * 8, 8), 48:96], ret.at[pl.ds(g * 8, 8), 48:96], arecv.at[g]
                ).wait()

            @pl.when(i >= 2)
            def _():
                out_copy(g, slot).wait()

            spec = ret[pl.ds(g * 8, 8), 48:96, :]
            keep_low = wp_ref[0:1, :] <= lim_ref[0:48, 0:1]
            low = jnp.where(keep_low[None], spec, 0.0).reshape(8 * 48, PC)
            low = dot3(low, ghi[0], glo[0]).reshape(8, 48, PC)
            keep_high = wp_ref[1:2, :] <= lim_ref[48:96, 0:1]
            flipped = jnp.concatenate([spec[:, 40 - 8 * t : 48 - 8 * t, :] for t in range(6)], axis=1)
            high = jnp.where(keep_high[None], flipped, 0.0).reshape(8 * 48, PC)
            high = dot3(high, ghi[1], glo[1]).reshape(8, 48, PC)

            @pl.when(north)
            def _():
                obuf[slot, :, 0 : 48 - SHIFT, :] = low[:, SHIFT:48, :]
                obuf[slot, :, 48 - SHIFT : ROWS, :] = high

            @pl.when(jnp.logical_not(north))
            def _():
                obuf[slot, :, 0:48, :] = low
                obuf[slot, :, 48:96, :] = high

            out_copy(g, slot).start()
            return carry

        lax.fori_loop(0, NP, back, 0)
        for slot in range(2):
            out_copy(0, slot).wait()

        def sent(i, carry):
            p = lax.rem(lon + i, NP)
            sum_to(p).wait_send()
            strips_to(p, p, lon).wait_send()
            return carry

        lax.fori_loop(1, NP, sent, 0)

    @pl.when(is_value | is_off)
    def _():
        for i, (src, dst) in enumerate(tables):
            pltpu.make_async_copy(src, dst, tab_sem.at[i]).wait()

        first = jnp.where(is_off, 0, NOFF)
        last = jnp.where(is_off, NOFF, NCH)
        half = np.float32(np.sqrt(0.5))

        def chunk(c, carry):
            def arrived(r0, rn, _):
                def wait_one(s, carry):
                    ref = recv.at[c, s, :, r0 : r0 + rn]
                    pltpu.make_async_copy(ref, ref, frecv.at[c, s]).wait()
                    return carry

                lax.fori_loop(0, NP, wait_one, 0)

            variants(arrived)

            def fold(f, carry):
                row0 = pl.multiple_of(f * PR, PR)
                rows = pl.ds(row0, ROWS)
                x = [recv[c, s, f] for s in range(NP)]
                s0, s1, s2, s3 = [x[j] + x[j + 4] for j in range(4)]
                d0, d1, d2, d3 = [x[j] - x[j + 4] for j in range(4)]
                plus, minus = half * (d1 + d3), half * (d1 - d3)
                out = (
                    (s0 + s2) + (s1 + s3), (s0 + s2) - (s1 + s3),
                    d0 + minus, -(d2 + plus),
                    s0 - s2, s3 - s1,
                    d0 - minus, d2 - plus,
                )
                for i in range(8):
                    yb[i, rows, 0:COLS] = out[i]
                return carry

            lax.fori_loop(0, CF, fold, 0)

            def group(g, carry):
                spec = dot3(yb[2 * g], thi[g, 0:PC, :], tlo[g, 0:PC, :])
                spec += dot3(yb[2 * g + 1], thi[g, PC:, :], tlo[g, PC:, :])
                keep = wv_ref[g] <= lim_ref[:, 0:1]
                spec = jnp.where(keep[None], spec.reshape(CF, PR, PC), 0.0).reshape(CF * PR, PC)
                zb[2 * g] = dot3(spec, uhi[g, :, 0:PC], ulo[g, :, 0:PC])
                zb[2 * g + 1] = dot3(spec, uhi[g, :, PC:], ulo[g, :, PC:])
                return carry

            lax.fori_loop(0, 4, group, 0)

            def unfold(f, carry):
                rows = pl.ds(pl.multiple_of(f * PR, PR), PR)
                a0, b0, a1, b1, a2, b2, a3, b3 = [zb[i, rows, :] for i in range(8)]
                even = (a0 + b0 + a2, a0 - b0 - b2, a0 + b0 - a2, a0 - b0 + b2)
                odd = (a1 + a3, half * ((a1 - a3) - (b1 + b3)), b3 - b1, half * ((a3 - a1) - (b1 + b3)))
                for j in range(4):
                    ret[(c * NP + j) * CF + f] = even[j] + odd[j]
                    ret[(c * NP + j + 4) * CF + f] = even[j] - odd[j]
                return carry

            lax.fori_loop(0, CF, unfold, 0)

            def give_back(r0, _, rn):
                def one(i, carry):
                    p = lax.rem(lon + i, NP)
                    src = ret.at[pl.ds((c * NP + p) * CF, CF), r0 : r0 + rn]
                    dst = filt_ref.at[pl.ds(lon * 8 + c * CF, CF), r0 : r0 + rn]
                    local = is_value & (p == lon)

                    @pl.when(jnp.logical_not(local))
                    def _():
                        pltpu.make_async_remote_copy(
                            src_ref=src, dst_ref=dst, send_sem=rsend.at[c, p],
                            recv_sem=rrecv.at[c, lon], device_id=(served, p), device_id_type=MESH,
                        ).start()

                    @pl.when(local)
                    def _():
                        pltpu.make_async_copy(src, dst, rrecv.at[c, lon]).start()

                    return carry

                lax.fori_loop(0, NP, one, 0)

            variants(give_back)
            return carry

        lax.fori_loop(first, last, chunk, 0)

        def drain_returns(r0, _, rn):
            def one(n, carry):
                c = first + n // NP
                p = lax.rem(n, NP)
                src = ret.at[pl.ds((c * NP + p) * CF, CF), r0 : r0 + rn]

                @pl.when(jnp.logical_not(is_value & (p == lon)))
                def _():
                    pltpu.make_async_copy(src, src, rsend.at[c, p]).wait()

                return carry

            lax.fori_loop(0, (last - first) * NP, one, 0)

        variants(drain_returns)

    @pl.when(is_value)
    def _():
        def drain(r0, rn, rb):
            def one(n, carry):
                c = n // NP
                p = lax.rem(n, NP)
                src = recv.at[c, p, :, r0 : r0 + rn]
                dst = filt_ref.at[pl.ds(p * 8 + c * CF, CF), r0 : r0 + rb]

                @pl.when((c < NOFF) | (p != lon))
                def _():
                    pltpu.make_async_copy(src, src, fsend.at[c, p]).wait()

                pltpu.make_async_copy(dst, dst, rrecv.at[c, p]).wait()
                return carry

            lax.fori_loop(0, NCH * NP, one, 0)

        variants(drain)

    sedge[...] = rawedge[...]

    @pl.when(depth <= 3)
    def _():
        for i, r0 in enumerate((0, 88)):
            pltpu.make_async_copy(filt_ref.at[:, r0 : r0 + 8], fedge.at[i], esem.at[i]).start()
        for i, (r0, row) in enumerate(((0, 0), (88, ROWS - 1))):
            pltpu.make_async_copy(filt_ref.at[:, r0 : r0 + 8], fedge.at[i], esem.at[i]).wait()
            keep = own_ref[row : row + 1, 0:1] >= 0.0
            for f in range(FIELDS):
                sedge[i, f : f + 1, :] = jnp.where(
                    keep, fedge[i, f, row - r0 : row - r0 + 1, :], rawedge[i, f : f + 1, :]
                )

    def edge_copy(i):
        step = 15 if i == 0 else 1
        return pltpu.make_async_remote_copy(
            src_ref=sedge.at[i], dst_ref=edge_ref.at[i], send_sem=lsend.at[i], recv_sem=lrecv.at[i],
            device_id=(lax.rem(lat + step, 16), lon), device_id_type=MESH,
        )

    edge_copy(0).start()
    edge_copy(1).start()
    side_copy(0).wait()
    side_copy(1).wait()
    edge_copy(0).wait()
    edge_copy(1).wait()


def stencil_kernel(
    u_ref, v_ref, t_ref, h_ref, fu_ref, fv_ref, ft_ref, fh_ref, side_ref, edge_ref, row_ref,
    wind_out, t_out, h_out, st,
):
    level = pl.program_id(0)
    lat = lax.axis_index("lat")
    listed = row_ref[0, :, 0:1] >= 0.0
    lane = lax.broadcasted_iota(jnp.int32, (PR, 128), 1)
    row = lax.broadcasted_iota(jnp.int32, (PR, PC), 0)
    has_north = lat > 0
    has_south = lat < 15
    state = []
    for k, (raw, smooth) in enumerate(((u_ref, fu_ref), (v_ref, fv_ref), (t_ref, ft_ref), (h_ref, fh_ref))):
        f = k * LEV + level
        st[k, 0:ROWS, 0:COLS] = raw[0]
        east = jnp.sum(jnp.where(lane == f, side_ref[1], 0.0), axis=1, keepdims=True)
        west = jnp.sum(jnp.where(lane == f + FIELDS, side_ref[0], 0.0), axis=1, keepdims=True)
        tail = st[k, :, 256:PC]
        tail = jnp.where(lane == COLS - 256, east, tail)
        tail = jnp.where(lane == 127, west, tail)
        st[k, :, 256:PC] = tail
        field = jnp.where(listed, smooth[0], st[k])
        above = jnp.where(has_north, edge_ref[1, pl.ds(f, 1), :], 0.0)
        below = jnp.where(has_south, edge_ref[0, pl.ds(f, 1), :], 0.0)
        field = jnp.where(row == ROWS, below, field)
        field = jnp.where(row == PR - 1, above, field)
        state.append(field)
    u, v, t, h = state
    cos = row_ref[1, :, 0:1]
    inv = row_ref[2, :, 0:1]
    sin = row_ref[3, :, 0:1]

    def dx(a):
        return (pltpu.roll(a, PC - 1, 1) - pltpu.roll(a, 1, 1)) * 0.5

    def dy(a):
        return (pltpu.roll(a, PR - 1, 0) - pltpu.roll(a, 1, 0)) * 0.5

    cu = 0.05 * u * inv
    cv = 0.2 * v
    new_h = h - (0.05 * inv) * dx(u * h) - (0.2 * inv) * dy(v * h * cos)
    new_t = t - cu * dx(t) - cv * dy(t)
    new_u = u - cu * dx(u) - cv * dy(u) - (0.1 * inv) * dx(h) + (0.3 * sin) * v
    new_v = v - cu * dx(v) - cv * dy(v) - 0.3 * dy(h) - (0.3 * sin) * u
    wind_out[0, 0] = new_u[0:ROWS, 0:COLS]
    wind_out[1, 0] = new_v[0:ROWS, 0:COLS]
    t_out[0] = new_t[0:ROWS, 0:COLS]
    h_out[0] = new_h[0:ROWS, 0:COLS]


def limits(first_row, polar_rows, cutoffs):
    rows = first_row + jnp.arange(PR, dtype=jnp.int32)
    hits = polar_rows[None, :] == rows[:, None]
    limit = jnp.max(jnp.where(hits, cutoffs[None, :], -1), axis=1).astype(F32)
    return jnp.broadcast_to(limit[:, None], (PR, 128))


def body(winds, theta, thick, polar_rows, cutoffs):
    lat = lax.axis_index("lat")
    served = jnp.where((lat >= 4) & (lat < 8), lat - 4, jnp.where((lat >= 8) & (lat < 12), lat + 4, lat))
    shift = jnp.where(lat == 0, SHIFT, 0)
    lim = limits(served * ROWS - shift, polar_rows, cutoffs)
    own = limits(lat * ROWS, polar_rows, cutoffs)
    thi, tlo, uhi, ulo, wv = value_tables()
    fhi, flo, ghi, glo, wp = packed_tables()
    vm = pl.BlockSpec(memory_space=pltpu.VMEM)
    hbm = pl.BlockSpec(memory_space=pl.ANY)
    dma = pltpu.SemaphoreType.DMA
    filt, side, edge = pl.pallas_call(
        filter_kernel,
        out_shape=(
            jax.ShapeDtypeStruct((FIELDS, PR, PC), F32),
            jax.ShapeDtypeStruct((2, PR, 128), F32),
            jax.ShapeDtypeStruct((2, FIELDS, PC), F32),
        ),
        in_specs=[hbm, hbm, hbm, vm, vm, vm, vm] + [hbm] * 8,
        out_specs=(hbm, hbm, hbm),
        scratch_shapes=[
            pltpu.VMEM((4, 2 * PC, PC), BF16), pltpu.VMEM((4, 2 * PC, PC), BF16),
            pltpu.VMEM((4, PC, 2 * PC), BF16), pltpu.VMEM((4, PC, 2 * PC), BF16),
            pltpu.VMEM((2, PC, PC), BF16), pltpu.VMEM((2, PC, PC), BF16),
            pltpu.VMEM((2, PC, PC), BF16), pltpu.VMEM((2, PC, PC), BF16),
            pltpu.VMEM((NCH, NP, CF, ROWS, COLS), F32),
            pltpu.VMEM((FIELDS, PR, PC), F32),
            pltpu.VMEM((FIELDS, 48, PC), F32),
            pltpu.VMEM((2, 8, ROWS, COLS), F32),
            pltpu.VMEM((8, PR, PC), F32),
            pltpu.VMEM((2, 8, PR, PC), F32),
            pltpu.VMEM((8, CF * PR, PC), F32),
            pltpu.VMEM((8, CF * PR, PC), F32),
            pltpu.VMEM((PR, 128), F32),
            pltpu.VMEM((2, FIELDS, PC), F32),
            pltpu.VMEM((2, FIELDS, 8, PC), F32),
            pltpu.VMEM((2, FIELDS, PC), F32),
            dma((4,)), dma((2,)),
            dma((NCH, NP)), dma((NCH, NP)), dma((NCH, NP)), dma((NCH, NP)),
            dma((NP,)), dma((NP,)), dma((NP,)), dma((NP,)),
            dma((2,)), dma((2,)), dma((2,)), dma((2,)), dma((2,)), dma((2,)),
        ],
        compiler_params=pltpu.CompilerParams(
            collective_id=1, has_side_effects=True, vmem_limit_bytes=58 * 2**20
        ),
        name="polar_filter",
    )(
        winds.reshape(2 * LEV, ROWS, COLS), theta, thick, lim, own,
        jnp.asarray(wv)[:, None, :], jnp.asarray(wp), thi, tlo, uhi, ulo, fhi, flo, ghi, glo,
    )

    rows = jnp.arange(PR, dtype=jnp.int32)
    rows = lat * ROWS + jnp.where(rows == PR - 1, -1, rows)
    angle = (rows.astype(F32) + 0.5) * (jnp.pi / NLAT)
    cos, sin = jnp.sin(angle), -jnp.cos(angle)
    trig = jnp.stack([cos, 1.0 / cos, sin])
    row_info = jnp.concatenate([own[None], jnp.broadcast_to(trig[:, :, None], (3, PR, 128))], axis=0)

    def raw(block):
        return pl.BlockSpec((1, ROWS, COLS), lambda l: (l + block, 0, 0))

    def smooth(block):
        return pl.BlockSpec((1, PR, PC), lambda l: (l + block, 0, 0))

    def whole(*shape):
        return pl.BlockSpec(shape, lambda l: (0,) * len(shape))

    flat = winds.reshape(2 * LEV, ROWS, COLS)
    return pl.pallas_call(
        stencil_kernel,
        grid=(LEV,),
        out_shape=(
            jax.ShapeDtypeStruct((2, LEV, ROWS, COLS), F32),
            jax.ShapeDtypeStruct((LEV, ROWS, COLS), F32),
            jax.ShapeDtypeStruct((LEV, ROWS, COLS), F32),
        ),
        in_specs=[
            raw(0), raw(LEV), raw(0), raw(0), smooth(0), smooth(LEV), smooth(2 * LEV), smooth(3 * LEV),
            whole(2, PR, 128), whole(2, FIELDS, PC), whole(4, PR, 128),
        ],
        out_specs=(
            pl.BlockSpec((2, 1, ROWS, COLS), lambda l: (0, l, 0, 0)),
            pl.BlockSpec((1, ROWS, COLS), lambda l: (l, 0, 0)),
            pl.BlockSpec((1, ROWS, COLS), lambda l: (l, 0, 0)),
        ),
        scratch_shapes=[pltpu.VMEM((4, PR, PC), F32)],
        compiler_params=pltpu.CompilerParams(vmem_limit_bytes=32 * 2**20),
        name="stencil",
    )(flat, flat, theta, thick, filt, filt, filt, filt, side, edge, row_info)


def solution(mesh):
    in_specs = (P(None, None, "lat", "lon"), P(None, "lat", "lon"), P(None, "lat", "lon"), P(), P())
    out_specs = (P(None, None, "lat", "lon"), P(None, "lat", "lon"), P(None, "lat", "lon"))
    return jax.shard_map(body, mesh=mesh, in_specs=in_specs, out_specs=out_specs, check_vma=False)
```

```python
import functools

import jax
import jax.numpy as jnp
import numpy as np
from jax import lax
from jax.experimental import pallas as pl
from jax.experimental.pallas import tpu as pltpu
from jax.sharding import PartitionSpec as P

NLON = 2880
NLAT = 1440
LEV = 16
ROWS = 90
COLS = 360
HALF = ROWS // 2
PC = 384
NP = 8
SUB = 8
NCH = 6
CR = ROWS // NCH
OFF1 = 0
OFF2 = 0
BLOCK = 9
MESH = pl.DeviceIdType.MESH
F32 = jnp.float32
BF16 = jnp.bfloat16


def split(table):
    hi = table.astype(np.float32).astype(BF16)
    lo = (table - hi.astype(np.float64)).astype(np.float32).astype(BF16)
    return np.asarray(hi), np.asarray(lo)


@functools.lru_cache(maxsize=None)
def value_tables():
    q = np.arange(PC)
    q = np.where(q == PC - 1, -1, q)
    forward = np.zeros((4, 2 * PC, PC))
    inverse = np.zeros((4, PC, 2 * PC))
    waves = np.full((4, PC), 1e9)
    m = np.arange(90)
    for g in range(4):
        parts = [(0, 0, 0), (4, 1, 0)] if g == 0 else [(g, 0, 1), (8 - g, 0, -1)]
        for slot, (r, half, sign) in enumerate(parts):
            k = 8 * m + r
            angle = 2.0 * np.pi * ((k[:, None] * q[None, :]) % NLON) / NLON
            cos, sin = np.cos(angle), np.sin(angle)
            re = slice(slot * 180, slot * 180 + 90)
            im = slice(slot * 180 + 90, slot * 180 + 180)
            waves[g, re] = k
            waves[g, im] = k
            weight = np.where(k == 0, 1.0, 2.0)[:, None] / NLON
            own = np.zeros((PC, 2 * PC))
            if sign == 0:
                own[re, half * PC : (half + 1) * PC] = cos
                own[im, half * PC : (half + 1) * PC] = -sin
            else:
                own[re, :PC] = cos
                own[im, :PC] = -sin
                own[re, PC:] = sign * sin
                own[im, PC:] = sign * cos
            scaled = own.copy()
            scaled[re] *= weight
            scaled[im] *= weight
            inverse[g] += scaled
            keep = np.concatenate([np.arange(PC) < COLS] * 2)
            forward[g] += (own * keep[None, :]).T
    used = np.concatenate([(np.arange(PC) <= COLS) | (np.arange(PC) == PC - 1)] * 2)
    inverse = inverse * used[None, None, :]
    return split(forward) + split(inverse) + (waves.astype(np.float32),)


@functools.lru_cache(maxsize=None)
def packed_tables():
    lane = np.arange(PC)
    wave = (lane + 1) // 2
    is_cos = (lane == 0) | (lane % 2 == 1)
    q = np.arange(PC)
    q = np.where(q == PC - 1, -1, q)
    used = (np.arange(PC) <= COLS) | (np.arange(PC) == PC - 1)
    forward = np.zeros((NP, 2, PC, PC))
    inverse = np.zeros((NP, 2, PC, PC))
    for p in range(NP):
        n = COLS * p + q
        angle = 2.0 * np.pi * ((wave[:, None] * n[None, :]) % NLON) / NLON
        base = np.where(is_cos[:, None], np.cos(angle), np.sin(angle))
        weight = np.where(wave == 0, 1.0, 2.0)[:, None] / NLON
        back = base * weight * used[None, :]
        ahead = (base * (np.arange(PC) < COLS)[None, :]).T
        forward[p, 0], forward[p, 1] = ahead, ahead[:, ::-1]
        inverse[p, 0], inverse[p, 1] = back, back[::-1]
    waves = np.stack([wave, wave[::-1]]).astype(np.float32)
    return split(forward) + split(inverse) + (waves,)


def dot3(x, hi, lo):
    x_hi = x.astype(BF16)
    x_lo = (x - x_hi.astype(F32)).astype(BF16)
    total = jnp.dot(x_hi, lo, preferred_element_type=F32)
    total += jnp.dot(x_lo, hi, preferred_element_type=F32)
    return total + jnp.dot(x_hi, hi, preferred_element_type=F32)


def wide(lim):
    return jnp.concatenate([lim, lim, lim], axis=-1)


def filter_kernel(
    w_ref, t_ref, h_ref, lim_ref, wv_ref, wp_ref,
    thi_ref, tlo_ref, uhi_ref, ulo_ref, fhi_ref, flo_ref, ghi_ref, glo_ref,
    state_ref,
    thi, tlo, uhi, ulo, fhi, flo, ghi, glo,
    recv, ret, strips, srecv, arecv, stage, obuf, xs, yb, zb, rawp, cols, side, zero,
    tab_sem, stage_sem, fsend, frecv, rsend, rrecv, ssend, srecv_sem, asend, arecv_sem,
    hsend, hrecv, lsend, lrecv, osem, zsem,
):
    lat = lax.axis_index("lat")
    lon = lax.axis_index("lon")
    north = lat < 8
    depth = jnp.where(north, lat, 15 - lat)
    partner = jnp.where(north, jnp.where(lat < 4, lat + 4, lat - 4), jnp.where(lat >= 12, lat - 4, lat + 4))
    is_packed = depth == 0
    is_value = (depth >= 1) & (depth <= 3)
    is_off = (depth == 5) | (depth == 6)
    served = jnp.where(is_off, partner, lat)
    served_depth = jnp.where(is_off, depth - 4, depth)
    n_off = jnp.where(served_depth == 1, OFF1, jnp.where(served_depth == 2, OFF2, 0))
    begin = jnp.where(served == 12, 2 * NCH // 3, 0)
    end = jnp.where(served == 3, NCH // 3, NCH)
    first = jnp.where(is_off, 0, jnp.maximum(begin, n_off))
    last = jnp.where(is_off, n_off, end)
    sources = (w_ref.at[0], w_ref.at[1], t_ref, h_ref)

    bar = pltpu.get_barrier_semaphore()
    for i in range(1, NP):
        pl.semaphore_signal(bar, inc=1, device_id=(lat, lax.rem(lon + i, NP)), device_id_type=MESH)
    for i in (1, 15):
        pl.semaphore_signal(bar, inc=1, device_id=(lax.rem(lat + i, 16), lon), device_id_type=MESH)
    n_signals = 9
    if OFF1 or OFF2:
        for i in range(NP):
            pl.semaphore_signal(bar, inc=1, device_id=(partner, lax.rem(lon + i, NP)), device_id_type=MESH)
        n_signals += NP

    tables = ((thi_ref, thi), (tlo_ref, tlo), (uhi_ref, uhi), (ulo_ref, ulo))
    packs = ((fhi_ref, fhi), (flo_ref, flo), (ghi_ref, ghi), (glo_ref, glo))

    @pl.when(is_packed)
    def _():
        for i, (src, dst) in enumerate(packs):
            pltpu.make_async_copy(src.at[lon], dst, tab_sem.at[i]).start()

    def part(g, rows):
        return sources[g // 2].at[rows, 8 * (g % 2) : 8 * (g % 2) + 8]

    def stage_copy(g, slot):
        return pltpu.make_async_copy(part(g, slice(0, ROWS)), stage.at[slot], stage_sem.at[slot])

    def state_part(p, start, count):
        return state_ref.at[p // 2, pl.ds(start, count), pl.ds(pl.multiple_of(lax.rem(p, 2) * 8, 8), 8)]

    @pl.when(is_packed | (depth >= 3))
    def _():
        stage_copy(0, 0).start()

    pl.semaphore_wait(bar, n_signals)

    @pl.when(is_value)
    def _():
        def per_copy(n, carry):
            c = begin + n // NP
            p = lax.rem(lon + n, NP)
            target = jnp.where(c < n_off, partner, lat)
            local = (c >= n_off) & (p == lon)
            dst = recv.at[c, lon]
            for g in range(NP):
                src = part(g, pl.ds(c * CR, CR))

                @pl.when((p == g) & jnp.logical_not(local))
                def _(src=src):
                    pltpu.make_async_remote_copy(
                        src_ref=src, dst_ref=dst, send_sem=fsend.at[c, p],
                        recv_sem=frecv.at[c, lon], device_id=(target, p), device_id_type=MESH,
                    ).start()

                @pl.when((p == g) & local)
                def _(src=src):
                    pltpu.make_async_copy(src, dst, frecv.at[c, lon]).start()

            return carry

        lax.fori_loop(0, (end - begin) * NP, per_copy, 0)

    @pl.when(is_value | is_off)
    def _():
        for i, (src, dst) in enumerate(tables):
            pltpu.make_async_copy(src, dst, tab_sem.at[i]).start()
        yb[...] = jnp.zeros_like(yb)

    def strip_copy(p):
        return pltpu.make_async_remote_copy(
            src_ref=strips.at[p], dst_ref=srecv.at[lon], send_sem=ssend.at[p],
            recv_sem=srecv_sem.at[lon], device_id=(lat, p), device_id_type=MESH,
        )

    @pl.when(is_packed)
    def _():
        xs[...] = jnp.zeros_like(xs)
        for i, (src, dst) in enumerate(packs):
            pltpu.make_async_copy(src.at[lon], dst, tab_sem.at[i]).wait()
        for g in range(NP):
            slot = g % 2
            if g + 1 < NP:
                stage_copy(g + 1, 1 - slot).start()
            stage_copy(g, slot).wait()
            xs[:, 0:COLS] = stage[slot].reshape(ROWS * SUB, COLS)
            low = dot3(xs[0 : HALF * SUB, :], fhi[0], flo[0]).reshape(HALF, SUB, PC)
            strips[g] = jnp.where(wp_ref[0:1, :] <= wide(lim_ref[0:HALF]), low, 0.0)
            high = dot3(xs[HALF * SUB :, :], fhi[1], flo[1]).reshape(HALF, SUB, PC)
            obuf[slot, 0:HALF] = jnp.where(wp_ref[1:2, :] <= wide(lim_ref[HALF:]), high, 0.0)

            def pair(i, carry, g=g, slot=slot):
                strips[g, i] += obuf[slot, HALF - 1 - i]
                return carry

            lax.fori_loop(0, HALF, pair, 0)

            @pl.when(lon != g)
            def _(g=g):
                strip_copy(g).start()

            @pl.when(lon == g)
            def _(g=g):
                pltpu.make_async_copy(strips.at[g], srecv.at[g], srecv_sem.at[g]).start()

        def wait_part(s, carry):
            pltpu.make_async_copy(srecv.at[s], srecv.at[s], srecv_sem.at[s]).wait()
            return carry

        lax.fori_loop(0, NP, wait_part, 0)

        def add(i, carry):
            total = srecv[0, i]
            for s in range(1, NP):
                total = total + srecv[s, i]
            arecv[lon, i] = total
            return carry

        lax.fori_loop(0, HALF, add, 0)

        def sum_to(p):
            return pltpu.make_async_remote_copy(
                src_ref=arecv.at[lon], dst_ref=arecv.at[lon], send_sem=asend.at[p],
                recv_sem=arecv_sem.at[lon], device_id=(lat, p), device_id_type=MESH,
            )

        def send(i, carry):
            sum_to(lax.rem(lon + i, NP)).start()
            return carry

        lax.fori_loop(1, NP, send, 0)

        def out_copy(p, slot):
            return pltpu.make_async_copy(obuf.at[slot], state_part(p, 1, ROWS), osem.at[slot])

        def back(i, carry):
            g = lax.rem(lon + i, NP)
            slot = lax.rem(i, 2)

            @pl.when(i > 0)
            def _():
                pltpu.make_async_copy(arecv.at[g], arecv.at[g], arecv_sem.at[g]).wait()

            @pl.when(i >= 2)
            def _():
                out_copy(g, slot).wait()

            spec = arecv[g]
            low = jnp.where(wp_ref[0:1, :] <= wide(lim_ref[0:HALF]), spec, 0.0).reshape(HALF * SUB, PC)
            obuf[slot, 0:HALF] = dot3(low, ghi[0], glo[0]).reshape(HALF, SUB, PC)

            def flip(j, carry):
                xs[pl.ds(pl.multiple_of(j * SUB, SUB), SUB), :] = arecv[g, HALF - 1 - j]
                return carry

            lax.fori_loop(0, HALF, flip, 0)
            high = xs[0 : HALF * SUB, :].reshape(HALF, SUB, PC)
            high = jnp.where(wp_ref[1:2, :] <= wide(lim_ref[HALF:]), high, 0.0).reshape(HALF * SUB, PC)
            obuf[slot, HALF:ROWS] = dot3(high, ghi[1], glo[1]).reshape(HALF, SUB, PC)
            out_copy(g, slot).start()
            return carry

        lax.fori_loop(0, NP, back, 0)
        for slot in range(2):
            out_copy(0, slot).wait()

        def sent(i, carry):
            p = lax.rem(lon + i, NP)
            sum_to(p).wait_send()
            strip_copy(p).wait_send()
            return carry

        lax.fori_loop(1, NP, sent, 0)

    @pl.when(is_value | is_off)
    def _():
        for i, (src, dst) in enumerate(tables):
            pltpu.make_async_copy(src, dst, tab_sem.at[i]).wait()

        half = np.float32(np.sqrt(0.5))

        def chunk(c, carry):
            def arrived(s, carry):
                pltpu.make_async_copy(recv.at[c, s], recv.at[c, s], frecv.at[c, s]).wait()
                return carry

            lax.fori_loop(0, NP, arrived, 0)

            def fold(r, carry):
                rows = pl.ds(pl.multiple_of(r * SUB, SUB), SUB)
                x = [recv[c, s, r] for s in range(NP)]
                s0, s1, s2, s3 = [x[j] + x[j + 4] for j in range(4)]
                d0, d1, d2, d3 = [x[j] - x[j + 4] for j in range(4)]
                plus, minus = half * (d1 + d3), half * (d1 - d3)
                out = (
                    (s0 + s2) + (s1 + s3), (s0 + s2) - (s1 + s3),
                    d0 + minus, -(d2 + plus),
                    s0 - s2, s3 - s1,
                    d0 - minus, d2 - plus,
                )
                for i in range(8):
                    yb[i, rows, 0:COLS] = out[i]
                return carry

            lax.fori_loop(0, CR, fold, 0)
            limit = wide(lim_ref[pl.ds(c * CR, CR)])

            def group(g, carry):
                spec = dot3(yb[2 * g], thi[g, 0:PC, :], tlo[g, 0:PC, :])
                spec += dot3(yb[2 * g + 1], thi[g, PC:, :], tlo[g, PC:, :])
                spec = jnp.where(wv_ref[g] <= limit, spec.reshape(CR, SUB, PC), 0.0).reshape(CR * SUB, PC)
                zb[2 * g] = dot3(spec, uhi[g, :, 0:PC], ulo[g, :, 0:PC])
                zb[2 * g + 1] = dot3(spec, uhi[g, :, PC:], ulo[g, :, PC:])
                return carry

            lax.fori_loop(0, 4, group, 0)

            def unfold(r, carry):
                rows = pl.ds(pl.multiple_of(r * SUB, SUB), SUB)
                a0, b0, a1, b1, a2, b2, a3, b3 = [zb[i, rows, :] for i in range(8)]
                even = (a0 + b0 + a2, a0 - b0 - b2, a0 + b0 - a2, a0 - b0 + b2)
                odd = (a1 + a3, half * ((a1 - a3) - (b1 + b3)), b3 - b1, half * ((a3 - a1) - (b1 + b3)))
                for j in range(4):
                    ret[c, j, r] = even[j] + odd[j]
                    ret[c, j + 4, r] = even[j] - odd[j]
                return carry

            lax.fori_loop(0, CR, unfold, 0)

            @pl.when(served_depth >= 2)
            def _():
                lane = lax.broadcasted_iota(jnp.int32, (SUB, 128), 1)

                def select(r, carry):
                    listed = wide(lim_ref[c * CR + r]) >= 0.0
                    for p in range(NP):
                        rawp[p, :, 0:COLS] = recv[c, p, r]
                    for p in range(NP):
                        east = recv[c, (p + 1) % NP, r, :, 0:1]
                        west = recv[c, (p + 7) % NP, r, :, COLS - 1 : COLS]
                        tail = jnp.where(lane == COLS - 256, east, rawp[p, :, 256:PC])
                        tail = jnp.where(lane == 127, west, tail)
                        raw = jnp.concatenate([rawp[p, :, 0:256], tail], axis=-1)
                        ret[c, p, r] = jnp.where(listed, ret[c, p, r], raw)
                    return carry

                lax.fori_loop(0, CR, select, 0)

            def give_back(i, carry):
                p = lax.rem(lon + i, NP)
                dst = state_part(lon, 1 + c * CR, CR)
                local = is_value & (p == lon)

                @pl.when(jnp.logical_not(local))
                def _():
                    pltpu.make_async_remote_copy(
                        src_ref=ret.at[c, p], dst_ref=dst, send_sem=rsend.at[c, p],
                        recv_sem=rrecv.at[c, lon], device_id=(served, p), device_id_type=MESH,
                    ).start()

                @pl.when(local)
                def _():
                    pltpu.make_async_copy(ret.at[c, p], dst, rrecv.at[c, lon]).start()

                return carry

            lax.fori_loop(0, NP, give_back, 0)
            return carry

        lax.fori_loop(first, last, chunk, 0)

        def returned(n, carry):
            c = first + n // NP
            p = lax.rem(n, NP)

            @pl.when(is_off | (p != lon))
            def _():
                pltpu.make_async_copy(ret.at[c, p], ret.at[c, p], rsend.at[c, p]).wait()

            return carry

        lax.fori_loop(0, (last - first) * NP, returned, 0)

    @pl.when(depth >= 3)
    def _():
        lane = lax.broadcasted_iota(jnp.int32, (SUB, 128), 1)
        for g in range(NP):
            slot = g % 2
            if g + 1 < NP:
                stage_copy(g + 1, 1 - slot).start()
            stage_copy(g, slot).wait()

            def gather(j, carry, slot=slot):
                head, tail = carry
                head = jnp.where(lane == j, stage[slot, j, :, 0:1], head)
                tail = jnp.where(lane == j, stage[slot, j, :, COLS - 1 : COLS], tail)
                return head, tail

            zeros = jnp.zeros((SUB, 128), F32)
            head, tail = lax.fori_loop(0, ROWS, gather, (zeros, zeros))
            cols[0, g] = head
            cols[1, g] = tail

        def side_copy(i):
            step = NP - 1 if i == 0 else 1
            return pltpu.make_async_remote_copy(
                src_ref=cols.at[i], dst_ref=side.at[i], send_sem=hsend.at[i], recv_sem=hrecv.at[i],
                device_id=(lat, lax.rem(lon + step, NP)), device_id_type=MESH,
            )

        for i in range(2):
            side_copy(i).start()
        stage_copy(0, 0).start()
        for i in range(2):
            side_copy(i).wait()

        own_start = jnp.where(lat == 3, ROWS // 3, 0)

        def out_copy(g, slot, act):
            full = pltpu.make_async_copy(obuf.at[slot], state_part(g, 1, ROWS), osem.at[slot])
            some = pltpu.make_async_copy(
                obuf.at[slot, pl.ds(own_start, 2 * ROWS // 3)],
                state_part(g, 1 + own_start, 2 * ROWS // 3), osem.at[slot],
            )

            @pl.when(depth > 3)
            def _():
                act(full)

            @pl.when(depth == 3)
            def _():
                act(some)

        for g in range(NP):
            slot = g % 2
            if g + 1 < NP:
                stage_copy(g + 1, 1 - slot).start()
            stage_copy(g, slot).wait()
            if g >= 2:
                out_copy(g, slot, lambda copy: copy.wait())
            obuf[slot, :, :, 0:COLS] = stage[slot]

            def insert(j, carry, g=g, slot=slot):
                east = jnp.sum(jnp.where(lane == j, side[0, g], 0.0), axis=1, keepdims=True)
                west = jnp.sum(jnp.where(lane == j, side[1, g], 0.0), axis=1, keepdims=True)
                tail = obuf[slot, j, :, 256:PC]
                tail = jnp.where(lane == COLS - 256, east, tail)
                obuf[slot, j, :, 256:PC] = jnp.where(lane == 127, west, tail)
                return carry

            lax.fori_loop(0, ROWS, insert, 0)
            out_copy(g, slot, lambda copy: copy.start())
        for slot in range(2):
            out_copy(0, slot, lambda copy: copy.wait())

    @pl.when(is_value)
    def _():
        def drain(n, carry):
            c = begin + n // NP
            p = lax.rem(n, NP)

            @pl.when((c < n_off) | (p != lon))
            def _():
                pltpu.make_async_copy(recv.at[c, p], recv.at[c, p], fsend.at[c, p]).wait()

            dst = state_part(p, 1 + c * CR, CR)
            pltpu.make_async_copy(dst, dst, rrecv.at[c, p]).wait()
            return carry

        lax.fori_loop(0, (end - begin) * NP, drain, 0)

    def edge_copy(i):
        row, there, step = ((1, ROWS + 1, 15), (ROWS, 0, 1))[i]
        return pltpu.make_async_remote_copy(
            src_ref=state_ref.at[:, row], dst_ref=state_ref.at[:, there],
            send_sem=lsend.at[i], recv_sem=lrecv.at[i],
            device_id=(lax.rem(lat + step, 16), lon), device_id_type=MESH,
        )

    def blank(row):
        return pltpu.make_async_copy(zero, state_ref.at[:, row], zsem)

    inner = (lat > 0, lat < 15)
    for i in range(2):
        @pl.when(inner[i])
        def _(i=i):
            edge_copy(i).start()

    for i, row in ((0, 0), (1, ROWS + 1)):
        @pl.when(jnp.logical_not(inner[i]))
        def _(row=row):
            zero[...] = jnp.zeros_like(zero)
            blank(row).start()
            blank(row).wait()

    for i in range(2):
        @pl.when(inner[i])
        def _(i=i):
            edge_copy(i).wait_send()

        @pl.when(inner[1 - i])
        def _(i=i):
            edge_copy(i).wait_recv()


def stencil_kernel(trig_ref, state_ref, wind_out, t_out, h_out):
    base = lax.axis_index("lat") * ROWS + pl.program_id(0) * BLOCK

    def dx(a):
        return pltpu.roll(a, PC - 1, 1) - pltpu.roll(a, 1, 1)

    def one(r, carry):
        at = base + r
        cos_n, cos_s = trig_ref[0, at], trig_ref[0, at + 2]
        inv = trig_ref[1, at + 1]
        turn = 0.3 * trig_ref[2, at + 1]
        u, v, t, h = [state_ref[k, r + 1] for k in range(4)]
        un, vn, tn, hn = [state_ref[k, r] for k in range(4)]
        us, vs, ts, hs = [state_ref[k, r + 2] for k in range(4)]
        cu = (0.025 * inv) * u
        cv = 0.1 * v
        new_h = h - (0.025 * inv) * dx(u * h) - (0.1 * inv) * (vs * hs * cos_s - vn * hn * cos_n)
        new_t = t - cu * dx(t) - cv * (ts - tn)
        new_u = u - cu * dx(u) - cv * (us - un) - (0.05 * inv) * dx(h) + turn * v
        new_v = v - cu * dx(v) - cv * (vs - vn) - 0.15 * (hs - hn) - turn * u
        wind_out[0, r] = new_u[:, 0:COLS]
        wind_out[1, r] = new_v[:, 0:COLS]
        t_out[r] = new_t[:, 0:COLS]
        h_out[r] = new_h[:, 0:COLS]
        return carry

    lax.fori_loop(0, BLOCK, one, 0, unroll=True)


@functools.lru_cache(maxsize=None)
def trig_table():
    row = np.arange(-1, NLAT + 1).astype(np.float32) + np.float32(0.5)
    angle = (row * np.float32(np.pi / NLAT)).astype(np.float64)
    cos = np.sin(angle).astype(np.float32)
    sin = -np.cos(angle).astype(np.float32)
    return np.stack([cos, (1.0 / cos.astype(np.float64)).astype(np.float32), sin])


def body(winds, theta, thick, polar_rows, cutoffs):
    lat = lax.axis_index("lat")
    served = jnp.where((lat >= 4) & (lat < 8), lat - 4, jnp.where((lat >= 8) & (lat < 12), lat + 4, lat))
    rows = served * ROWS + jnp.arange(ROWS, dtype=jnp.int32)
    hits = polar_rows[None, :] == rows[:, None]
    limit = jnp.max(jnp.where(hits, cutoffs[None, :], -1), axis=1).astype(F32)
    lim = jnp.broadcast_to(limit[:, None, None], (ROWS, SUB, 128))
    thi, tlo, uhi, ulo, wv = value_tables()
    fhi, flo, ghi, glo, wp = packed_tables()
    vm = pl.BlockSpec(memory_space=pltpu.VMEM)
    hbm = pl.BlockSpec(memory_space=pl.ANY)
    dma = pltpu.SemaphoreType.DMA
    state = pl.pallas_call(
        filter_kernel,
        out_shape=jax.ShapeDtypeStruct((4, ROWS + 2, LEV, PC), F32),
        in_specs=[hbm, hbm, hbm, vm, vm, vm] + [hbm] * 8,
        out_specs=hbm,
        scratch_shapes=[
            pltpu.VMEM((4, 2 * PC, PC), BF16), pltpu.VMEM((4, 2 * PC, PC), BF16),
            pltpu.VMEM((4, PC, 2 * PC), BF16), pltpu.VMEM((4, PC, 2 * PC), BF16),
            pltpu.VMEM((2, PC, PC), BF16), pltpu.VMEM((2, PC, PC), BF16),
            pltpu.VMEM((2, PC, PC), BF16), pltpu.VMEM((2, PC, PC), BF16),
            pltpu.VMEM((NCH, NP, CR, SUB, COLS), F32),
            pltpu.VMEM((NCH, NP, CR, SUB, PC), F32),
            pltpu.VMEM((NP, HALF, SUB, PC), F32),
            pltpu.VMEM((NP, HALF, SUB, PC), F32),
            pltpu.VMEM((NP, HALF, SUB, PC), F32),
            pltpu.VMEM((2, ROWS, SUB, COLS), F32),
            pltpu.VMEM((2, ROWS, SUB, PC), F32),
            pltpu.VMEM((ROWS * SUB, PC), F32),
            pltpu.VMEM((8, CR * SUB, PC), F32),
            pltpu.VMEM((8, CR * SUB, PC), F32),
            pltpu.VMEM((NP, SUB, PC), F32),
            pltpu.VMEM((2, NP, SUB, 128), F32),
            pltpu.VMEM((2, NP, SUB, 128), F32),
            pltpu.VMEM((4, LEV, PC), F32),
            dma((4,)), dma((2,)),
            dma((NCH, NP)), dma((NCH, NP)), dma((NCH, NP)), dma((NCH, NP)),
            dma((NP,)), dma((NP,)), dma((NP,)), dma((NP,)),
            dma((2,)), dma((2,)), dma((2,)), dma((2,)), dma((2,)), dma,
        ],
        compiler_params=pltpu.CompilerParams(
            collective_id=1, has_side_effects=True, vmem_limit_bytes=58 * 2**20
        ),
        name="polar_filter",
    )(
        winds.transpose(0, 2, 1, 3), theta.transpose(1, 0, 2), thick.transpose(1, 0, 2), lim,
        jnp.asarray(wv)[:, None, :], jnp.asarray(wp), thi, tlo, uhi, ulo, fhi, flo, ghi, glo,
    )
    new_winds, new_t, new_h = pl.pallas_call(
        stencil_kernel,
        grid=(ROWS // BLOCK,),
        out_shape=(
            jax.ShapeDtypeStruct((2, ROWS, LEV, COLS), F32),
            jax.ShapeDtypeStruct((ROWS, LEV, COLS), F32),
            jax.ShapeDtypeStruct((ROWS, LEV, COLS), F32),
        ),
        in_specs=[
            pl.BlockSpec(memory_space=pltpu.SMEM),
            pl.BlockSpec(
                (pl.Element(4), pl.Element(BLOCK + 2), pl.Element(LEV), pl.Element(PC)),
                lambda i: (0, i * BLOCK, 0, 0),
            ),
        ],
        out_specs=(
            pl.BlockSpec((2, BLOCK, LEV, COLS), lambda i: (0, i, 0, 0)),
            pl.BlockSpec((BLOCK, LEV, COLS), lambda i: (i, 0, 0)),
            pl.BlockSpec((BLOCK, LEV, COLS), lambda i: (i, 0, 0)),
        ),
        compiler_params=pltpu.CompilerParams(vmem_limit_bytes=32 * 2**20),
        name="stencil",
    )(jnp.asarray(trig_table()), state)
    return new_winds.transpose(0, 2, 1, 3), new_t.transpose(1, 0, 2), new_h.transpose(1, 0, 2)


def solution(mesh):
    in_specs = (P(None, None, "lat", "lon"), P(None, "lat", "lon"), P(None, "lat", "lon"), P(), P())
    out_specs = (P(None, None, "lat", "lon"), P(None, "lat", "lon"), P(None, "lat", "lon"))
    return jax.shard_map(body, mesh=mesh, in_specs=in_specs, out_specs=out_specs, check_vma=False)
```

```python
import functools

import jax
import jax.numpy as jnp
import numpy as np
from jax import lax
from jax.experimental import pallas as pl
from jax.experimental.pallas import tpu as pltpu
from jax.sharding import PartitionSpec as P

NLON = 2880
NLAT = 1440
LEV = 16
ROWS = 90
COLS = 360
HALF = ROWS // 2
PC = 384
NP = 8
SUB = 8
NCH = 9
CR = ROWS // NCH
OFF1 = 6
OFF2 = 5
MID = 5
BLOCK = 9
MESH = pl.DeviceIdType.MESH
F32 = jnp.float32
BF16 = jnp.bfloat16


def split(table):
    hi = table.astype(np.float32).astype(BF16)
    lo = (table - hi.astype(np.float64)).astype(np.float32).astype(BF16)
    return np.asarray(hi), np.asarray(lo)


@functools.lru_cache(maxsize=None)
def value_tables():
    q = np.arange(PC)
    q = np.where(q == PC - 1, -1, q)
    forward = np.zeros((4, 2 * PC, PC))
    inverse = np.zeros((4, PC, 2 * PC))
    waves = np.full((4, PC), 1e9)
    m = np.arange(90)
    for g in range(4):
        parts = [(0, 0, 0), (4, 1, 0)] if g == 0 else [(g, 0, 1), (8 - g, 0, -1)]
        for slot, (r, half, sign) in enumerate(parts):
            k = 8 * m + r
            angle = 2.0 * np.pi * ((k[:, None] * q[None, :]) % NLON) / NLON
            cos, sin = np.cos(angle), np.sin(angle)
            re = slice(slot * 180, slot * 180 + 90)
            im = slice(slot * 180 + 90, slot * 180 + 180)
            waves[g, re] = k
            waves[g, im] = k
            weight = np.where(k == 0, 1.0, 2.0)[:, None] / NLON
            own = np.zeros((PC, 2 * PC))
            if sign == 0:
                own[re, half * PC : (half + 1) * PC] = cos
                own[im, half * PC : (half + 1) * PC] = -sin
            else:
                own[re, :PC] = cos
                own[im, :PC] = -sin
                own[re, PC:] = sign * sin
                own[im, PC:] = sign * cos
            scaled = own.copy()
            scaled[re] *= weight
            scaled[im] *= weight
            inverse[g] += scaled
            keep = np.concatenate([np.arange(PC) < COLS] * 2)
            forward[g] += (own * keep[None, :]).T
    used = np.concatenate([(np.arange(PC) <= COLS) | (np.arange(PC) == PC - 1)] * 2)
    inverse = inverse * used[None, None, :]
    return split(forward) + split(inverse) + (waves.astype(np.float32),)


@functools.lru_cache(maxsize=None)
def packed_tables():
    lane = np.arange(PC)
    wave = (lane + 1) // 2
    is_cos = (lane == 0) | (lane % 2 == 1)
    q = np.arange(PC)
    q = np.where(q == PC - 1, -1, q)
    used = (np.arange(PC) <= COLS) | (np.arange(PC) == PC - 1)
    forward = np.zeros((NP, 2, PC, PC))
    inverse = np.zeros((NP, 2, PC, PC))
    for p in range(NP):
        n = COLS * p + q
        angle = 2.0 * np.pi * ((wave[:, None] * n[None, :]) % NLON) / NLON
        base = np.where(is_cos[:, None], np.cos(angle), np.sin(angle))
        weight = np.where(wave == 0, 1.0, 2.0)[:, None] / NLON
        back = base * weight * used[None, :]
        ahead = (base * (np.arange(PC) < COLS)[None, :]).T
        forward[p, 0], forward[p, 1] = ahead, ahead[:, ::-1]
        inverse[p, 0], inverse[p, 1] = back, back[::-1]
    waves = np.stack([wave, wave[::-1]]).astype(np.float32)
    return split(forward) + split(inverse) + (waves,)


def dot3(x, hi, lo):
    x_hi = x.astype(BF16)
    x_lo = (x - x_hi.astype(F32)).astype(BF16)
    total = jnp.dot(x_hi, lo, preferred_element_type=F32)
    total += jnp.dot(x_lo, hi, preferred_element_type=F32)
    return total + jnp.dot(x_hi, hi, preferred_element_type=F32)


def wide(lim):
    return jnp.concatenate([lim, lim, lim], axis=-1)


def filter_kernel(
    w_ref, t_ref, h_ref, lim_ref, wv_ref, wp_ref,
    thi_ref, tlo_ref, uhi_ref, ulo_ref, fhi_ref, flo_ref, ghi_ref, glo_ref,
    state_ref,
    thi, tlo, uhi, ulo, fhi, flo, ghi, glo,
    recv, ret, strips, srecv, arecv, stage, obuf, xs, yb, zb, rawp, cols, side, zero, home,
    tab_sem, stage_sem, fsend, frecv, rsend, rrecv, ssend, srecv_sem, asend, arecv_sem,
    hsend, hrecv, lsend, lrecv, osem, zsem, xsend, xrecv,
):
    lat = lax.axis_index("lat")
    lon = lax.axis_index("lon")
    north = lat < 8
    depth = jnp.where(north, lat, 15 - lat)
    partner = jnp.where(north, jnp.where(lat < 4, lat + 4, lat - 4), jnp.where(lat >= 12, lat - 4, lat + 4))
    is_packed = depth == 0
    is_value = (depth >= 1) & (depth <= 3)
    is_off = (depth == 5) | (depth == 6)
    served = jnp.where(is_off, partner, lat)
    served_depth = jnp.where(is_off, depth - 4, depth)
    n_off = jnp.where(served_depth == 1, OFF1, jnp.where(served_depth == 2, OFF2, 0))
    begin = jnp.where(served == 12, 2 * NCH // 3, 0)
    end = jnp.where(served == 3, NCH // 3, NCH)
    first = jnp.where(is_off, 0, jnp.maximum(begin, n_off))
    last = jnp.where(is_off, n_off, end)
    sources = (w_ref.at[0], w_ref.at[1], t_ref, h_ref)

    bar = pltpu.get_barrier_semaphore()
    for i in range(1, NP):
        pl.semaphore_signal(bar, inc=1, device_id=(lat, lax.rem(lon + i, NP)), device_id_type=MESH)
    for i in (1, 15):
        pl.semaphore_signal(bar, inc=1, device_id=(lax.rem(lat + i, 16), lon), device_id_type=MESH)
    n_signals = 9
    if OFF1 or OFF2:
        for i in range(NP):
            pl.semaphore_signal(bar, inc=1, device_id=(partner, lax.rem(lon + i, NP)), device_id_type=MESH)
        n_signals += NP

    tables = ((thi_ref, thi), (tlo_ref, tlo), (uhi_ref, uhi), (ulo_ref, ulo))
    packs = ((fhi_ref, fhi), (flo_ref, flo), (ghi_ref, ghi), (glo_ref, glo))

    @pl.when(is_packed)
    def _():
        for i, (src, dst) in enumerate(packs):
            pltpu.make_async_copy(src.at[lon], dst, tab_sem.at[i]).start()

    def part(g, rows):
        return sources[g // 2].at[rows, 8 * (g % 2) : 8 * (g % 2) + 8]

    def stage_copy(g, slot):
        return pltpu.make_async_copy(part(g, slice(0, ROWS)), stage.at[slot], stage_sem.at[slot])

    def state_part(p, start, count):
        return state_ref.at[p // 2, pl.ds(start, count), pl.ds(pl.multiple_of(lax.rem(p, 2) * 8, 8), 8)]

    @pl.when(depth >= 3)
    def _():
        stage_copy(0, 0).start()

    pl.semaphore_wait(bar, n_signals)

    def relay(c, k):
        return pltpu.make_async_remote_copy(
            src_ref=sources[k].at[pl.ds(c * CR, CR)], dst_ref=home.at[c, k],
            send_sem=xsend.at[c, k], recv_sem=xrecv.at[c, k],
            device_id=(partner, lon), device_id_type=MESH,
        )

    def relay_all(c, act):
        for k in range(4):
            act(relay(c, k))

    def relay_next(c, carry):
        relay_all(c - 2, lambda copy: copy.wait_send())
        relay_all(c, lambda copy: copy.start())
        return carry

    def relay_only(c, carry):
        relay_all(c, lambda copy: copy.start())
        return carry

    @pl.when(is_value)
    def _():
        lax.fori_loop(0, jnp.minimum(n_off, 2), relay_only, 0)

        def per_copy(n, carry):
            c = first + n // NP
            p = lax.rem(lon + n, NP)
            dst = recv.at[c, lon]
            for g in range(NP):
                src = part(g, pl.ds(c * CR, CR))

                @pl.when((p == g) & (p != lon))
                def _(src=src):
                    pltpu.make_async_remote_copy(
                        src_ref=src, dst_ref=dst, send_sem=fsend.at[c, p],
                        recv_sem=frecv.at[c, lon], device_id=(lat, p), device_id_type=MESH,
                    ).start()

                @pl.when((p == g) & (p == lon))
                def _(src=src):
                    pltpu.make_async_copy(src, dst, frecv.at[c, lon]).start()

            return carry

        lax.fori_loop(0, (last - first) * NP, per_copy, 0)

    @pl.when(is_value | is_off)
    def _():
        for i, (src, dst) in enumerate(tables):
            pltpu.make_async_copy(src, dst, tab_sem.at[i]).start()
        yb[...] = jnp.zeros_like(yb)

    def strip_copy(p):
        return pltpu.make_async_remote_copy(
            src_ref=strips.at[p], dst_ref=srecv.at[lon], send_sem=ssend.at[p],
            recv_sem=srecv_sem.at[lon], device_id=(lat, p), device_id_type=MESH,
        )

    @pl.when(is_packed)
    def _():
        xs[...] = jnp.zeros_like(xs)
        for i, (src, dst) in enumerate(packs):
            pltpu.make_async_copy(src.at[lon], dst, tab_sem.at[i]).wait()

        def load_part(g, slot):
            half = pl.ds(pl.multiple_of(lax.rem(g, 2) * 8, 8), 8)
            for k in range(4):
                @pl.when(g // 2 == k)
                def _(k=k):
                    pltpu.make_async_copy(sources[k].at[:, half], stage.at[slot], stage_sem.at[slot]).start()

        load_part(lax.rem(lon + 1, NP), 0)

        def ahead(i, carry):
            g = lax.rem(lon + 1 + i, NP)
            slot = lax.rem(i, 2)

            @pl.when(i + 1 < NP)
            def _():
                load_part(lax.rem(g + 1, NP), 1 - slot)

            pltpu.make_async_copy(stage.at[slot], stage.at[slot], stage_sem.at[slot]).wait()
            xs[:, 0:COLS] = stage[slot].reshape(ROWS * SUB, COLS)
            low = dot3(xs[0 : HALF * SUB, :], fhi[0], flo[0]).reshape(HALF, SUB, PC)
            strips[g] = jnp.where(wp_ref[0:1, :] <= wide(lim_ref[0:HALF]), low, 0.0)
            high = dot3(xs[HALF * SUB :, :], fhi[1], flo[1]).reshape(HALF, SUB, PC)
            obuf[slot, 0:HALF] = jnp.where(wp_ref[1:2, :] <= wide(lim_ref[HALF:]), high, 0.0)

            def pair(j, carry):
                strips[g, j] += obuf[slot, HALF - 1 - j]
                return carry

            lax.fori_loop(0, HALF, pair, 0, unroll=9)

            @pl.when(lon != g)
            def _():
                strip_copy(g).start()

            @pl.when(lon == g)
            def _():
                pltpu.make_async_copy(strips.at[g], srecv.at[g], srecv_sem.at[g]).start()

            return carry

        lax.fori_loop(0, NP, ahead, 0)

        def wait_part(s, carry):
            pltpu.make_async_copy(srecv.at[s], srecv.at[s], srecv_sem.at[s]).wait()
            return carry

        lax.fori_loop(0, NP, wait_part, 0)

        def add(i, carry):
            total = srecv[0, i]
            for s in range(1, NP):
                total = total + srecv[s, i]
            arecv[lon, i] = total
            return carry

        lax.fori_loop(0, HALF, add, 0, unroll=5)

        def sum_to(p):
            return pltpu.make_async_remote_copy(
                src_ref=arecv.at[lon], dst_ref=arecv.at[lon], send_sem=asend.at[p],
                recv_sem=arecv_sem.at[lon], device_id=(lat, p), device_id_type=MESH,
            )

        def send(i, carry):
            sum_to(lax.rem(lon + i, NP)).start()
            return carry

        lax.fori_loop(1, NP, send, 0)

        def out_copy(p, slot):
            return pltpu.make_async_copy(obuf.at[slot], state_part(p, 1, ROWS), osem.at[slot])

        def back(i, carry):
            g = lax.rem(lon + i, NP)
            slot = lax.rem(i, 2)

            @pl.when(i > 0)
            def _():
                pltpu.make_async_copy(arecv.at[g], arecv.at[g], arecv_sem.at[g]).wait()

            @pl.when(i >= 2)
            def _():
                out_copy(g, slot).wait()

            spec = arecv[g]
            low = jnp.where(wp_ref[0:1, :] <= wide(lim_ref[0:HALF]), spec, 0.0).reshape(HALF * SUB, PC)
            obuf[slot, 0:HALF] = dot3(low, ghi[0], glo[0]).reshape(HALF, SUB, PC)

            def flip(j, carry):
                xs[pl.ds(pl.multiple_of(j * SUB, SUB), SUB), :] = arecv[g, HALF - 1 - j]
                return carry

            lax.fori_loop(0, HALF, flip, 0, unroll=9)
            high = xs[0 : HALF * SUB, :].reshape(HALF, SUB, PC)
            high = jnp.where(wp_ref[1:2, :] <= wide(lim_ref[HALF:]), high, 0.0).reshape(HALF * SUB, PC)
            obuf[slot, HALF:ROWS] = dot3(high, ghi[1], glo[1]).reshape(HALF, SUB, PC)
            out_copy(g, slot).start()
            return carry

        lax.fori_loop(0, NP, back, 0)
        for slot in range(2):
            out_copy(0, slot).wait()

        def sent(i, carry):
            p = lax.rem(lon + i, NP)
            sum_to(p).wait_send()
            strip_copy(p).wait_send()
            return carry

        lax.fori_loop(1, NP, sent, 0)

    @pl.when(depth >= 3)
    def _():
        lane = lax.broadcasted_iota(jnp.int32, (SUB, 128), 1)
        for g in range(NP):
            slot = g % 2
            if g + 1 < NP:
                stage_copy(g + 1, 1 - slot).start()
            stage_copy(g, slot).wait()

            def gather(j, carry, slot=slot):
                head, tail = carry
                head = jnp.where(lane == j, stage[slot, j, :, 0:1], head)
                tail = jnp.where(lane == j, stage[slot, j, :, COLS - 1 : COLS], tail)
                return head, tail

            zeros = jnp.zeros((SUB, 128), F32)
            head, tail = lax.fori_loop(0, ROWS, gather, (zeros, zeros), unroll=18)
            cols[0, g] = head
            cols[1, g] = tail

        def side_copy(i):
            step = NP - 1 if i == 0 else 1
            return pltpu.make_async_remote_copy(
                src_ref=cols.at[i], dst_ref=side.at[i], send_sem=hsend.at[i], recv_sem=hrecv.at[i],
                device_id=(lat, lax.rem(lon + step, NP)), device_id_type=MESH,
            )

        for i in range(2):
            side_copy(i).start()
        stage_copy(0, 0).start()
        for i in range(2):
            side_copy(i).wait()

        own_start = jnp.where(lat == 3, ROWS // 3, 0)

        def out_copy(g, slot, act):
            full = pltpu.make_async_copy(obuf.at[slot], state_part(g, 1, ROWS), osem.at[slot])
            some = pltpu.make_async_copy(
                obuf.at[slot, pl.ds(own_start, 2 * ROWS // 3)],
                state_part(g, 1 + own_start, 2 * ROWS // 3), osem.at[slot],
            )

            @pl.when(depth > 3)
            def _():
                act(full)

            @pl.when(depth == 3)
            def _():
                act(some)

        for g in range(NP):
            slot = g % 2
            if g + 1 < NP:
                stage_copy(g + 1, 1 - slot).start()
            stage_copy(g, slot).wait()
            if g >= 2:
                out_copy(g, slot, lambda copy: copy.wait())

            def insert(j, carry, g=g, slot=slot):
                obuf[slot, j, :, 0:COLS] = stage[slot, j]
                east = pltpu.roll(side[0, g], lax.rem(COLS - 256 + 128 - j, 128), 1)
                west = pltpu.roll(side[1, g], 127 - j, 1)
                tail = obuf[slot, j, :, 256:PC]
                tail = jnp.where(lane == COLS - 256, east, tail)
                obuf[slot, j, :, 256:PC] = jnp.where(lane == 127, west, tail)
                return carry

            lax.fori_loop(0, ROWS, insert, 0, unroll=9)
            out_copy(g, slot, lambda copy: copy.start())
        for slot in range(2):
            out_copy(0, slot, lambda copy: copy.wait())

    @pl.when(is_value | is_off)
    def _():
        for i, (src, dst) in enumerate(tables):
            pltpu.make_async_copy(src, dst, tab_sem.at[i]).wait()

        half = np.float32(np.sqrt(0.5))

        def chunk(c, carry):
            def arrived(s, carry):
                pltpu.make_async_copy(recv.at[c, s], recv.at[c, s], frecv.at[c, s]).wait()
                return carry

            lax.fori_loop(0, NP, arrived, 0)

            def fold(r, carry):
                rows = pl.ds(pl.multiple_of(r * SUB, SUB), SUB)
                x = [recv[c, s, r] for s in range(NP)]
                s0, s1, s2, s3 = [x[j] + x[j + 4] for j in range(4)]
                d0, d1, d2, d3 = [x[j] - x[j + 4] for j in range(4)]
                plus, minus = half * (d1 + d3), half * (d1 - d3)
                out = (
                    (s0 + s2) + (s1 + s3), (s0 + s2) - (s1 + s3),
                    d0 + minus, -(d2 + plus),
                    s0 - s2, s3 - s1,
                    d0 - minus, d2 - plus,
                )
                for i in range(8):
                    yb[i, rows, 0:COLS] = out[i]
                return carry

            lax.fori_loop(0, CR, fold, 0)
            limit = wide(lim_ref[pl.ds(c * CR, CR)])

            def group(g, carry):
                spec = dot3(yb[2 * g], thi[g, 0:PC, :], tlo[g, 0:PC, :])
                spec += dot3(yb[2 * g + 1], thi[g, PC:, :], tlo[g, PC:, :])
                spec = jnp.where(wv_ref[g] <= limit, spec.reshape(CR, SUB, PC), 0.0).reshape(CR * SUB, PC)
                zb[2 * g] = dot3(spec, uhi[g, :, 0:PC], ulo[g, :, 0:PC])
                zb[2 * g + 1] = dot3(spec, uhi[g, :, PC:], ulo[g, :, PC:])
                return carry

            lax.fori_loop(0, 4, group, 0)

            def unfold(r, carry):
                rows = pl.ds(pl.multiple_of(r * SUB, SUB), SUB)
                a0, b0, a1, b1, a2, b2, a3, b3 = [zb[i, rows, :] for i in range(8)]
                even = (a0 + b0 + a2, a0 - b0 - b2, a0 + b0 - a2, a0 - b0 + b2)
                odd = (a1 + a3, half * ((a1 - a3) - (b1 + b3)), b3 - b1, half * ((a3 - a1) - (b1 + b3)))
                for j in range(4):
                    ret[c, j, r] = even[j] + odd[j]
                    ret[c, j + 4, r] = even[j] - odd[j]
                return carry

            lax.fori_loop(0, CR, unfold, 0)

            @pl.when(served_depth >= 2)
            def _():
                lane = lax.broadcasted_iota(jnp.int32, (SUB, 128), 1)

                def select(r, carry):
                    listed = wide(lim_ref[c * CR + r]) >= 0.0
                    for p in range(NP):
                        rawp[p, :, 0:COLS] = recv[c, p, r]
                    for p in range(NP):
                        east = recv[c, (p + 1) % NP, r, :, 0:1]
                        west = recv[c, (p + 7) % NP, r, :, COLS - 1 : COLS]
                        tail = jnp.where(lane == COLS - 256, east, rawp[p, :, 256:PC])
                        tail = jnp.where(lane == 127, west, tail)
                        raw = jnp.concatenate([rawp[p, :, 0:256], tail], axis=-1)
                        ret[c, p, r] = jnp.where(listed, ret[c, p, r], raw)
                    return carry

                lax.fori_loop(0, CR, select, 0)

            def give_back(i, carry):
                p = lax.rem(lon + i, NP)
                dst = state_part(lon, 1 + c * CR, CR)
                local = is_value & (p == lon)

                @pl.when(jnp.logical_not(local))
                def _():
                    pltpu.make_async_remote_copy(
                        src_ref=ret.at[c, p], dst_ref=dst, send_sem=rsend.at[c, p],
                        recv_sem=rrecv.at[c, lon], device_id=(served, p), device_id_type=MESH,
                    ).start()

                @pl.when(local)
                def _():
                    pltpu.make_async_copy(ret.at[c, p], dst, rrecv.at[c, lon]).start()

                return carry

            lax.fori_loop(0, NP, give_back, 0)
            return carry

        def pass_on(c):
            relay_all(c, lambda copy: copy.wait_recv())
            dst = recv.at[c, lon]

            def home_part(p):
                return home.at[c, p // 2, :, pl.ds(pl.multiple_of(lax.rem(p, 2) * 8, 8), 8)]

            def to_owner(i, carry):
                p = lax.rem(lon + i, NP)
                pltpu.make_async_remote_copy(
                    src_ref=home_part(p), dst_ref=dst, send_sem=fsend.at[c, p],
                    recv_sem=frecv.at[c, lon], device_id=(lat, p), device_id_type=MESH,
                ).start()
                return carry

            lax.fori_loop(1, NP, to_owner, 0)
            pltpu.make_async_copy(home_part(lon), dst, frecv.at[c, lon]).start()

        def step(n, carry):
            @pl.when(is_off & (n < last))
            def _():
                pass_on(n)

            @pl.when(n > first)
            def _():
                chunk(n - 1, 0)

            return carry

        @pl.when(is_value)
        def _():
            lax.fori_loop(2, jnp.minimum(n_off, MID), relay_next, 0)

        lax.fori_loop(first, last + 1, step, 0)

        @pl.when(is_value)
        def _():
            lax.fori_loop(MID, n_off, relay_next, 0)

        def returned(n, carry):
            c = first + n // NP
            p = lax.rem(n, NP)

            @pl.when(is_off | (p != lon))
            def _():
                pltpu.make_async_copy(ret.at[c, p], ret.at[c, p], rsend.at[c, p]).wait()

            @pl.when(p != lon)
            def _():
                pltpu.make_async_copy(recv.at[c, p], recv.at[c, p], fsend.at[c, p]).wait()

            return carry

        lax.fori_loop(0, (last - first) * NP, returned, 0)

    @pl.when(is_value)
    def _():
        def drain(n, carry):
            c = begin + n // NP
            p = lax.rem(n, NP)

            dst = state_part(p, 1 + c * CR, CR)
            pltpu.make_async_copy(dst, dst, rrecv.at[c, p]).wait()
            return carry

        lax.fori_loop(0, (end - begin) * NP, drain, 0)

        def relayed(c, carry):
            relay_all(c, lambda copy: copy.wait_send())
            return carry

        lax.fori_loop(jnp.maximum(n_off - 2, 0), n_off, relayed, 0)

    def edge_copy(i):
        row, there, step = ((1, ROWS + 1, 15), (ROWS, 0, 1))[i]
        return pltpu.make_async_remote_copy(
            src_ref=state_ref.at[:, row], dst_ref=state_ref.at[:, there],
            send_sem=lsend.at[i], recv_sem=lrecv.at[i],
            device_id=(lax.rem(lat + step, 16), lon), device_id_type=MESH,
        )

    def blank(row):
        return pltpu.make_async_copy(zero, state_ref.at[:, row], zsem)

    inner = (lat > 0, lat < 15)
    for i in range(2):
        @pl.when(inner[i])
        def _(i=i):
            edge_copy(i).start()

    for i, row in ((0, 0), (1, ROWS + 1)):
        @pl.when(jnp.logical_not(inner[i]))
        def _(row=row):
            zero[...] = jnp.zeros_like(zero)
            blank(row).start()
            blank(row).wait()

    for i in range(2):
        @pl.when(inner[i])
        def _(i=i):
            edge_copy(i).wait_send()

        @pl.when(inner[1 - i])
        def _(i=i):
            edge_copy(i).wait_recv()


def stencil_kernel(trig_ref, state_ref, wind_out, t_out, h_out):
    base = lax.axis_index("lat") * ROWS + pl.program_id(0) * BLOCK

    def dx(a):
        return pltpu.roll(a, PC - 1, 1) - pltpu.roll(a, 1, 1)

    def one(r, carry):
        at = base + r
        cos_n, cos_s = trig_ref[0, at], trig_ref[0, at + 2]
        inv = trig_ref[1, at + 1]
        turn = 0.3 * trig_ref[2, at + 1]
        u, v, t, h = [state_ref[k, r + 1] for k in range(4)]
        un, vn, tn, hn = [state_ref[k, r] for k in range(4)]
        us, vs, ts, hs = [state_ref[k, r + 2] for k in range(4)]
        cu = (0.025 * inv) * u
        cv = 0.1 * v
        new_h = h - (0.025 * inv) * dx(u * h) - (0.1 * inv) * (vs * hs * cos_s - vn * hn * cos_n)
        new_t = t - cu * dx(t) - cv * (ts - tn)
        new_u = u - cu * dx(u) - cv * (us - un) - (0.05 * inv) * dx(h) + turn * v
        new_v = v - cu * dx(v) - cv * (vs - vn) - 0.15 * (hs - hn) - turn * u
        wind_out[0, r] = new_u[:, 0:COLS]
        wind_out[1, r] = new_v[:, 0:COLS]
        t_out[r] = new_t[:, 0:COLS]
        h_out[r] = new_h[:, 0:COLS]
        return carry

    lax.fori_loop(0, BLOCK, one, 0, unroll=True)


@functools.lru_cache(maxsize=None)
def trig_table():
    row = np.arange(-1, NLAT + 1).astype(np.float32) + np.float32(0.5)
    angle = (row * np.float32(np.pi / NLAT)).astype(np.float64)
    cos = np.sin(angle).astype(np.float32)
    sin = -np.cos(angle).astype(np.float32)
    return np.stack([cos, (1.0 / cos.astype(np.float64)).astype(np.float32), sin])


def body(winds, theta, thick, polar_rows, cutoffs):
    lat = lax.axis_index("lat")
    served = jnp.where((lat >= 4) & (lat < 8), lat - 4, jnp.where((lat >= 8) & (lat < 12), lat + 4, lat))
    rows = served * ROWS + jnp.arange(ROWS, dtype=jnp.int32)
    hits = polar_rows[None, :] == rows[:, None]
    limit = jnp.max(jnp.where(hits, cutoffs[None, :], -1), axis=1).astype(F32)
    lim = jnp.broadcast_to(limit[:, None, None], (ROWS, SUB, 128))
    thi, tlo, uhi, ulo, wv = value_tables()
    fhi, flo, ghi, glo, wp = packed_tables()
    vm = pl.BlockSpec(memory_space=pltpu.VMEM)
    hbm = pl.BlockSpec(memory_space=pl.ANY)
    dma = pltpu.SemaphoreType.DMA
    state = pl.pallas_call(
        filter_kernel,
        out_shape=jax.ShapeDtypeStruct((4, ROWS + 2, LEV, PC), F32),
        in_specs=[hbm, hbm, hbm, vm, vm, vm] + [hbm] * 8,
        out_specs=hbm,
        scratch_shapes=[
            pltpu.VMEM((4, 2 * PC, PC), BF16), pltpu.VMEM((4, 2 * PC, PC), BF16),
            pltpu.VMEM((4, PC, 2 * PC), BF16), pltpu.VMEM((4, PC, 2 * PC), BF16),
            pltpu.VMEM((2, PC, PC), BF16), pltpu.VMEM((2, PC, PC), BF16),
            pltpu.VMEM((2, PC, PC), BF16), pltpu.VMEM((2, PC, PC), BF16),
            pltpu.VMEM((NCH, NP, CR, SUB, COLS), F32),
            pltpu.VMEM((NCH, NP, CR, SUB, PC), F32),
            pltpu.VMEM((NP, HALF, SUB, PC), F32),
            pltpu.VMEM((NP, HALF, SUB, PC), F32),
            pltpu.VMEM((NP, HALF, SUB, PC), F32),
            pltpu.VMEM((2, ROWS, SUB, COLS), F32),
            pltpu.VMEM((2, ROWS, SUB, PC), F32),
            pltpu.VMEM((ROWS * SUB, PC), F32),
            pltpu.VMEM((8, CR * SUB, PC), F32),
            pltpu.VMEM((8, CR * SUB, PC), F32),
            pltpu.VMEM((NP, SUB, PC), F32),
            pltpu.VMEM((2, NP, SUB, 128), F32),
            pltpu.VMEM((2, NP, SUB, 128), F32),
            pltpu.VMEM((4, LEV, PC), F32),
            pltpu.VMEM((max(OFF1, OFF2), 4, CR, LEV, COLS), F32),
            dma((4,)), dma((2,)),
            dma((NCH, NP)), dma((NCH, NP)), dma((NCH, NP)), dma((NCH, NP)),
            dma((NP,)), dma((NP,)), dma((NP,)), dma((NP,)),
            dma((2,)), dma((2,)), dma((2,)), dma((2,)), dma((2,)), dma,
            dma((NCH, 4)), dma((NCH, 4)),
        ],
        compiler_params=pltpu.CompilerParams(
            collective_id=1, has_side_effects=True, vmem_limit_bytes=60 * 2**20
        ),
        name="polar_filter",
    )(
        winds.transpose(0, 2, 1, 3), theta.transpose(1, 0, 2), thick.transpose(1, 0, 2), lim,
        jnp.asarray(wv)[:, None, :], jnp.asarray(wp), thi, tlo, uhi, ulo, fhi, flo, ghi, glo,
    )
    new_winds, new_t, new_h = pl.pallas_call(
        stencil_kernel,
        grid=(ROWS // BLOCK,),
        out_shape=(
            jax.ShapeDtypeStruct((2, ROWS, LEV, COLS), F32),
            jax.ShapeDtypeStruct((ROWS, LEV, COLS), F32),
            jax.ShapeDtypeStruct((ROWS, LEV, COLS), F32),
        ),
        in_specs=[
            pl.BlockSpec(memory_space=pltpu.SMEM),
            pl.BlockSpec(
                (pl.Element(4), pl.Element(BLOCK + 2), pl.Element(LEV), pl.Element(PC)),
                lambda i: (0, i * BLOCK, 0, 0),
            ),
        ],
        out_specs=(
            pl.BlockSpec((2, BLOCK, LEV, COLS), lambda i: (0, i, 0, 0)),
            pl.BlockSpec((BLOCK, LEV, COLS), lambda i: (i, 0, 0)),
            pl.BlockSpec((BLOCK, LEV, COLS), lambda i: (i, 0, 0)),
        ),
        compiler_params=pltpu.CompilerParams(vmem_limit_bytes=32 * 2**20),
        name="stencil",
    )(jnp.asarray(trig_table()), state)
    return new_winds.transpose(0, 2, 1, 3), new_t.transpose(1, 0, 2), new_h.transpose(1, 0, 2)


def solution(mesh):
    in_specs = (P(None, None, "lat", "lon"), P(None, "lat", "lon"), P(None, "lat", "lon"), P(), P())
    out_specs = (P(None, None, "lat", "lon"), P(None, "lat", "lon"), P(None, "lat", "lon"))
    return jax.shard_map(body, mesh=mesh, in_specs=in_specs, out_specs=out_specs, check_vma=False)
```

```python
import functools

import jax
import jax.numpy as jnp
import numpy as np
from jax import lax
from jax.experimental import pallas as pl
from jax.experimental.pallas import tpu as pltpu
from jax.sharding import PartitionSpec as P

NLON = 2880
NLAT = 1440
LEV = 16
ROWS = 90
COLS = 360
HALF = ROWS // 2
PC = 384
NP = 8
SUB = 8
NCH = 9
CR = ROWS // NCH
OFF1 = 5
OFF2 = 4
NSUB = 3
SR = HALF // NSUB
NG = 4
BLOCK = 9
MESH = pl.DeviceIdType.MESH
F32 = jnp.float32
BF16 = jnp.bfloat16


def split(table):
    hi = table.astype(np.float32).astype(BF16)
    lo = (table - hi.astype(np.float64)).astype(np.float32).astype(BF16)
    return np.asarray(hi), np.asarray(lo)


@functools.lru_cache(maxsize=None)
def value_tables():
    q = np.arange(PC)
    q = np.where(q == PC - 1, -1, q)
    forward = np.zeros((4, 2 * PC, PC))
    inverse = np.zeros((4, PC, 2 * PC))
    waves = np.full((4, PC), 1e9)
    m = np.arange(90)
    for g in range(4):
        parts = [(0, 0, 0), (4, 1, 0)] if g == 0 else [(g, 0, 1), (8 - g, 0, -1)]
        for slot, (r, half, sign) in enumerate(parts):
            k = 8 * m + r
            angle = 2.0 * np.pi * ((k[:, None] * q[None, :]) % NLON) / NLON
            cos, sin = np.cos(angle), np.sin(angle)
            re = slice(slot * 180, slot * 180 + 90)
            im = slice(slot * 180 + 90, slot * 180 + 180)
            waves[g, re] = k
            waves[g, im] = k
            weight = np.where(k == 0, 1.0, 2.0)[:, None] / NLON
            own = np.zeros((PC, 2 * PC))
            if sign == 0:
                own[re, half * PC : (half + 1) * PC] = cos
                own[im, half * PC : (half + 1) * PC] = -sin
            else:
                own[re, :PC] = cos
                own[im, :PC] = -sin
                own[re, PC:] = sign * sin
                own[im, PC:] = sign * cos
            scaled = own.copy()
            scaled[re] *= weight
            scaled[im] *= weight
            inverse[g] += scaled
            keep = np.concatenate([np.arange(PC) < COLS] * 2)
            forward[g] += (own * keep[None, :]).T
    used = np.concatenate([(np.arange(PC) <= COLS) | (np.arange(PC) == PC - 1)] * 2)
    inverse = inverse * used[None, None, :]
    return split(forward) + split(inverse) + (waves.astype(np.float32),)


@functools.lru_cache(maxsize=None)
def packed_tables():
    lane = np.arange(PC)
    wave = (lane + 1) // 2
    is_cos = (lane == 0) | (lane % 2 == 1)
    q = np.arange(PC)
    q = np.where(q == PC - 1, -1, q)
    used = (np.arange(PC) <= COLS) | (np.arange(PC) == PC - 1)
    forward = np.zeros((NP, 2, PC, PC))
    inverse = np.zeros((NP, 2, PC, PC))
    for p in range(NP):
        n = COLS * p + q
        angle = 2.0 * np.pi * ((wave[:, None] * n[None, :]) % NLON) / NLON
        base = np.where(is_cos[:, None], np.cos(angle), np.sin(angle))
        weight = np.where(wave == 0, 1.0, 2.0)[:, None] / NLON
        back = base * weight * used[None, :]
        ahead = (base * (np.arange(PC) < COLS)[None, :]).T
        forward[p, 0], forward[p, 1] = ahead, ahead[:, ::-1]
        inverse[p, 0], inverse[p, 1] = back, back[::-1]
    waves = np.stack([wave, wave[::-1]]).astype(np.float32)
    return split(forward) + split(inverse) + (waves,)


def dot3(x, hi, lo):
    x_hi = x.astype(BF16)
    x_lo = (x - x_hi.astype(F32)).astype(BF16)
    total = jnp.dot(x_hi, lo, preferred_element_type=F32)
    total += jnp.dot(x_lo, hi, preferred_element_type=F32)
    return total + jnp.dot(x_hi, hi, preferred_element_type=F32)


def wide(lim):
    return jnp.concatenate([lim, lim, lim], axis=-1)


def filter_kernel(
    w_ref, t_ref, h_ref, lim_ref, wv_ref, wp_ref,
    thi_ref, tlo_ref, uhi_ref, ulo_ref, fhi_ref, flo_ref, ghi_ref, glo_ref,
    state_ref,
    thi, tlo, uhi, ulo, fhi, flo, ghi, glo,
    recv, ret, srecv, stage, obuf, pbuf, xs, yb, zb, rawp, cols, side, zero, home,
    tab_sem, stage_sem, fsend, frecv, rsend, rrecv, ssend, srecv_sem, asend, arecv_sem,
    hsend, hrecv, lsend, lrecv, osem, zsem, xsend, xrecv, part_sem, psem,
):
    lat = lax.axis_index("lat")
    lon = lax.axis_index("lon")
    north = lat < 8
    depth = jnp.where(north, lat, 15 - lat)
    partner = jnp.where(north, jnp.where(lat < 4, lat + 4, lat - 4), jnp.where(lat >= 12, lat - 4, lat + 4))
    is_packed = depth == 0
    is_value = (depth >= 1) & (depth <= 3)
    is_off = (depth == 5) | (depth == 6)
    served = jnp.where(is_off, partner, lat)
    served_depth = jnp.where(is_off, depth - 4, depth)
    n_off = jnp.where(served_depth == 1, OFF1, jnp.where(served_depth == 2, OFF2, 0))
    begin = jnp.where(served == 12, 2 * NCH // 3, 0)
    end = jnp.where(served == 3, NCH // 3, NCH)
    first = jnp.where(is_off, 0, jnp.maximum(begin, n_off))
    last = jnp.where(is_off, n_off, end)
    sources = (w_ref.at[0], w_ref.at[1], t_ref, h_ref)

    bar = pltpu.get_barrier_semaphore()
    for i in range(1, NP):
        pl.semaphore_signal(bar, inc=1, device_id=(lat, lax.rem(lon + i, NP)), device_id_type=MESH)
    for i in (1, 15):
        pl.semaphore_signal(bar, inc=1, device_id=(lax.rem(lat + i, 16), lon), device_id_type=MESH)
    n_signals = 9
    if OFF1 or OFF2:
        for i in range(NP):
            pl.semaphore_signal(bar, inc=1, device_id=(partner, lax.rem(lon + i, NP)), device_id_type=MESH)
        n_signals += NP

    tables = ((thi_ref, thi), (tlo_ref, tlo), (uhi_ref, uhi), (ulo_ref, ulo))
    packs = ((fhi_ref, fhi), (flo_ref, flo), (ghi_ref, ghi), (glo_ref, glo))

    @pl.when(is_packed)
    def _():
        for i, (src, dst) in enumerate(packs):
            pltpu.make_async_copy(src.at[lon], dst, tab_sem.at[i]).start()

    @pl.when(is_value | is_off)
    def _():
        for i, (src, dst) in enumerate(tables):
            pltpu.make_async_copy(src, dst, tab_sem.at[i]).start()
        yb[...] = jnp.zeros_like(yb)

    def part(g, rows):
        return sources[g // 2].at[rows, 8 * (g % 2) : 8 * (g % 2) + 8]

    def whole_part(g):
        return pltpu.make_async_copy(part(g, slice(0, ROWS)), recv.at[g], part_sem.at[g])

    @pl.when(is_packed)
    def _():
        for g in range(NP):
            whole_part(g).start()

    def stage_copy(g, slot):
        return pltpu.make_async_copy(part(g, slice(0, ROWS)), stage.at[slot], stage_sem.at[slot])

    def state_part(p, start, count):
        return state_ref.at[p // 2, pl.ds(start, count), pl.ds(pl.multiple_of(lax.rem(p, 2) * 8, 8), 8)]

    @pl.when(depth >= 3)
    def _():
        stage_copy(0, 0).start()

    pl.semaphore_wait(bar, n_signals)

    def relay(c, k):
        return pltpu.make_async_remote_copy(
            src_ref=sources[k].at[pl.ds(c * CR, CR)], dst_ref=home.at[c, k],
            send_sem=xsend.at[c, k], recv_sem=xrecv.at[c, k],
            device_id=(partner, lon), device_id_type=MESH,
        )

    def relay_all(c, act):
        for k in range(4):
            act(relay(c, k))

    def stay(c):
        def per_owner(i, carry):
            p = lax.rem(lon + i, NP)
            dst = recv.at[lon, pl.ds(c * CR, CR)]
            half = pl.ds(pl.multiple_of(lax.rem(p, 2) * 8, 8), 8)
            for k in range(4):
                src = sources[k].at[pl.ds(c * CR, CR), half]

                @pl.when((p // 2 == k) & (p != lon))
                def _(src=src):
                    pltpu.make_async_remote_copy(
                        src_ref=src, dst_ref=dst, send_sem=fsend.at[c, p],
                        recv_sem=frecv.at[c, lon], device_id=(lat, p), device_id_type=MESH,
                    ).start()

                @pl.when((p // 2 == k) & (p == lon))
                def _(src=src):
                    pltpu.make_async_copy(src, dst, frecv.at[c, lon]).start()

            return carry

        lax.fori_loop(0, NP, per_owner, 0)

    def strip_copy(p, sub):
        rows = pl.ds(sub * SR, SR)
        return pltpu.make_async_remote_copy(
            src_ref=ret.at[p, rows], dst_ref=srecv.at[lon, rows], send_sem=ssend.at[sub, p],
            recv_sem=srecv_sem.at[sub, lon], device_id=(lat, p), device_id_type=MESH,
        )

    @pl.when(is_packed)
    def _():
        xs[...] = jnp.zeros_like(xs)
        for i, (src, dst) in enumerate(packs):
            pltpu.make_async_copy(src.at[lon], dst, tab_sem.at[i]).wait()
        for g in range(NP):
            whole_part(g).wait()

        def keep(sub):
            near = wp_ref[0:1, :] <= wide(lim_ref[pl.ds(sub * SR, SR)])
            far = wp_ref[1:2, :] <= wide(lim_ref[pl.ds(ROWS - SR - sub * SR, SR)])
            return near[None], far[None]

        def ahead(n, carry):
            sub = n // (NP // NG)
            base = lon + 1 + lax.rem(n, NP // NG) * NG
            for i in range(NG):
                g = lax.rem(base + i, NP)
                near = recv[g, pl.ds(sub * SR, SR)].reshape(SR * SUB, COLS)
                far = recv[g, pl.ds(ROWS - SR - sub * SR, SR)].reshape(SR * SUB, COLS)
                xs[0, i * SR * SUB : (i + 1) * SR * SUB, 0:COLS] = near
                xs[1, i * SR * SUB : (i + 1) * SR * SUB, 0:COLS] = far
            keep_near, keep_far = keep(sub)
            shape = (NG, SR, SUB, PC)
            pbuf[0, :, 0] = jnp.where(keep_near, dot3(xs[0], fhi[0], flo[0]).reshape(shape), 0.0)
            pbuf[0, :, 1] = jnp.where(keep_far, dot3(xs[1], fhi[1], flo[1]).reshape(shape), 0.0)
            for i in range(NG):
                g = lax.rem(base + i, NP)
                for j in range(SR):
                    ret[g, sub * SR + j] = pbuf[0, i, 0, j] + pbuf[0, i, 1, SR - 1 - j]

                @pl.when(lon != g)
                def _(g=g):
                    strip_copy(g, sub).start()

                @pl.when(lon == g)
                def _(g=g):
                    rows = pl.ds(sub * SR, SR)
                    pltpu.make_async_copy(ret.at[g, rows], srecv.at[g, rows], srecv_sem.at[sub, g]).start()

            return carry

        lax.fori_loop(0, NSUB * (NP // NG), ahead, 0)

        def sum_rows(p, sub):
            return ret.at[p, pl.ds(HALF + sub * SR, SR)]

        def sum_to(p, sub):
            return pltpu.make_async_remote_copy(
                src_ref=sum_rows(lon, sub), dst_ref=sum_rows(lon, sub), send_sem=asend.at[sub, p],
                recv_sem=arecv_sem.at[sub, lon], device_id=(lat, p), device_id_type=MESH,
            )

        def add_up(sub, carry):
            def wait_part(p, carry):
                ref = srecv.at[p, pl.ds(sub * SR, SR)]
                pltpu.make_async_copy(ref, ref, srecv_sem.at[sub, p]).wait()
                return carry

            lax.fori_loop(0, NP, wait_part, 0)

            def add(j, carry):
                total = srecv[0, sub * SR + j]
                for p in range(1, NP):
                    total = total + srecv[p, sub * SR + j]
                ret[lon, HALF + sub * SR + j] = total
                return carry

            lax.fori_loop(0, SR, add, 0, unroll=5)

            def send(i, carry):
                sum_to(lax.rem(lon + i, NP), sub).start()
                return carry

            lax.fori_loop(1, NP, send, 0)
            return carry

        lax.fori_loop(0, NSUB, add_up, 0)

        def out_copies(n, act):
            slot = lax.rem(n, 2)
            sub = n // (NP // NG)
            base = lon + lax.rem(n, NP // NG) * NG
            for i in range(NG):
                g = lax.rem(base + i, NP)
                for far in range(2):
                    start = ROWS - SR - sub * SR if far else sub * SR
                    act(pltpu.make_async_copy(
                        pbuf.at[slot, i, far], state_part(g, 1 + start, SR), psem.at[slot, i, far]
                    ))

        def back(n, carry):
            slot = lax.rem(n, 2)
            sub = n // (NP // NG)
            base = lon + lax.rem(n, NP // NG) * NG
            for i in range(NG):
                g = lax.rem(base + i, NP)

                @pl.when(g != lon)
                def _(g=g):
                    pltpu.make_async_copy(sum_rows(g, sub), sum_rows(g, sub), arecv_sem.at[sub, g]).wait()

                for j in range(SR):
                    spec = ret[g, HALF + sub * SR + j]
                    xs[0, (i * SR + j) * SUB : (i * SR + j + 1) * SUB, :] = spec
                    xs[1, (i * SR + SR - 1 - j) * SUB : (i * SR + SR - j) * SUB, :] = spec

            @pl.when(n >= 2)
            def _():
                out_copies(n - 2, lambda copy: copy.wait())

            shape = (NG, SR, SUB, PC)
            for far, keep_it in enumerate(keep(sub)):
                spec = jnp.where(keep_it, xs[far].reshape(shape), 0.0).reshape(NG * SR * SUB, PC)
                pbuf[slot, :, far] = dot3(spec, ghi[far], glo[far]).reshape(shape)
            out_copies(n, lambda copy: copy.start())
            return carry

        steps = NSUB * (NP // NG)
        lax.fori_loop(0, steps, back, 0)
        for n in (steps - 2, steps - 1):
            out_copies(n, lambda copy: copy.wait())

        def sent(n, carry):
            sub = n // (NP - 1)
            p = lax.rem(lon + 1 + lax.rem(n, NP - 1), NP)
            sum_to(p, sub).wait_send()
            strip_copy(p, sub).wait_send()
            return carry

        lax.fori_loop(0, NSUB * (NP - 1), sent, 0)

    @pl.when(depth >= 3)
    def _():
        lane = lax.broadcasted_iota(jnp.int32, (SUB, 128), 1)
        for g in range(NP):
            slot = g % 2
            if g + 1 < NP:
                stage_copy(g + 1, 1 - slot).start()
            stage_copy(g, slot).wait()

            def gather(j, carry, slot=slot):
                head, tail = carry
                head = jnp.where(lane == j, stage[slot, j, :, 0:1], head)
                tail = jnp.where(lane == j, stage[slot, j, :, COLS - 1 : COLS], tail)
                return head, tail

            zeros = jnp.zeros((SUB, 128), F32)
            head, tail = lax.fori_loop(0, ROWS, gather, (zeros, zeros), unroll=18)
            cols[0, g] = head
            cols[1, g] = tail

        def side_copy(i):
            step = NP - 1 if i == 0 else 1
            return pltpu.make_async_remote_copy(
                src_ref=cols.at[i], dst_ref=side.at[i], send_sem=hsend.at[i], recv_sem=hrecv.at[i],
                device_id=(lat, lax.rem(lon + step, NP)), device_id_type=MESH,
            )

        for i in range(2):
            side_copy(i).start()
        stage_copy(0, 0).start()
        for i in range(2):
            side_copy(i).wait()

        own_start = jnp.where(lat == 3, ROWS // 3, 0)

        def out_copy(g, slot, act):
            full = pltpu.make_async_copy(obuf.at[slot], state_part(g, 1, ROWS), osem.at[slot])
            some = pltpu.make_async_copy(
                obuf.at[slot, pl.ds(own_start, 2 * ROWS // 3)],
                state_part(g, 1 + own_start, 2 * ROWS // 3), osem.at[slot],
            )

            @pl.when(depth > 3)
            def _():
                act(full)

            @pl.when(depth == 3)
            def _():
                act(some)

        for g in range(NP):
            slot = g % 2
            if g + 1 < NP:
                stage_copy(g + 1, 1 - slot).start()
            stage_copy(g, slot).wait()
            if g >= 2:
                out_copy(g, slot, lambda copy: copy.wait())

            def insert(j, carry, g=g, slot=slot):
                obuf[slot, j, :, 0:COLS] = stage[slot, j]
                east = pltpu.roll(side[0, g], lax.rem(COLS - 256 + 128 - j, 128), 1)
                west = pltpu.roll(side[1, g], 127 - j, 1)
                tail = obuf[slot, j, :, 256:PC]
                tail = jnp.where(lane == COLS - 256, east, tail)
                obuf[slot, j, :, 256:PC] = jnp.where(lane == 127, west, tail)
                return carry

            lax.fori_loop(0, ROWS, insert, 0, unroll=9)
            out_copy(g, slot, lambda copy: copy.start())
        for slot in range(2):
            out_copy(0, slot, lambda copy: copy.wait())

    @pl.when(is_value | is_off)
    def _():
        half = np.float32(np.sqrt(0.5))

        def chunk(c, carry):
            def arrived(s, carry):
                ref = recv.at[s, pl.ds(c * CR, CR)]
                pltpu.make_async_copy(ref, ref, frecv.at[c, s]).wait()
                return carry

            lax.fori_loop(0, NP, arrived, 0)

            def fold(r, carry):
                rows = pl.ds(pl.multiple_of(r * SUB, SUB), SUB)
                x = [recv[s, c * CR + r] for s in range(NP)]
                s0, s1, s2, s3 = [x[j] + x[j + 4] for j in range(4)]
                d0, d1, d2, d3 = [x[j] - x[j + 4] for j in range(4)]
                plus, minus = half * (d1 + d3), half * (d1 - d3)
                out = (
                    (s0 + s2) + (s1 + s3), (s0 + s2) - (s1 + s3),
                    d0 + minus, -(d2 + plus),
                    s0 - s2, s3 - s1,
                    d0 - minus, d2 - plus,
                )
                for i in range(8):
                    yb[i, rows, 0:COLS] = out[i]
                return carry

            lax.fori_loop(0, CR, fold, 0)
            limit = wide(lim_ref[pl.ds(c * CR, CR)])

            def group(g, carry):
                spec = dot3(yb[2 * g], thi[g, 0:PC, :], tlo[g, 0:PC, :])
                spec += dot3(yb[2 * g + 1], thi[g, PC:, :], tlo[g, PC:, :])
                spec = jnp.where(wv_ref[g] <= limit, spec.reshape(CR, SUB, PC), 0.0).reshape(CR * SUB, PC)
                zb[2 * g] = dot3(spec, uhi[g, :, 0:PC], ulo[g, :, 0:PC])
                zb[2 * g + 1] = dot3(spec, uhi[g, :, PC:], ulo[g, :, PC:])
                return carry

            lax.fori_loop(0, 4, group, 0)

            def unfold(r, carry):
                rows = pl.ds(pl.multiple_of(r * SUB, SUB), SUB)
                a0, b0, a1, b1, a2, b2, a3, b3 = [zb[i, rows, :] for i in range(8)]
                even = (a0 + b0 + a2, a0 - b0 - b2, a0 + b0 - a2, a0 - b0 + b2)
                odd = (a1 + a3, half * ((a1 - a3) - (b1 + b3)), b3 - b1, half * ((a3 - a1) - (b1 + b3)))
                for j in range(4):
                    ret[j, c * CR + r] = even[j] + odd[j]
                    ret[j + 4, c * CR + r] = even[j] - odd[j]
                return carry

            lax.fori_loop(0, CR, unfold, 0)

            @pl.when(served_depth >= 2)
            def _():
                lane = lax.broadcasted_iota(jnp.int32, (SUB, 128), 1)

                def select(r, carry):
                    listed = wide(lim_ref[c * CR + r]) >= 0.0
                    for p in range(NP):
                        rawp[p, :, 0:COLS] = recv[p, c * CR + r]
                    for p in range(NP):
                        east = recv[(p + 1) % NP, c * CR + r, :, 0:1]
                        west = recv[(p + 7) % NP, c * CR + r, :, COLS - 1 : COLS]
                        tail = jnp.where(lane == COLS - 256, east, rawp[p, :, 256:PC])
                        tail = jnp.where(lane == 127, west, tail)
                        raw = jnp.concatenate([rawp[p, :, 0:256], tail], axis=-1)
                        ret[p, c * CR + r] = jnp.where(listed, ret[p, c * CR + r], raw)
                    return carry

                lax.fori_loop(0, CR, select, 0)

            def give_back(i, carry):
                p = lax.rem(lon + i, NP)
                src = ret.at[p, pl.ds(c * CR, CR)]
                dst = state_part(lon, 1 + c * CR, CR)
                local = is_value & (p == lon)

                @pl.when(jnp.logical_not(local))
                def _():
                    pltpu.make_async_remote_copy(
                        src_ref=src, dst_ref=dst, send_sem=rsend.at[c, p],
                        recv_sem=rrecv.at[c, lon], device_id=(served, p), device_id_type=MESH,
                    ).start()

                @pl.when(local)
                def _():
                    pltpu.make_async_copy(src, dst, rrecv.at[c, lon]).start()

                return carry

            lax.fori_loop(0, NP, give_back, 0)
            return carry

        def pass_on(c):
            relay_all(c, lambda copy: copy.wait_recv())
            dst = recv.at[lon, pl.ds(c * CR, CR)]

            def home_part(p):
                return home.at[c, p // 2, :, pl.ds(pl.multiple_of(lax.rem(p, 2) * 8, 8), 8)]

            def to_owner(i, carry):
                p = lax.rem(lon + i, NP)
                pltpu.make_async_remote_copy(
                    src_ref=home_part(p), dst_ref=dst, send_sem=fsend.at[c, p],
                    recv_sem=frecv.at[c, lon], device_id=(lat, p), device_id_type=MESH,
                ).start()
                return carry

            lax.fori_loop(1, NP, to_owner, 0)
            pltpu.make_async_copy(home_part(lon), dst, frecv.at[c, lon]).start()

        n_loc = last - first

        def step(n, carry):
            @pl.when(is_value & (n < n_off))
            def _():
                @pl.when(n >= 2)
                def _():
                    relay_all(n - 2, lambda copy: copy.wait_send())

                relay_all(n, lambda copy: copy.start())

            @pl.when(is_value & (n < n_loc))
            def _():
                stay(first + n)

            @pl.when(is_off & (n < n_off))
            def _():
                pass_on(n)

            @pl.when(n == 1)
            def _():
                for i, (src, dst) in enumerate(tables):
                    pltpu.make_async_copy(src, dst, tab_sem.at[i]).wait()

            lag = jnp.where(is_off, 1, 2)

            @pl.when((n >= lag) & (n < n_loc + lag))
            def _():
                chunk(first + n - lag, 0)

            return carry

        lax.fori_loop(0, jnp.where(is_off, n_off + 1, jnp.maximum(n_off, n_loc + 2)), step, 0)

        def returned(n, carry):
            c = first + n // NP
            p = lax.rem(n, NP)

            @pl.when(is_off | (p != lon))
            def _():
                ref = ret.at[p, pl.ds(c * CR, CR)]
                pltpu.make_async_copy(ref, ref, rsend.at[c, p]).wait()

            @pl.when(p != lon)
            def _():
                ref = recv.at[p, pl.ds(c * CR, CR)]
                pltpu.make_async_copy(ref, ref, fsend.at[c, p]).wait()

            return carry

        lax.fori_loop(0, (last - first) * NP, returned, 0)

    @pl.when(is_value)
    def _():
        def drain(n, carry):
            c = begin + n // NP
            p = lax.rem(n, NP)

            dst = state_part(p, 1 + c * CR, CR)
            pltpu.make_async_copy(dst, dst, rrecv.at[c, p]).wait()
            return carry

        lax.fori_loop(0, (end - begin) * NP, drain, 0)

        def relayed(c, carry):
            relay_all(c, lambda copy: copy.wait_send())
            return carry

        lax.fori_loop(jnp.maximum(n_off - 2, 0), n_off, relayed, 0)

    def edge_copy(i):
        row, there, step = ((1, ROWS + 1, 15), (ROWS, 0, 1))[i]
        return pltpu.make_async_remote_copy(
            src_ref=state_ref.at[:, row], dst_ref=state_ref.at[:, there],
            send_sem=lsend.at[i], recv_sem=lrecv.at[i],
            device_id=(lax.rem(lat + step, 16), lon), device_id_type=MESH,
        )

    def blank(row):
        return pltpu.make_async_copy(zero, state_ref.at[:, row], zsem)

    inner = (lat > 0, lat < 15)
    for i in range(2):
        @pl.when(inner[i])
        def _(i=i):
            edge_copy(i).start()

    for i, row in ((0, 0), (1, ROWS + 1)):
        @pl.when(jnp.logical_not(inner[i]))
        def _(row=row):
            zero[...] = jnp.zeros_like(zero)
            blank(row).start()
            blank(row).wait()

    for i in range(2):
        @pl.when(inner[i])
        def _(i=i):
            edge_copy(i).wait_send()

        @pl.when(inner[1 - i])
        def _(i=i):
            edge_copy(i).wait_recv()


def stencil_kernel(trig_ref, state_ref, wind_out, t_out, h_out):
    base = lax.axis_index("lat") * ROWS + pl.program_id(0) * BLOCK

    def dx(a):
        return pltpu.roll(a, PC - 1, 1) - pltpu.roll(a, 1, 1)

    def one(r, carry):
        at = base + r
        cos_n, cos_s = trig_ref[0, at], trig_ref[0, at + 2]
        inv = trig_ref[1, at + 1]
        turn = 0.3 * trig_ref[2, at + 1]
        u, v, t, h = [state_ref[k, r + 1] for k in range(4)]
        un, vn, tn, hn = [state_ref[k, r] for k in range(4)]
        us, vs, ts, hs = [state_ref[k, r + 2] for k in range(4)]
        cu = (0.025 * inv) * u
        cv = 0.1 * v
        new_h = h - (0.025 * inv) * dx(u * h) - (0.1 * inv) * (vs * hs * cos_s - vn * hn * cos_n)
        new_t = t - cu * dx(t) - cv * (ts - tn)
        new_u = u - cu * dx(u) - cv * (us - un) - (0.05 * inv) * dx(h) + turn * v
        new_v = v - cu * dx(v) - cv * (vs - vn) - 0.15 * (hs - hn) - turn * u
        wind_out[0, r] = new_u[:, 0:COLS]
        wind_out[1, r] = new_v[:, 0:COLS]
        t_out[r] = new_t[:, 0:COLS]
        h_out[r] = new_h[:, 0:COLS]
        return carry

    lax.fori_loop(0, BLOCK, one, 0, unroll=True)


@functools.lru_cache(maxsize=None)
def trig_table():
    row = np.arange(-1, NLAT + 1).astype(np.float32) + np.float32(0.5)
    angle = (row * np.float32(np.pi / NLAT)).astype(np.float64)
    cos = np.sin(angle).astype(np.float32)
    sin = -np.cos(angle).astype(np.float32)
    return np.stack([cos, (1.0 / cos.astype(np.float64)).astype(np.float32), sin])


def body(winds, theta, thick, polar_rows, cutoffs):
    lat = lax.axis_index("lat")
    served = jnp.where((lat >= 4) & (lat < 8), lat - 4, jnp.where((lat >= 8) & (lat < 12), lat + 4, lat))
    rows = served * ROWS + jnp.arange(ROWS, dtype=jnp.int32)
    hits = polar_rows[None, :] == rows[:, None]
    limit = jnp.max(jnp.where(hits, cutoffs[None, :], -1), axis=1).astype(F32)
    lim = jnp.broadcast_to(limit[:, None, None], (ROWS, SUB, 128))
    thi, tlo, uhi, ulo, wv = value_tables()
    fhi, flo, ghi, glo, wp = packed_tables()
    vm = pl.BlockSpec(memory_space=pltpu.VMEM)
    hbm = pl.BlockSpec(memory_space=pl.ANY)
    dma = pltpu.SemaphoreType.DMA
    state = pl.pallas_call(
        filter_kernel,
        out_shape=jax.ShapeDtypeStruct((4, ROWS + 2, LEV, PC), F32),
        in_specs=[hbm, hbm, hbm, vm, vm, vm] + [hbm] * 8,
        out_specs=hbm,
        scratch_shapes=[
            pltpu.VMEM((4, 2 * PC, PC), BF16), pltpu.VMEM((4, 2 * PC, PC), BF16),
            pltpu.VMEM((4, PC, 2 * PC), BF16), pltpu.VMEM((4, PC, 2 * PC), BF16),
            pltpu.VMEM((2, PC, PC), BF16), pltpu.VMEM((2, PC, PC), BF16),
            pltpu.VMEM((2, PC, PC), BF16), pltpu.VMEM((2, PC, PC), BF16),
            pltpu.VMEM((NP, ROWS, SUB, COLS), F32),
            pltpu.VMEM((NP, ROWS, SUB, PC), F32),
            pltpu.VMEM((NP, HALF, SUB, PC), F32),
            pltpu.VMEM((2, ROWS, SUB, COLS), F32),
            pltpu.VMEM((2, ROWS, SUB, PC), F32),
            pltpu.VMEM((2, NG, 2, SR, SUB, PC), F32),
            pltpu.VMEM((2, NG * SR * SUB, PC), F32),
            pltpu.VMEM((8, CR * SUB, PC), F32),
            pltpu.VMEM((8, CR * SUB, PC), F32),
            pltpu.VMEM((NP, SUB, PC), F32),
            pltpu.VMEM((2, NP, SUB, 128), F32),
            pltpu.VMEM((2, NP, SUB, 128), F32),
            pltpu.VMEM((4, LEV, PC), F32),
            pltpu.VMEM((max(OFF1, OFF2), 4, CR, LEV, COLS), F32),
            dma((4,)), dma((2,)),
            dma((NCH, NP)), dma((NCH, NP)), dma((NCH, NP)), dma((NCH, NP)),
            dma((NSUB, NP)), dma((NSUB, NP)), dma((NSUB, NP)), dma((NSUB, NP)),
            dma((2,)), dma((2,)), dma((2,)), dma((2,)), dma((2,)), dma,
            dma((NCH, 4)), dma((NCH, 4)), dma((NP,)), dma((2, NG, 2)),
        ],
        compiler_params=pltpu.CompilerParams(
            collective_id=1, has_side_effects=True, vmem_limit_bytes=60 * 2**20
        ),
        name="polar_filter",
    )(
        winds.transpose(0, 2, 1, 3), theta.transpose(1, 0, 2), thick.transpose(1, 0, 2), lim,
        jnp.asarray(wv)[:, None, :], jnp.asarray(wp), thi, tlo, uhi, ulo, fhi, flo, ghi, glo,
    )
    new_winds, new_t, new_h = pl.pallas_call(
        stencil_kernel,
        grid=(ROWS // BLOCK,),
        out_shape=(
            jax.ShapeDtypeStruct((2, ROWS, LEV, COLS), F32),
            jax.ShapeDtypeStruct((ROWS, LEV, COLS), F32),
            jax.ShapeDtypeStruct((ROWS, LEV, COLS), F32),
        ),
        in_specs=[
            pl.BlockSpec(memory_space=pltpu.SMEM),
            pl.BlockSpec(
                (pl.Element(4), pl.Element(BLOCK + 2), pl.Element(LEV), pl.Element(PC)),
                lambda i: (0, i * BLOCK, 0, 0),
            ),
        ],
        out_specs=(
            pl.BlockSpec((2, BLOCK, LEV, COLS), lambda i: (0, i, 0, 0)),
            pl.BlockSpec((BLOCK, LEV, COLS), lambda i: (i, 0, 0)),
            pl.BlockSpec((BLOCK, LEV, COLS), lambda i: (i, 0, 0)),
        ),
        compiler_params=pltpu.CompilerParams(vmem_limit_bytes=60 * 2**20),
        name="stencil",
    )(jnp.asarray(trig_table()), state)
    return new_winds.transpose(0, 2, 1, 3), new_t.transpose(1, 0, 2), new_h.transpose(1, 0, 2)


def solution(mesh):
    in_specs = (P(None, None, "lat", "lon"), P(None, "lat", "lon"), P(None, "lat", "lon"), P(), P())
    out_specs = (P(None, None, "lat", "lon"), P(None, "lat", "lon"), P(None, "lat", "lon"))
    return jax.shard_map(body, mesh=mesh, in_specs=in_specs, out_specs=out_specs, check_vma=False)
```

```python
import functools

import jax
import jax.numpy as jnp
import numpy as np
from jax import lax
from jax.experimental import pallas as pl
from jax.experimental.pallas import tpu as pltpu
from jax.sharding import PartitionSpec as P

NLON = 2880
NLAT = 1440
LEV = 16
ROWS = 90
COLS = 360
HALF = ROWS // 2
PC = 384
NP = 8
SUB = 8
NCH = 15
CR = ROWS // NCH
OFF1 = 10
OFF2 = 7
NSUB = 3
SR = HALF // NSUB
NG = 4
BLOCK = 18
MESH = pl.DeviceIdType.MESH
F32 = jnp.float32
BF16 = jnp.bfloat16


def split(table):
    hi = table.astype(np.float32).astype(BF16)
    lo = (table - hi.astype(np.float64)).astype(np.float32).astype(BF16)
    return np.asarray(hi), np.asarray(lo)


@functools.lru_cache(maxsize=None)
def value_tables():
    q = np.arange(PC)
    q = np.where(q == PC - 1, -1, q)
    forward = np.zeros((4, 2 * PC, PC))
    inverse = np.zeros((4, PC, 2 * PC))
    waves = np.full((4, PC), 1e9)
    m = np.arange(90)
    for g in range(4):
        parts = [(0, 0, 0), (4, 1, 0)] if g == 0 else [(g, 0, 1), (8 - g, 0, -1)]
        for slot, (r, half, sign) in enumerate(parts):
            k = 8 * m + r
            angle = 2.0 * np.pi * ((k[:, None] * q[None, :]) % NLON) / NLON
            cos, sin = np.cos(angle), np.sin(angle)
            re = slice(slot * 180, slot * 180 + 90)
            im = slice(slot * 180 + 90, slot * 180 + 180)
            waves[g, re] = k
            waves[g, im] = k
            weight = np.where(k == 0, 1.0, 2.0)[:, None] / NLON
            own = np.zeros((PC, 2 * PC))
            if sign == 0:
                own[re, half * PC : (half + 1) * PC] = cos
                own[im, half * PC : (half + 1) * PC] = -sin
            else:
                own[re, :PC] = cos
                own[im, :PC] = -sin
                own[re, PC:] = sign * sin
                own[im, PC:] = sign * cos
            scaled = own.copy()
            scaled[re] *= weight
            scaled[im] *= weight
            inverse[g] += scaled
            keep = np.concatenate([np.arange(PC) < COLS] * 2)
            forward[g] += (own * keep[None, :]).T
    used = np.concatenate([(np.arange(PC) <= COLS) | (np.arange(PC) == PC - 1)] * 2)
    inverse = inverse * used[None, None, :]
    return split(forward) + split(inverse) + (waves.astype(np.float32),)


@functools.lru_cache(maxsize=None)
def packed_tables():
    lane = np.arange(PC)
    wave = (lane + 1) // 2
    is_cos = (lane == 0) | (lane % 2 == 1)
    q = np.arange(PC)
    q = np.where(q == PC - 1, -1, q)
    used = (np.arange(PC) <= COLS) | (np.arange(PC) == PC - 1)
    forward = np.zeros((NP, 2, PC, PC))
    inverse = np.zeros((NP, 2, PC, PC))
    for p in range(NP):
        n = COLS * p + q
        angle = 2.0 * np.pi * ((wave[:, None] * n[None, :]) % NLON) / NLON
        base = np.where(is_cos[:, None], np.cos(angle), np.sin(angle))
        weight = np.where(wave == 0, 1.0, 2.0)[:, None] / NLON
        back = base * weight * used[None, :]
        ahead = (base * (np.arange(PC) < COLS)[None, :]).T
        forward[p, 0], forward[p, 1] = ahead, ahead[:, ::-1]
        inverse[p, 0], inverse[p, 1] = back, back[::-1]
    waves = np.stack([wave, wave[::-1]]).astype(np.float32)
    return split(forward) + split(inverse) + (waves,)


def dot3(x, hi, lo):
    x_hi = x.astype(BF16)
    x_lo = (x - x_hi.astype(F32)).astype(BF16)
    count = x.shape[0]
    both = jnp.dot(jnp.concatenate([x_lo, x_hi], axis=0), hi, preferred_element_type=F32)
    return jnp.dot(x_hi, lo, preferred_element_type=F32) + both[:count] + both[count:]


def wide(lim):
    return jnp.concatenate([lim, lim, lim], axis=-1)


def filter_kernel(
    w_ref, t_ref, h_ref, lim_ref, wv_ref, wp_ref,
    thi_ref, tlo_ref, uhi_ref, ulo_ref, fhi_ref, flo_ref, ghi_ref, glo_ref,
    state_ref,
    thi, tlo, uhi, ulo, fhi, flo, ghi, glo,
    recv, ret, srecv, stage, obuf, pbuf, xs, yb, zb, rawp, cols, side, zero, home,
    tab_sem, stage_sem, fsend, frecv, rsend, rrecv, ssend, srecv_sem, asend, arecv_sem,
    hsend, hrecv, lsend, lrecv, osem, zsem, xsend, xrecv, part_sem, psem,
):
    lat = lax.axis_index("lat")
    lon = lax.axis_index("lon")
    north = lat < 8
    depth = jnp.where(north, lat, 15 - lat)
    partner = jnp.where(north, jnp.where(lat < 4, lat + 4, lat - 4), jnp.where(lat >= 12, lat - 4, lat + 4))
    is_packed = depth == 0
    is_value = (depth >= 1) & (depth <= 3)
    is_off = (depth == 5) | (depth == 6)
    served = jnp.where(is_off, partner, lat)
    served_depth = jnp.where(is_off, depth - 4, depth)
    n_off = jnp.where(served_depth == 1, OFF1, jnp.where(served_depth == 2, OFF2, 0))
    begin = jnp.where(served == 12, 2 * NCH // 3, 0)
    end = jnp.where(served == 3, NCH // 3, NCH)
    first = jnp.where(is_off, 0, jnp.maximum(begin, n_off))
    last = jnp.where(is_off, n_off, end)
    sources = (w_ref.at[0], w_ref.at[1], t_ref, h_ref)

    bar = pltpu.get_barrier_semaphore()
    for i in range(1, NP):
        pl.semaphore_signal(bar, inc=1, device_id=(lat, lax.rem(lon + i, NP)), device_id_type=MESH)
    for i in (1, 15):
        pl.semaphore_signal(bar, inc=1, device_id=(lax.rem(lat + i, 16), lon), device_id_type=MESH)
    n_signals = 9
    if OFF1 or OFF2:
        for i in range(NP):
            pl.semaphore_signal(bar, inc=1, device_id=(partner, lax.rem(lon + i, NP)), device_id_type=MESH)
        n_signals += NP

    tables = ((thi_ref, thi), (tlo_ref, tlo), (uhi_ref, uhi), (ulo_ref, ulo))
    packs = ((fhi_ref, fhi), (flo_ref, flo), (ghi_ref, ghi), (glo_ref, glo))

    @pl.when(is_packed)
    def _():
        for i, (src, dst) in enumerate(packs):
            pltpu.make_async_copy(src.at[lon], dst, tab_sem.at[i]).start()

    @pl.when(is_value | is_off)
    def _():
        for i, (src, dst) in enumerate(tables):
            pltpu.make_async_copy(src, dst, tab_sem.at[i]).start()
        yb[...] = jnp.zeros_like(yb)

    def part(g, rows):
        return sources[g // 2].at[rows, 8 * (g % 2) : 8 * (g % 2) + 8]

    def whole_part(g):
        return pltpu.make_async_copy(part(g, slice(0, ROWS)), recv.at[g], part_sem.at[g])

    @pl.when(is_packed)
    def _():
        for g in range(NP):
            whole_part(g).start()

    def stage_copy(g, slot):
        return pltpu.make_async_copy(part(g, slice(0, ROWS)), stage.at[slot], stage_sem.at[slot])

    def state_part(p, start, count):
        return state_ref.at[p // 2, pl.ds(start, count), pl.ds(pl.multiple_of(lax.rem(p, 2) * 8, 8), 8)]

    @pl.when(depth >= 3)
    def _():
        stage_copy(0, 0).start()

    pl.semaphore_wait(bar, n_signals)

    def relay(c, k):
        return pltpu.make_async_remote_copy(
            src_ref=sources[k].at[pl.ds(c * CR, CR)], dst_ref=home.at[c, k],
            send_sem=xsend.at[c, k], recv_sem=xrecv.at[c, k],
            device_id=(partner, lon), device_id_type=MESH,
        )

    def relay_all(c, act):
        for k in range(4):
            act(relay(c, k))

    def stay(c):
        def per_owner(i, carry):
            p = lax.rem(lon + i, NP)
            dst = recv.at[lon, pl.ds(c * CR, CR)]
            half = pl.ds(pl.multiple_of(lax.rem(p, 2) * 8, 8), 8)
            for k in range(4):
                src = sources[k].at[pl.ds(c * CR, CR), half]

                @pl.when((p // 2 == k) & (p != lon))
                def _(src=src):
                    pltpu.make_async_remote_copy(
                        src_ref=src, dst_ref=dst, send_sem=fsend.at[c, p],
                        recv_sem=frecv.at[c, lon], device_id=(lat, p), device_id_type=MESH,
                    ).start()

                @pl.when((p // 2 == k) & (p == lon))
                def _(src=src):
                    pltpu.make_async_copy(src, dst, frecv.at[c, lon]).start()

            return carry

        lax.fori_loop(0, NP, per_owner, 0)

    def strip_copy(p, sub):
        rows = pl.ds(sub * SR, SR)
        return pltpu.make_async_remote_copy(
            src_ref=ret.at[p, rows], dst_ref=srecv.at[lon, rows], send_sem=ssend.at[sub, p],
            recv_sem=srecv_sem.at[sub, lon], device_id=(lat, p), device_id_type=MESH,
        )

    @pl.when(is_packed)
    def _():
        xs[...] = jnp.zeros_like(xs)
        for i, (src, dst) in enumerate(packs):
            pltpu.make_async_copy(src.at[lon], dst, tab_sem.at[i]).wait()
        for g in range(NP):
            whole_part(g).wait()

        def keep(sub):
            near = wp_ref[0:1, :] <= wide(lim_ref[pl.ds(sub * SR, SR)])
            far = wp_ref[1:2, :] <= wide(lim_ref[pl.ds(ROWS - SR - sub * SR, SR)])
            return near[None], far[None]

        def ahead(n, carry):
            sub = n // (NP // NG)
            base = lon + 1 + lax.rem(n, NP // NG) * NG
            for i in range(NG):
                g = lax.rem(base + i, NP)
                near = recv[g, pl.ds(sub * SR, SR)].reshape(SR * SUB, COLS)
                far = recv[g, pl.ds(ROWS - SR - sub * SR, SR)].reshape(SR * SUB, COLS)
                xs[0, i * SR * SUB : (i + 1) * SR * SUB, 0:COLS] = near
                xs[1, i * SR * SUB : (i + 1) * SR * SUB, 0:COLS] = far
            keep_near, keep_far = keep(sub)
            shape = (NG, SR, SUB, PC)
            pbuf[0, :, 0] = jnp.where(keep_near, dot3(xs[0], fhi[0], flo[0]).reshape(shape), 0.0)
            pbuf[0, :, 1] = jnp.where(keep_far, dot3(xs[1], fhi[1], flo[1]).reshape(shape), 0.0)
            for i in range(NG):
                g = lax.rem(base + i, NP)
                for j in range(SR):
                    ret[g, sub * SR + j] = pbuf[0, i, 0, j] + pbuf[0, i, 1, SR - 1 - j]

                @pl.when(lon != g)
                def _(g=g):
                    strip_copy(g, sub).start()

                @pl.when(lon == g)
                def _(g=g):
                    rows = pl.ds(sub * SR, SR)
                    pltpu.make_async_copy(ret.at[g, rows], srecv.at[g, rows], srecv_sem.at[sub, g]).start()

            return carry

        lax.fori_loop(0, NSUB * (NP // NG), ahead, 0)

        def sum_rows(p, sub):
            return ret.at[p, pl.ds(HALF + sub * SR, SR)]

        def sum_to(p, sub):
            return pltpu.make_async_remote_copy(
                src_ref=sum_rows(lon, sub), dst_ref=sum_rows(lon, sub), send_sem=asend.at[sub, p],
                recv_sem=arecv_sem.at[sub, lon], device_id=(lat, p), device_id_type=MESH,
            )

        def add_up(sub, carry):
            def wait_part(p, carry):
                ref = srecv.at[p, pl.ds(sub * SR, SR)]
                pltpu.make_async_copy(ref, ref, srecv_sem.at[sub, p]).wait()
                return carry

            lax.fori_loop(0, NP, wait_part, 0)

            def add(j, carry):
                total = srecv[0, sub * SR + j]
                for p in range(1, NP):
                    total = total + srecv[p, sub * SR + j]
                ret[lon, HALF + sub * SR + j] = total
                return carry

            lax.fori_loop(0, SR, add, 0, unroll=5)

            def send(i, carry):
                sum_to(lax.rem(lon + i, NP), sub).start()
                return carry

            lax.fori_loop(1, NP, send, 0)
            return carry

        lax.fori_loop(0, NSUB, add_up, 0)

        def out_copies(n, act):
            slot = lax.rem(n, 2)
            sub = n // (NP // NG)
            base = lon + lax.rem(n, NP // NG) * NG
            for i in range(NG):
                g = lax.rem(base + i, NP)
                for far in range(2):
                    start = ROWS - SR - sub * SR if far else sub * SR
                    act(pltpu.make_async_copy(
                        pbuf.at[slot, i, far], state_part(g, 1 + start, SR), psem.at[slot, i, far]
                    ))

        def back(n, carry):
            slot = lax.rem(n, 2)
            sub = n // (NP // NG)
            base = lon + lax.rem(n, NP // NG) * NG
            for i in range(NG):
                g = lax.rem(base + i, NP)

                @pl.when(g != lon)
                def _(g=g):
                    pltpu.make_async_copy(sum_rows(g, sub), sum_rows(g, sub), arecv_sem.at[sub, g]).wait()

                for j in range(SR):
                    spec = ret[g, HALF + sub * SR + j]
                    xs[0, (i * SR + j) * SUB : (i * SR + j + 1) * SUB, :] = spec
                    xs[1, (i * SR + SR - 1 - j) * SUB : (i * SR + SR - j) * SUB, :] = spec

            @pl.when(n >= 2)
            def _():
                out_copies(n - 2, lambda copy: copy.wait())

            shape = (NG, SR, SUB, PC)
            for far, keep_it in enumerate(keep(sub)):
                spec = jnp.where(keep_it, xs[far].reshape(shape), 0.0).reshape(NG * SR * SUB, PC)
                pbuf[slot, :, far] = dot3(spec, ghi[far], glo[far]).reshape(shape)
            out_copies(n, lambda copy: copy.start())
            return carry

        steps = NSUB * (NP // NG)
        lax.fori_loop(0, steps, back, 0)
        for n in (steps - 2, steps - 1):
            out_copies(n, lambda copy: copy.wait())

        def sent(n, carry):
            sub = n // (NP - 1)
            p = lax.rem(lon + 1 + lax.rem(n, NP - 1), NP)
            sum_to(p, sub).wait_send()
            strip_copy(p, sub).wait_send()
            return carry

        lax.fori_loop(0, NSUB * (NP - 1), sent, 0)

    def side_copy(i):
        step = NP - 1 if i == 0 else 1
        return pltpu.make_async_remote_copy(
            src_ref=cols.at[i], dst_ref=side.at[i], send_sem=hsend.at[i], recv_sem=hrecv.at[i],
            device_id=(lat, lax.rem(lon + step, NP)), device_id_type=MESH,
        )

    own_start = jnp.where(lat == 3, ROWS // 3, 0)

    def raw_copy(g, slot, act):
        full = pltpu.make_async_copy(obuf.at[slot], state_part(g, 1, ROWS), osem.at[slot])
        some = pltpu.make_async_copy(
            obuf.at[slot, pl.ds(own_start, 2 * ROWS // 3)],
            state_part(g, 1 + own_start, 2 * ROWS // 3), osem.at[slot],
        )

        @pl.when(depth > 3)
        def _():
            act(full)

        @pl.when(depth == 3)
        def _():
            act(some)

    def raw_out(g, carry):
        slot = lax.rem(g, 2)
        half = pl.ds(pl.multiple_of(slot * 8, 8), 8)
        for k in range(4):
            @pl.when(g // 2 == k)
            def _(k=k):
                pltpu.make_async_copy(sources[k].at[:, half], stage.at[slot], stage_sem.at[slot]).start()

        @pl.when(g >= 2)
        def _():
            raw_copy(g - 2, slot, lambda copy: copy.wait())

        pltpu.make_async_copy(stage.at[slot], stage.at[slot], stage_sem.at[slot]).wait()
        lane = lax.broadcasted_iota(jnp.int32, (SUB, 128), 1)

        def insert(j, carry):
            obuf[slot, j, :, 0:COLS] = stage[slot, j]
            east = pltpu.roll(side[0, g], lax.rem(COLS - 256 + 128 - j, 128), 1)
            west = pltpu.roll(side[1, g], 127 - j, 1)
            tail = obuf[slot, j, :, 256:PC]
            tail = jnp.where(lane == COLS - 256, east, tail)
            obuf[slot, j, :, 256:PC] = jnp.where(lane == 127, west, tail)
            return carry

        lax.fori_loop(0, ROWS, insert, 0, unroll=9)
        raw_copy(g, slot, lambda copy: copy.start())
        return carry

    @pl.when(depth >= 3)
    def _():
        lane = lax.broadcasted_iota(jnp.int32, (SUB, 128), 1)
        for g in range(NP):
            slot = g % 2
            if g + 1 < NP:
                stage_copy(g + 1, 1 - slot).start()
            stage_copy(g, slot).wait()

            def gather(j, carry, slot=slot):
                head, tail = carry
                head = jnp.where(lane == j, stage[slot, j, :, 0:1], head)
                tail = jnp.where(lane == j, stage[slot, j, :, COLS - 1 : COLS], tail)
                return head, tail

            zeros = jnp.zeros((SUB, 128), F32)
            head, tail = lax.fori_loop(0, ROWS, gather, (zeros, zeros), unroll=18)
            cols[0, g] = head
            cols[1, g] = tail

        for i in range(2):
            side_copy(i).start()

        @pl.when(jnp.logical_not(is_off))
        def _():
            for i in range(2):
                side_copy(i).wait()
            lax.fori_loop(0, NP, raw_out, 0)

    @pl.when(is_value | is_off)
    def _():
        half = np.float32(np.sqrt(0.5))

        def chunk(c, carry):
            def arrived(s, carry):
                ref = recv.at[s, pl.ds(c * CR, CR)]
                pltpu.make_async_copy(ref, ref, frecv.at[c, s]).wait()
                return carry

            lax.fori_loop(0, NP, arrived, 0)

            def fold(r, carry):
                rows = pl.ds(pl.multiple_of(r * SUB, SUB), SUB)
                x = [recv[s, c * CR + r] for s in range(NP)]
                s0, s1, s2, s3 = [x[j] + x[j + 4] for j in range(4)]
                d0, d1, d2, d3 = [x[j] - x[j + 4] for j in range(4)]
                plus, minus = half * (d1 + d3), half * (d1 - d3)
                out = (
                    (s0 + s2) + (s1 + s3), (s0 + s2) - (s1 + s3),
                    d0 + minus, -(d2 + plus),
                    s0 - s2, s3 - s1,
                    d0 - minus, d2 - plus,
                )
                for i in range(8):
                    yb[i, rows, 0:COLS] = out[i]
                return carry

            lax.fori_loop(0, CR, fold, 0, unroll=3)
            limit = wide(lim_ref[pl.ds(c * CR, CR)])

            def group(g, carry):
                spec = dot3(yb[2 * g], thi[g, 0:PC, :], tlo[g, 0:PC, :])
                spec += dot3(yb[2 * g + 1], thi[g, PC:, :], tlo[g, PC:, :])
                spec = jnp.where(wv_ref[g] <= limit, spec.reshape(CR, SUB, PC), 0.0).reshape(CR * SUB, PC)
                zb[2 * g] = dot3(spec, uhi[g, :, 0:PC], ulo[g, :, 0:PC])
                zb[2 * g + 1] = dot3(spec, uhi[g, :, PC:], ulo[g, :, PC:])
                return carry

            lax.fori_loop(0, 4, group, 0)

            def unfold(r, carry):
                rows = pl.ds(pl.multiple_of(r * SUB, SUB), SUB)
                a0, b0, a1, b1, a2, b2, a3, b3 = [zb[i, rows, :] for i in range(8)]
                even = (a0 + b0 + a2, a0 - b0 - b2, a0 + b0 - a2, a0 - b0 + b2)
                odd = (a1 + a3, half * ((a1 - a3) - (b1 + b3)), b3 - b1, half * ((a3 - a1) - (b1 + b3)))
                for j in range(4):
                    ret[j, c * CR + r] = even[j] + odd[j]
                    ret[j + 4, c * CR + r] = even[j] - odd[j]
                return carry

            lax.fori_loop(0, CR, unfold, 0, unroll=3)

            @pl.when(served_depth >= 2)
            def _():
                lane = lax.broadcasted_iota(jnp.int32, (SUB, 128), 1)

                def select(r, carry):
                    listed = wide(lim_ref[c * CR + r]) >= 0.0
                    for p in range(NP):
                        rawp[p, :, 0:COLS] = recv[p, c * CR + r]
                    for p in range(NP):
                        east = recv[(p + 1) % NP, c * CR + r, :, 0:1]
                        west = recv[(p + 7) % NP, c * CR + r, :, COLS - 1 : COLS]
                        tail = jnp.where(lane == COLS - 256, east, rawp[p, :, 256:PC])
                        tail = jnp.where(lane == 127, west, tail)
                        raw = jnp.concatenate([rawp[p, :, 0:256], tail], axis=-1)
                        ret[p, c * CR + r] = jnp.where(listed, ret[p, c * CR + r], raw)
                    return carry

                lax.fori_loop(0, CR, select, 0, unroll=2)

            def give_back(i, carry):
                p = lax.rem(lon + i, NP)
                src = ret.at[p, pl.ds(c * CR, CR)]
                dst = state_part(lon, 1 + c * CR, CR)
                local = is_value & (p == lon)

                @pl.when(jnp.logical_not(local))
                def _():
                    pltpu.make_async_remote_copy(
                        src_ref=src, dst_ref=dst, send_sem=rsend.at[c, p],
                        recv_sem=rrecv.at[c, lon], device_id=(served, p), device_id_type=MESH,
                    ).start()

                @pl.when(local)
                def _():
                    pltpu.make_async_copy(src, dst, rrecv.at[c, lon]).start()

                return carry

            lax.fori_loop(0, NP, give_back, 0)
            return carry

        def pass_on(c):
            relay_all(c, lambda copy: copy.wait_recv())
            dst = recv.at[lon, pl.ds(c * CR, CR)]

            def home_part(p):
                return home.at[c, p // 2, :, pl.ds(pl.multiple_of(lax.rem(p, 2) * 8, 8), 8)]

            def to_owner(i, carry):
                p = lax.rem(lon + i, NP)
                pltpu.make_async_remote_copy(
                    src_ref=home_part(p), dst_ref=dst, send_sem=fsend.at[c, p],
                    recv_sem=frecv.at[c, lon], device_id=(lat, p), device_id_type=MESH,
                ).start()
                return carry

            lax.fori_loop(1, NP, to_owner, 0)
            pltpu.make_async_copy(home_part(lon), dst, frecv.at[c, lon]).start()

        n_loc = last - first

        def step(n, carry):
            @pl.when(is_value & (n < n_off))
            def _():
                @pl.when(n >= 2)
                def _():
                    relay_all(n - 2, lambda copy: copy.wait_send())

                relay_all(n, lambda copy: copy.start())

            @pl.when(is_value & (n < n_loc))
            def _():
                stay(first + n)

            @pl.when(is_off & (n < n_off))
            def _():
                pass_on(n)

            @pl.when(n == 1)
            def _():
                for i, (src, dst) in enumerate(tables):
                    pltpu.make_async_copy(src, dst, tab_sem.at[i]).wait()

            lag = jnp.where(is_off, 1, 2)

            @pl.when((n >= lag) & (n < n_loc + lag))
            def _():
                chunk(first + n - lag, 0)

            @pl.when(is_off & (n >= 1))
            def _():
                @pl.when(n == 1)
                def _():
                    for i in range(2):
                        side_copy(i).wait()

                lax.fori_loop(jnp.minimum(n - 1, NP), jnp.where(n == n_off, NP, jnp.minimum(n, NP)), raw_out, 0)

            return carry

        lax.fori_loop(0, jnp.where(is_off, n_off + 1, jnp.maximum(n_off, n_loc + 2)), step, 0)

        def returned(n, carry):
            c = first + n // NP
            p = lax.rem(n, NP)

            @pl.when(is_off | (p != lon))
            def _():
                ref = ret.at[p, pl.ds(c * CR, CR)]
                pltpu.make_async_copy(ref, ref, rsend.at[c, p]).wait()

            @pl.when(p != lon)
            def _():
                ref = recv.at[p, pl.ds(c * CR, CR)]
                pltpu.make_async_copy(ref, ref, fsend.at[c, p]).wait()

            return carry

        lax.fori_loop(0, (last - first) * NP, returned, 0)

    @pl.when(is_value)
    def _():
        def drain(n, carry):
            c = begin + n // NP
            p = lax.rem(n, NP)

            dst = state_part(p, 1 + c * CR, CR)
            pltpu.make_async_copy(dst, dst, rrecv.at[c, p]).wait()
            return carry

        lax.fori_loop(0, (end - begin) * NP, drain, 0)

        def relayed(c, carry):
            relay_all(c, lambda copy: copy.wait_send())
            return carry

        lax.fori_loop(jnp.maximum(n_off - 2, 0), n_off, relayed, 0)

    @pl.when(depth >= 3)
    def _():
        for slot in range(2):
            raw_copy(slot, slot, lambda copy: copy.wait())

    def edge_copy(i):
        row, there, step = ((1, ROWS + 1, 15), (ROWS, 0, 1))[i]
        return pltpu.make_async_remote_copy(
            src_ref=state_ref.at[:, row], dst_ref=state_ref.at[:, there],
            send_sem=lsend.at[i], recv_sem=lrecv.at[i],
            device_id=(lax.rem(lat + step, 16), lon), device_id_type=MESH,
        )

    def blank(row):
        return pltpu.make_async_copy(zero, state_ref.at[:, row], zsem)

    inner = (lat > 0, lat < 15)
    for i in range(2):
        @pl.when(inner[i])
        def _(i=i):
            edge_copy(i).start()

    for i, row in ((0, 0), (1, ROWS + 1)):
        @pl.when(jnp.logical_not(inner[i]))
        def _(row=row):
            zero[...] = jnp.zeros_like(zero)
            blank(row).start()
            blank(row).wait()

    for i in range(2):
        @pl.when(inner[i])
        def _(i=i):
            edge_copy(i).wait_send()

        @pl.when(inner[1 - i])
        def _(i=i):
            edge_copy(i).wait_recv()


def stencil_kernel(trig_ref, state_ref, wind_out, t_out, h_out):
    base = lax.axis_index("lat") * ROWS + pl.program_id(0) * BLOCK

    def dx(a):
        return pltpu.roll(a, PC - 1, 1) - pltpu.roll(a, 1, 1)

    def one(r, carry):
        at = base + r
        cos_n, cos_s = trig_ref[0, at], trig_ref[0, at + 2]
        inv = trig_ref[1, at + 1]
        turn = 0.3 * trig_ref[2, at + 1]
        u, v, t, h = [state_ref[k, r + 1] for k in range(4)]
        un, vn, tn, hn = [state_ref[k, r] for k in range(4)]
        us, vs, ts, hs = [state_ref[k, r + 2] for k in range(4)]
        cu = (0.025 * inv) * u
        cv = 0.1 * v
        new_h = h - (0.025 * inv) * dx(u * h) - (0.1 * inv) * (vs * hs * cos_s - vn * hn * cos_n)
        new_t = t - cu * dx(t) - cv * (ts - tn)
        new_u = u - cu * dx(u) - cv * (us - un) - (0.05 * inv) * dx(h) + turn * v
        new_v = v - cu * dx(v) - cv * (vs - vn) - 0.15 * (hs - hn) - turn * u
        wind_out[0, r] = new_u[:, 0:COLS]
        wind_out[1, r] = new_v[:, 0:COLS]
        t_out[r] = new_t[:, 0:COLS]
        h_out[r] = new_h[:, 0:COLS]
        return carry

    lax.fori_loop(0, BLOCK, one, 0, unroll=True)


@functools.lru_cache(maxsize=None)
def trig_table():
    row = np.arange(-1, NLAT + 1).astype(np.float32) + np.float32(0.5)
    angle = (row * np.float32(np.pi / NLAT)).astype(np.float64)
    cos = np.sin(angle).astype(np.float32)
    sin = -np.cos(angle).astype(np.float32)
    return np.stack([cos, (1.0 / cos.astype(np.float64)).astype(np.float32), sin])


def body(winds, theta, thick, polar_rows, cutoffs):
    lat = lax.axis_index("lat")
    served = jnp.where((lat >= 4) & (lat < 8), lat - 4, jnp.where((lat >= 8) & (lat < 12), lat + 4, lat))
    rows = served * ROWS + jnp.arange(ROWS, dtype=jnp.int32)
    hits = polar_rows[None, :] == rows[:, None]
    limit = jnp.max(jnp.where(hits, cutoffs[None, :], -1), axis=1).astype(F32)
    lim = jnp.broadcast_to(limit[:, None, None], (ROWS, SUB, 128))
    thi, tlo, uhi, ulo, wv = value_tables()
    fhi, flo, ghi, glo, wp = packed_tables()
    vm = pl.BlockSpec(memory_space=pltpu.VMEM)
    hbm = pl.BlockSpec(memory_space=pl.ANY)
    dma = pltpu.SemaphoreType.DMA
    state = pl.pallas_call(
        filter_kernel,
        out_shape=jax.ShapeDtypeStruct((4, ROWS + 2, LEV, PC), F32),
        in_specs=[hbm, hbm, hbm, vm, vm, vm] + [hbm] * 8,
        out_specs=hbm,
        scratch_shapes=[
            pltpu.VMEM((4, 2 * PC, PC), BF16), pltpu.VMEM((4, 2 * PC, PC), BF16),
            pltpu.VMEM((4, PC, 2 * PC), BF16), pltpu.VMEM((4, PC, 2 * PC), BF16),
            pltpu.VMEM((2, PC, PC), BF16), pltpu.VMEM((2, PC, PC), BF16),
            pltpu.VMEM((2, PC, PC), BF16), pltpu.VMEM((2, PC, PC), BF16),
            pltpu.VMEM((NP, ROWS, SUB, COLS), F32),
            pltpu.VMEM((NP, ROWS, SUB, PC), F32),
            pltpu.VMEM((NP, HALF, SUB, PC), F32),
            pltpu.VMEM((2, ROWS, SUB, COLS), F32),
            pltpu.VMEM((2, ROWS, SUB, PC), F32),
            pltpu.VMEM((2, NG, 2, SR, SUB, PC), F32),
            pltpu.VMEM((2, NG * SR * SUB, PC), F32),
            pltpu.VMEM((8, CR * SUB, PC), F32),
            pltpu.VMEM((8, CR * SUB, PC), F32),
            pltpu.VMEM((NP, SUB, PC), F32),
            pltpu.VMEM((2, NP, SUB, 128), F32),
            pltpu.VMEM((2, NP, SUB, 128), F32),
            pltpu.VMEM((4, LEV, PC), F32),
            pltpu.VMEM((max(OFF1, OFF2), 4, CR, LEV, COLS), F32),
            dma((4,)), dma((2,)),
            dma((NCH, NP)), dma((NCH, NP)), dma((NCH, NP)), dma((NCH, NP)),
            dma((NSUB, NP)), dma((NSUB, NP)), dma((NSUB, NP)), dma((NSUB, NP)),
            dma((2,)), dma((2,)), dma((2,)), dma((2,)), dma((2,)), dma,
            dma((NCH, 4)), dma((NCH, 4)), dma((NP,)), dma((2, NG, 2)),
        ],
        compiler_params=pltpu.CompilerParams(
            collective_id=1, has_side_effects=True, vmem_limit_bytes=60 * 2**20
        ),
        name="polar_filter",
    )(
        winds.transpose(0, 2, 1, 3), theta.transpose(1, 0, 2), thick.transpose(1, 0, 2), lim,
        jnp.asarray(wv)[:, None, :], jnp.asarray(wp), thi, tlo, uhi, ulo, fhi, flo, ghi, glo,
    )
    new_winds, new_t, new_h = pl.pallas_call(
        stencil_kernel,
        grid=(ROWS // BLOCK,),
        out_shape=(
            jax.ShapeDtypeStruct((2, ROWS, LEV, COLS), F32),
            jax.ShapeDtypeStruct((ROWS, LEV, COLS), F32),
            jax.ShapeDtypeStruct((ROWS, LEV, COLS), F32),
        ),
        in_specs=[
            pl.BlockSpec(memory_space=pltpu.SMEM),
            pl.BlockSpec(
                (pl.Element(4), pl.Element(BLOCK + 2), pl.Element(LEV), pl.Element(PC)),
                lambda i: (0, i * BLOCK, 0, 0),
            ),
        ],
        out_specs=(
            pl.BlockSpec((2, BLOCK, LEV, COLS), lambda i: (0, i, 0, 0)),
            pl.BlockSpec((BLOCK, LEV, COLS), lambda i: (i, 0, 0)),
            pl.BlockSpec((BLOCK, LEV, COLS), lambda i: (i, 0, 0)),
        ),
        compiler_params=pltpu.CompilerParams(vmem_limit_bytes=60 * 2**20),
        name="stencil",
    )(jnp.asarray(trig_table()), state)
    return new_winds.transpose(0, 2, 1, 3), new_t.transpose(1, 0, 2), new_h.transpose(1, 0, 2)


def solution(mesh):
    in_specs = (P(None, None, "lat", "lon"), P(None, "lat", "lon"), P(None, "lat", "lon"), P(), P())
    out_specs = (P(None, None, "lat", "lon"), P(None, "lat", "lon"), P(None, "lat", "lon"))
    return jax.shard_map(body, mesh=mesh, in_specs=in_specs, out_specs=out_specs, check_vma=False)
```

```python
import functools

import jax
import jax.numpy as jnp
import numpy as np
from jax import lax
from jax.experimental import pallas as pl
from jax.experimental.pallas import tpu as pltpu
from jax.sharding import PartitionSpec as P

NLON = 2880
NLAT = 1440
LEV = 16
ROWS = 90
COLS = 360
HALF = ROWS // 2
PC = 384
NP = 8
SUB = 8
NCH = 15
CR = ROWS // NCH
OFF1 = 10
OFF2 = 7
NSUB = 3
SR = HALF // NSUB
NG = 4
BLOCK = 18
MESH = pl.DeviceIdType.MESH
F32 = jnp.float32
BF16 = jnp.bfloat16


def split(table):
    hi = table.astype(np.float32).astype(BF16)
    lo = (table - hi.astype(np.float64)).astype(np.float32).astype(BF16)
    return np.asarray(hi), np.asarray(lo)


@functools.lru_cache(maxsize=None)
def value_tables():
    q = np.arange(PC)
    q = np.where(q == PC - 1, -1, q)
    forward = np.zeros((4, 2 * PC, PC))
    inverse = np.zeros((4, PC, 2 * PC))
    waves = np.full((4, PC), 1e9)
    m = np.arange(90)
    for g in range(4):
        parts = [(0, 0, 0), (4, 1, 0)] if g == 0 else [(g, 0, 1), (8 - g, 0, -1)]
        for slot, (r, half, sign) in enumerate(parts):
            k = 8 * m + r
            angle = 2.0 * np.pi * ((k[:, None] * q[None, :]) % NLON) / NLON
            cos, sin = np.cos(angle), np.sin(angle)
            re = slice(slot * 180, slot * 180 + 90)
            im = slice(slot * 180 + 90, slot * 180 + 180)
            waves[g, re] = k
            waves[g, im] = k
            weight = np.where(k == 0, 1.0, 2.0)[:, None] / NLON
            own = np.zeros((PC, 2 * PC))
            if sign == 0:
                own[re, half * PC : (half + 1) * PC] = cos
                own[im, half * PC : (half + 1) * PC] = -sin
            else:
                own[re, :PC] = cos
                own[im, :PC] = -sin
                own[re, PC:] = sign * sin
                own[im, PC:] = sign * cos
            scaled = own.copy()
            scaled[re] *= weight
            scaled[im] *= weight
            inverse[g] += scaled
            keep = np.concatenate([np.arange(PC) < COLS] * 2)
            forward[g] += (own * keep[None, :]).T
    used = np.concatenate([(np.arange(PC) <= COLS) | (np.arange(PC) == PC - 1)] * 2)
    inverse = inverse * used[None, None, :]
    return split(forward) + split(inverse) + (waves.astype(np.float32),)


@functools.lru_cache(maxsize=None)
def packed_tables():
    lane = np.arange(PC)
    wave = (lane + 1) // 2
    is_cos = (lane == 0) | (lane % 2 == 1)
    q = np.arange(PC)
    q = np.where(q == PC - 1, -1, q)
    used = (np.arange(PC) <= COLS) | (np.arange(PC) == PC - 1)
    forward = np.zeros((NP, 2, PC, PC))
    inverse = np.zeros((NP, 2, PC, PC))
    for p in range(NP):
        n = COLS * p + q
        angle = 2.0 * np.pi * ((wave[:, None] * n[None, :]) % NLON) / NLON
        base = np.where(is_cos[:, None], np.cos(angle), np.sin(angle))
        weight = np.where(wave == 0, 1.0, 2.0)[:, None] / NLON
        back = base * weight * used[None, :]
        ahead = (base * (np.arange(PC) < COLS)[None, :]).T
        forward[p, 0], forward[p, 1] = ahead, ahead[:, ::-1]
        inverse[p, 0], inverse[p, 1] = back, back[::-1]
    waves = np.stack([wave, wave[::-1]]).astype(np.float32)
    return split(forward) + split(inverse) + (waves,)


def dot3(x, hi, lo):
    x_hi = x.astype(BF16)
    x_lo = (x - x_hi.astype(F32)).astype(BF16)
    count = x.shape[0]
    both = jnp.dot(jnp.concatenate([x_lo, x_hi], axis=0), hi, preferred_element_type=F32)
    return jnp.dot(x_hi, lo, preferred_element_type=F32) + both[:count] + both[count:]


def wide(lim):
    return jnp.concatenate([lim, lim, lim], axis=-1)


def filter_kernel(
    w_ref, t_ref, h_ref, lim_ref, wv_ref, wp_ref,
    thi_ref, tlo_ref, uhi_ref, ulo_ref, fhi_ref, flo_ref, ghi_ref, glo_ref,
    state_ref,
    thi, tlo, uhi, ulo, fhi, flo, ghi, glo,
    recv, ret, srecv, stage, obuf, pbuf, xs, yb, zb, rawp, cols, side, zero, home,
    tab_sem, stage_sem, fsend, frecv, rsend, rrecv, ssend, srecv_sem, asend, arecv_sem,
    hsend, hrecv, lsend, lrecv, osem, zsem, xsend, xrecv, part_sem, psem,
):
    lat = lax.axis_index("lat")
    lon = lax.axis_index("lon")
    north = lat < 8
    depth = jnp.where(north, lat, 15 - lat)
    partner = jnp.where(north, jnp.where(lat < 4, lat + 4, lat - 4), jnp.where(lat >= 12, lat - 4, lat + 4))
    is_packed = depth == 0
    is_value = (depth >= 1) & (depth <= 3)
    is_off = (depth == 5) | (depth == 6)
    served = jnp.where(is_off, partner, lat)
    served_depth = jnp.where(is_off, depth - 4, depth)
    n_off = jnp.where(served_depth == 1, OFF1, jnp.where(served_depth == 2, OFF2, 0))
    begin = jnp.where(served == 12, 2 * NCH // 3, 0)
    end = jnp.where(served == 3, NCH // 3, NCH)
    first = jnp.where(is_off, 0, jnp.maximum(begin, n_off))
    last = jnp.where(is_off, n_off, end)
    sources = (w_ref.at[0], w_ref.at[1], t_ref, h_ref)

    bar = pltpu.get_barrier_semaphore()
    for i in range(1, NP):
        pl.semaphore_signal(bar, inc=1, device_id=(lat, lax.rem(lon + i, NP)), device_id_type=MESH)
    for i in (1, 15):
        pl.semaphore_signal(bar, inc=1, device_id=(lax.rem(lat + i, 16), lon), device_id_type=MESH)
    n_signals = 9
    if OFF1 or OFF2:
        for i in range(NP):
            pl.semaphore_signal(bar, inc=1, device_id=(partner, lax.rem(lon + i, NP)), device_id_type=MESH)
        n_signals += NP

    tables = ((thi_ref, thi), (tlo_ref, tlo), (uhi_ref, uhi), (ulo_ref, ulo))
    packs = ((fhi_ref, fhi), (flo_ref, flo), (ghi_ref, ghi), (glo_ref, glo))

    @pl.when(is_packed)
    def _():
        for i, (src, dst) in enumerate(packs):
            pltpu.make_async_copy(src.at[lon], dst, tab_sem.at[i]).start()

    @pl.when(is_value | is_off)
    def _():
        for i, (src, dst) in enumerate(tables):
            pltpu.make_async_copy(src, dst, tab_sem.at[i]).start()
        yb[...] = jnp.zeros_like(yb)

    def part(g, rows):
        return sources[g // 2].at[rows, 8 * (g % 2) : 8 * (g % 2) + 8]

    def whole_part(g):
        return pltpu.make_async_copy(part(g, slice(0, ROWS)), recv.at[g], part_sem.at[g])

    @pl.when(is_packed)
    def _():
        for g in range(NP):
            whole_part(g).start()

    def stage_copy(g, slot):
        return pltpu.make_async_copy(part(g, slice(0, ROWS)), stage.at[slot], stage_sem.at[slot])

    def state_part(p, start, count):
        return state_ref.at[p // 2, pl.ds(start, count), pl.ds(pl.multiple_of(lax.rem(p, 2) * 8, 8), 8)]

    @pl.when(depth >= 3)
    def _():
        stage_copy(0, 0).start()

    pl.semaphore_wait(bar, n_signals)

    def relay(c, k):
        return pltpu.make_async_remote_copy(
            src_ref=sources[k].at[pl.ds(c * CR, CR)], dst_ref=home.at[c, k],
            send_sem=xsend.at[c, k], recv_sem=xrecv.at[c, k],
            device_id=(partner, lon), device_id_type=MESH,
        )

    def relay_all(c, act):
        for k in range(4):
            act(relay(c, k))

    def stay(c):
        def per_owner(i, carry):
            p = lax.rem(lon + i, NP)
            dst = recv.at[lon, pl.ds(c * CR, CR)]
            half = pl.ds(pl.multiple_of(lax.rem(p, 2) * 8, 8), 8)
            for k in range(4):
                src = sources[k].at[pl.ds(c * CR, CR), half]

                @pl.when((p // 2 == k) & (p != lon))
                def _(src=src):
                    pltpu.make_async_remote_copy(
                        src_ref=src, dst_ref=dst, send_sem=fsend.at[c, p],
                        recv_sem=frecv.at[c, lon], device_id=(lat, p), device_id_type=MESH,
                    ).start()

                @pl.when((p // 2 == k) & (p == lon))
                def _(src=src):
                    pltpu.make_async_copy(src, dst, frecv.at[c, lon]).start()

            return carry

        lax.fori_loop(0, NP, per_owner, 0)

    def edge_copy(i):
        row, there, step = ((1, ROWS + 1, 15), (ROWS, 0, 1))[i]
        return pltpu.make_async_remote_copy(
            src_ref=state_ref.at[:, row], dst_ref=state_ref.at[:, there],
            send_sem=lsend.at[i], recv_sem=lrecv.at[i],
            device_id=(lax.rem(lat + step, 16), lon), device_id_type=MESH,
        )

    inner = (lat > 0, lat < 15)

    def edges_out():
        for i in range(2):
            @pl.when(inner[i])
            def _(i=i):
                edge_copy(i).start()

    def strip_copy(p, sub):
        rows = pl.ds(sub * SR, SR)
        return pltpu.make_async_remote_copy(
            src_ref=ret.at[p, rows], dst_ref=srecv.at[lon, rows], send_sem=ssend.at[sub, p],
            recv_sem=srecv_sem.at[sub, lon], device_id=(lat, p), device_id_type=MESH,
        )

    @pl.when(is_packed)
    def _():
        xs[...] = jnp.zeros_like(xs)
        for i, (src, dst) in enumerate(packs):
            pltpu.make_async_copy(src.at[lon], dst, tab_sem.at[i]).wait()
        for g in range(NP):
            whole_part(g).wait()

        def keep(sub):
            near = wp_ref[0:1, :] <= wide(lim_ref[pl.ds(sub * SR, SR)])
            far = wp_ref[1:2, :] <= wide(lim_ref[pl.ds(ROWS - SR - sub * SR, SR)])
            return near[None], far[None]

        def ahead(n, carry):
            sub = n // (NP // NG)
            base = lon + 1 + lax.rem(n, NP // NG) * NG
            for i in range(NG):
                g = lax.rem(base + i, NP)
                near = recv[g, pl.ds(sub * SR, SR)].reshape(SR * SUB, COLS)
                far = recv[g, pl.ds(ROWS - SR - sub * SR, SR)].reshape(SR * SUB, COLS)
                xs[0, i * SR * SUB : (i + 1) * SR * SUB, 0:COLS] = near
                xs[1, i * SR * SUB : (i + 1) * SR * SUB, 0:COLS] = far
            keep_near, keep_far = keep(sub)
            shape = (NG, SR, SUB, PC)
            pbuf[0, :, 0] = jnp.where(keep_near, dot3(xs[0], fhi[0], flo[0]).reshape(shape), 0.0)
            pbuf[0, :, 1] = jnp.where(keep_far, dot3(xs[1], fhi[1], flo[1]).reshape(shape), 0.0)
            for i in range(NG):
                g = lax.rem(base + i, NP)
                for j in range(SR):
                    ret[g, sub * SR + j] = pbuf[0, i, 0, j] + pbuf[0, i, 1, SR - 1 - j]

                @pl.when(lon != g)
                def _(g=g):
                    strip_copy(g, sub).start()

                @pl.when(lon == g)
                def _(g=g):
                    rows = pl.ds(sub * SR, SR)
                    pltpu.make_async_copy(ret.at[g, rows], srecv.at[g, rows], srecv_sem.at[sub, g]).start()

            return carry

        lax.fori_loop(0, NSUB * (NP // NG), ahead, 0)

        def sum_rows(p, sub):
            return ret.at[p, pl.ds(HALF + sub * SR, SR)]

        def sum_to(p, sub):
            return pltpu.make_async_remote_copy(
                src_ref=sum_rows(lon, sub), dst_ref=sum_rows(lon, sub), send_sem=asend.at[sub, p],
                recv_sem=arecv_sem.at[sub, lon], device_id=(lat, p), device_id_type=MESH,
            )

        def add_up(sub, carry):
            def wait_part(p, carry):
                ref = srecv.at[p, pl.ds(sub * SR, SR)]
                pltpu.make_async_copy(ref, ref, srecv_sem.at[sub, p]).wait()
                return carry

            lax.fori_loop(0, NP, wait_part, 0)

            def add(j, carry):
                total = srecv[0, sub * SR + j]
                for p in range(1, NP):
                    total = total + srecv[p, sub * SR + j]
                ret[lon, HALF + sub * SR + j] = total
                return carry

            lax.fori_loop(0, SR, add, 0, unroll=5)

            def send(i, carry):
                sum_to(lax.rem(lon + i, NP), sub).start()
                return carry

            lax.fori_loop(1, NP, send, 0)
            return carry

        lax.fori_loop(0, NSUB, add_up, 0)

        def out_copies(n, act):
            slot = lax.rem(n, 2)
            sub = n // (NP // NG)
            base = lon + lax.rem(n, NP // NG) * NG
            for i in range(NG):
                g = lax.rem(base + i, NP)
                for far in range(2):
                    start = ROWS - SR - sub * SR if far else sub * SR
                    act(pltpu.make_async_copy(
                        pbuf.at[slot, i, far], state_part(g, 1 + start, SR), psem.at[slot, i, far]
                    ))

        def back(n, carry):
            slot = lax.rem(n, 2)
            sub = n // (NP // NG)
            base = lon + lax.rem(n, NP // NG) * NG
            for i in range(NG):
                g = lax.rem(base + i, NP)

                @pl.when(g != lon)
                def _(g=g):
                    pltpu.make_async_copy(sum_rows(g, sub), sum_rows(g, sub), arecv_sem.at[sub, g]).wait()

                for j in range(SR):
                    spec = ret[g, HALF + sub * SR + j]
                    xs[0, (i * SR + j) * SUB : (i * SR + j + 1) * SUB, :] = spec
                    xs[1, (i * SR + SR - 1 - j) * SUB : (i * SR + SR - j) * SUB, :] = spec

            @pl.when(n >= 2)
            def _():
                out_copies(n - 2, lambda copy: copy.wait())

            @pl.when(n == 4)
            def _():
                edges_out()

            shape = (NG, SR, SUB, PC)
            for far, keep_it in enumerate(keep(sub)):
                spec = jnp.where(keep_it, xs[far].reshape(shape), 0.0).reshape(NG * SR * SUB, PC)
                pbuf[slot, :, far] = dot3(spec, ghi[far], glo[far]).reshape(shape)
            out_copies(n, lambda copy: copy.start())
            return carry

        steps = NSUB * (NP // NG)
        lax.fori_loop(0, steps, back, 0)
        for n in (steps - 2, steps - 1):
            out_copies(n, lambda copy: copy.wait())

        def sent(n, carry):
            sub = n // (NP - 1)
            p = lax.rem(lon + 1 + lax.rem(n, NP - 1), NP)
            sum_to(p, sub).wait_send()
            strip_copy(p, sub).wait_send()
            return carry

        lax.fori_loop(0, NSUB * (NP - 1), sent, 0)

    def side_copy(i):
        step = NP - 1 if i == 0 else 1
        return pltpu.make_async_remote_copy(
            src_ref=cols.at[i], dst_ref=side.at[i], send_sem=hsend.at[i], recv_sem=hrecv.at[i],
            device_id=(lat, lax.rem(lon + step, NP)), device_id_type=MESH,
        )

    own_start = jnp.where(lat == 3, ROWS // 3, 0)

    def raw_copy(g, slot, act):
        full = pltpu.make_async_copy(obuf.at[slot], state_part(g, 1, ROWS), osem.at[slot])
        some = pltpu.make_async_copy(
            obuf.at[slot, pl.ds(own_start, 2 * ROWS // 3)],
            state_part(g, 1 + own_start, 2 * ROWS // 3), osem.at[slot],
        )

        @pl.when(depth > 3)
        def _():
            act(full)

        @pl.when(depth == 3)
        def _():
            act(some)

    def raw_out(g, carry):
        slot = lax.rem(g, 2)
        half = pl.ds(pl.multiple_of(slot * 8, 8), 8)
        for k in range(4):
            @pl.when(g // 2 == k)
            def _(k=k):
                pltpu.make_async_copy(sources[k].at[:, half], stage.at[slot], stage_sem.at[slot]).start()

        @pl.when(g >= 2)
        def _():
            raw_copy(g - 2, slot, lambda copy: copy.wait())

        pltpu.make_async_copy(stage.at[slot], stage.at[slot], stage_sem.at[slot]).wait()
        lane = lax.broadcasted_iota(jnp.int32, (SUB, 128), 1)

        def insert(j, carry):
            obuf[slot, j, :, 0:COLS] = stage[slot, j]
            east = pltpu.roll(side[0, g], lax.rem(COLS - 256 + 128 - j, 128), 1)
            west = pltpu.roll(side[1, g], 127 - j, 1)
            tail = obuf[slot, j, :, 256:PC]
            tail = jnp.where(lane == COLS - 256, east, tail)
            obuf[slot, j, :, 256:PC] = jnp.where(lane == 127, west, tail)
            return carry

        lax.fori_loop(0, ROWS, insert, 0, unroll=9)
        raw_copy(g, slot, lambda copy: copy.start())
        return carry

    @pl.when(depth >= 3)
    def _():
        lane = lax.broadcasted_iota(jnp.int32, (SUB, 128), 1)
        for g in range(NP):
            slot = g % 2
            if g + 1 < NP:
                stage_copy(g + 1, 1 - slot).start()
            stage_copy(g, slot).wait()

            def gather(j, carry, slot=slot):
                head, tail = carry
                head = jnp.where(lane == j, stage[slot, j, :, 0:1], head)
                tail = jnp.where(lane == j, stage[slot, j, :, COLS - 1 : COLS], tail)
                return head, tail

            zeros = jnp.zeros((SUB, 128), F32)
            head, tail = lax.fori_loop(0, ROWS, gather, (zeros, zeros), unroll=18)
            cols[0, g] = head
            cols[1, g] = tail

        for i in range(2):
            side_copy(i).start()

        @pl.when(jnp.logical_not(is_off))
        def _():
            for i in range(2):
                side_copy(i).wait()
            lax.fori_loop(0, NP, raw_out, 0)

    @pl.when(is_value | is_off)
    def _():
        half = np.float32(np.sqrt(0.5))

        def chunk(c, carry):
            def arrived(s, carry):
                ref = recv.at[s, pl.ds(c * CR, CR)]
                pltpu.make_async_copy(ref, ref, frecv.at[c, s]).wait()
                return carry

            lax.fori_loop(0, NP, arrived, 0)

            def fold(r, carry):
                rows = pl.ds(pl.multiple_of(r * SUB, SUB), SUB)
                x = [recv[s, c * CR + r] for s in range(NP)]
                s0, s1, s2, s3 = [x[j] + x[j + 4] for j in range(4)]
                d0, d1, d2, d3 = [x[j] - x[j + 4] for j in range(4)]
                plus, minus = half * (d1 + d3), half * (d1 - d3)
                out = (
                    (s0 + s2) + (s1 + s3), (s0 + s2) - (s1 + s3),
                    d0 + minus, -(d2 + plus),
                    s0 - s2, s3 - s1,
                    d0 - minus, d2 - plus,
                )
                for i in range(8):
                    yb[i, rows, 0:COLS] = out[i]
                return carry

            lax.fori_loop(0, CR, fold, 0, unroll=3)
            limit = wide(lim_ref[pl.ds(c * CR, CR)])

            def group(g, carry):
                spec = dot3(yb[2 * g], thi[g, 0:PC, :], tlo[g, 0:PC, :])
                spec += dot3(yb[2 * g + 1], thi[g, PC:, :], tlo[g, PC:, :])
                spec = jnp.where(wv_ref[g] <= limit, spec.reshape(CR, SUB, PC), 0.0).reshape(CR * SUB, PC)
                zb[2 * g] = dot3(spec, uhi[g, :, 0:PC], ulo[g, :, 0:PC])
                zb[2 * g + 1] = dot3(spec, uhi[g, :, PC:], ulo[g, :, PC:])
                return carry

            lax.fori_loop(0, 4, group, 0)

            def unfold(r, carry):
                rows = pl.ds(pl.multiple_of(r * SUB, SUB), SUB)
                a0, b0, a1, b1, a2, b2, a3, b3 = [zb[i, rows, :] for i in range(8)]
                even = (a0 + b0 + a2, a0 - b0 - b2, a0 + b0 - a2, a0 - b0 + b2)
                odd = (a1 + a3, half * ((a1 - a3) - (b1 + b3)), b3 - b1, half * ((a3 - a1) - (b1 + b3)))
                for j in range(4):
                    ret[j, c * CR + r] = even[j] + odd[j]
                    ret[j + 4, c * CR + r] = even[j] - odd[j]
                return carry

            lax.fori_loop(0, CR, unfold, 0, unroll=3)

            @pl.when(served_depth >= 2)
            def _():
                lane = lax.broadcasted_iota(jnp.int32, (SUB, 128), 1)

                def select(r, carry):
                    listed = wide(lim_ref[c * CR + r]) >= 0.0
                    for p in range(NP):
                        rawp[p, :, 0:COLS] = recv[p, c * CR + r]
                    for p in range(NP):
                        east = recv[(p + 1) % NP, c * CR + r, :, 0:1]
                        west = recv[(p + 7) % NP, c * CR + r, :, COLS - 1 : COLS]
                        tail = jnp.where(lane == COLS - 256, east, rawp[p, :, 256:PC])
                        tail = jnp.where(lane == 127, west, tail)
                        raw = jnp.concatenate([rawp[p, :, 0:256], tail], axis=-1)
                        ret[p, c * CR + r] = jnp.where(listed, ret[p, c * CR + r], raw)
                    return carry

                lax.fori_loop(0, CR, select, 0, unroll=2)

            def give_back(i, carry):
                p = lax.rem(lon + i, NP)
                src = ret.at[p, pl.ds(c * CR, CR)]
                dst = state_part(lon, 1 + c * CR, CR)
                local = is_value & (p == lon)

                @pl.when(jnp.logical_not(local))
                def _():
                    pltpu.make_async_remote_copy(
                        src_ref=src, dst_ref=dst, send_sem=rsend.at[c, p],
                        recv_sem=rrecv.at[c, lon], device_id=(served, p), device_id_type=MESH,
                    ).start()

                @pl.when(local)
                def _():
                    pltpu.make_async_copy(src, dst, rrecv.at[c, lon]).start()

                return carry

            lax.fori_loop(0, NP, give_back, 0)
            return carry

        def pass_on(c):
            relay_all(c, lambda copy: copy.wait_recv())
            dst = recv.at[lon, pl.ds(c * CR, CR)]

            def home_part(p):
                return home.at[c, p // 2, :, pl.ds(pl.multiple_of(lax.rem(p, 2) * 8, 8), 8)]

            def to_owner(i, carry):
                p = lax.rem(lon + i, NP)
                pltpu.make_async_remote_copy(
                    src_ref=home_part(p), dst_ref=dst, send_sem=fsend.at[c, p],
                    recv_sem=frecv.at[c, lon], device_id=(lat, p), device_id_type=MESH,
                ).start()
                return carry

            lax.fori_loop(1, NP, to_owner, 0)
            pltpu.make_async_copy(home_part(lon), dst, frecv.at[c, lon]).start()

        n_loc = last - first

        def step(n, carry):
            @pl.when(is_value & (n < n_off))
            def _():
                @pl.when(n >= 2)
                def _():
                    relay_all(n - 2, lambda copy: copy.wait_send())

                relay_all(n, lambda copy: copy.start())

            @pl.when(is_value & (n < n_loc))
            def _():
                stay(first + n)

            @pl.when(is_off & (n < n_off))
            def _():
                pass_on(n)

            @pl.when(n == 1)
            def _():
                for i, (src, dst) in enumerate(tables):
                    pltpu.make_async_copy(src, dst, tab_sem.at[i]).wait()

            lag = jnp.where(is_off, 1, 2)

            @pl.when((n >= lag) & (n < n_loc + lag))
            def _():
                chunk(first + n - lag, 0)

            @pl.when(is_off & (n >= 1))
            def _():
                @pl.when(n == 1)
                def _():
                    for i in range(2):
                        side_copy(i).wait()

                lax.fori_loop(jnp.minimum(n - 1, NP), jnp.where(n == n_off, NP, jnp.minimum(n, NP)), raw_out, 0)

            return carry

        lax.fori_loop(0, jnp.where(is_off, n_off + 1, jnp.maximum(n_off, n_loc + 2)), step, 0)

        def returned(n, carry):
            c = first + n // NP
            p = lax.rem(n, NP)

            @pl.when(is_off | (p != lon))
            def _():
                ref = ret.at[p, pl.ds(c * CR, CR)]
                pltpu.make_async_copy(ref, ref, rsend.at[c, p]).wait()

            @pl.when(p != lon)
            def _():
                ref = recv.at[p, pl.ds(c * CR, CR)]
                pltpu.make_async_copy(ref, ref, fsend.at[c, p]).wait()

            return carry

        lax.fori_loop(0, (last - first) * NP, returned, 0)

    @pl.when(depth >= 3)
    def _():
        for slot in range(2):
            raw_copy(slot, slot, lambda copy: copy.wait())

    @pl.when(is_value)
    def _():
        def drain(m, carry):
            c = jnp.where(m == 0, begin, jnp.where(m == 1, end - 1, begin + m - 1))

            def one(p, carry):
                dst = state_part(p, 1 + c * CR, CR)
                pltpu.make_async_copy(dst, dst, rrecv.at[c, p]).wait()
                return carry

            lax.fori_loop(0, NP, one, 0)

            @pl.when(m == 1)
            def _():
                edges_out()

            return carry

        lax.fori_loop(0, end - begin, drain, 0)

        def relayed(c, carry):
            relay_all(c, lambda copy: copy.wait_send())
            return carry

        lax.fori_loop(jnp.maximum(n_off - 2, 0), n_off, relayed, 0)

    def blank(row):
        return pltpu.make_async_copy(zero, state_ref.at[:, row], zsem)

    @pl.when(depth >= 4)
    def _():
        edges_out()

    for i, row in ((0, 0), (1, ROWS + 1)):
        @pl.when(jnp.logical_not(inner[i]))
        def _(row=row):
            zero[...] = jnp.zeros_like(zero)
            blank(row).start()
            blank(row).wait()

    for i in range(2):
        @pl.when(inner[i])
        def _(i=i):
            edge_copy(i).wait_send()

        @pl.when(inner[1 - i])
        def _(i=i):
            edge_copy(i).wait_recv()


def stencil_kernel(trig_ref, state_ref, wind_out, t_out, h_out):
    base = lax.axis_index("lat") * ROWS + pl.program_id(0) * BLOCK

    def dx(a):
        return pltpu.roll(a, PC - 1, 1) - pltpu.roll(a, 1, 1)

    def one(r, carry):
        at = base + r
        cos_n, cos_s = trig_ref[0, at], trig_ref[0, at + 2]
        inv = trig_ref[1, at + 1]
        turn = 0.3 * trig_ref[2, at + 1]
        u, v, t, h = [state_ref[k, r + 1] for k in range(4)]
        un, vn, tn, hn = [state_ref[k, r] for k in range(4)]
        us, vs, ts, hs = [state_ref[k, r + 2] for k in range(4)]
        cu = (0.025 * inv) * u
        cv = 0.1 * v
        new_h = h - (0.025 * inv) * dx(u * h) - (0.1 * inv) * (vs * hs * cos_s - vn * hn * cos_n)
        new_t = t - cu * dx(t) - cv * (ts - tn)
        new_u = u - cu * dx(u) - cv * (us - un) - (0.05 * inv) * dx(h) + turn * v
        new_v = v - cu * dx(v) - cv * (vs - vn) - 0.15 * (hs - hn) - turn * u
        wind_out[0, r] = new_u[:, 0:COLS]
        wind_out[1, r] = new_v[:, 0:COLS]
        t_out[r] = new_t[:, 0:COLS]
        h_out[r] = new_h[:, 0:COLS]
        return carry

    lax.fori_loop(0, BLOCK, one, 0, unroll=True)


@functools.lru_cache(maxsize=None)
def trig_table():
    row = np.arange(-1, NLAT + 1).astype(np.float32) + np.float32(0.5)
    angle = (row * np.float32(np.pi / NLAT)).astype(np.float64)
    cos = np.sin(angle).astype(np.float32)
    sin = -np.cos(angle).astype(np.float32)
    return np.stack([cos, (1.0 / cos.astype(np.float64)).astype(np.float32), sin])


def body(winds, theta, thick, polar_rows, cutoffs):
    lat = lax.axis_index("lat")
    served = jnp.where((lat >= 4) & (lat < 8), lat - 4, jnp.where((lat >= 8) & (lat < 12), lat + 4, lat))
    rows = served * ROWS + jnp.arange(ROWS, dtype=jnp.int32)
    hits = polar_rows[None, :] == rows[:, None]
    limit = jnp.max(jnp.where(hits, cutoffs[None, :], -1), axis=1).astype(F32)
    lim = jnp.broadcast_to(limit[:, None, None], (ROWS, SUB, 128))
    thi, tlo, uhi, ulo, wv = value_tables()
    fhi, flo, ghi, glo, wp = packed_tables()
    vm = pl.BlockSpec(memory_space=pltpu.VMEM)
    hbm = pl.BlockSpec(memory_space=pl.ANY)
    dma = pltpu.SemaphoreType.DMA
    state = pl.pallas_call(
        filter_kernel,
        out_shape=jax.ShapeDtypeStruct((4, ROWS + 2, LEV, PC), F32),
        in_specs=[hbm, hbm, hbm, vm, vm, vm] + [hbm] * 8,
        out_specs=hbm,
        scratch_shapes=[
            pltpu.VMEM((4, 2 * PC, PC), BF16), pltpu.VMEM((4, 2 * PC, PC), BF16),
            pltpu.VMEM((4, PC, 2 * PC), BF16), pltpu.VMEM((4, PC, 2 * PC), BF16),
            pltpu.VMEM((2, PC, PC), BF16), pltpu.VMEM((2, PC, PC), BF16),
            pltpu.VMEM((2, PC, PC), BF16), pltpu.VMEM((2, PC, PC), BF16),
            pltpu.VMEM((NP, ROWS, SUB, COLS), F32),
            pltpu.VMEM((NP, ROWS, SUB, PC), F32),
            pltpu.VMEM((NP, HALF, SUB, PC), F32),
            pltpu.VMEM((2, ROWS, SUB, COLS), F32),
            pltpu.VMEM((2, ROWS, SUB, PC), F32),
            pltpu.VMEM((2, NG, 2, SR, SUB, PC), F32),
            pltpu.VMEM((2, NG * SR * SUB, PC), F32),
            pltpu.VMEM((8, CR * SUB, PC), F32),
            pltpu.VMEM((8, CR * SUB, PC), F32),
            pltpu.VMEM((NP, SUB, PC), F32),
            pltpu.VMEM((2, NP, SUB, 128), F32),
            pltpu.VMEM((2, NP, SUB, 128), F32),
            pltpu.VMEM((4, LEV, PC), F32),
            pltpu.VMEM((max(OFF1, OFF2), 4, CR, LEV, COLS), F32),
            dma((4,)), dma((2,)),
            dma((NCH, NP)), dma((NCH, NP)), dma((NCH, NP)), dma((NCH, NP)),
            dma((NSUB, NP)), dma((NSUB, NP)), dma((NSUB, NP)), dma((NSUB, NP)),
            dma((2,)), dma((2,)), dma((2,)), dma((2,)), dma((2,)), dma,
            dma((NCH, 4)), dma((NCH, 4)), dma((NP,)), dma((2, NG, 2)),
        ],
        compiler_params=pltpu.CompilerParams(
            collective_id=1, has_side_effects=True, vmem_limit_bytes=60 * 2**20
        ),
        name="polar_filter",
    )(
        winds.transpose(0, 2, 1, 3), theta.transpose(1, 0, 2), thick.transpose(1, 0, 2), lim,
        jnp.asarray(wv)[:, None, :], jnp.asarray(wp), thi, tlo, uhi, ulo, fhi, flo, ghi, glo,
    )
    new_winds, new_t, new_h = pl.pallas_call(
        stencil_kernel,
        grid=(ROWS // BLOCK,),
        out_shape=(
            jax.ShapeDtypeStruct((2, ROWS, LEV, COLS), F32),
            jax.ShapeDtypeStruct((ROWS, LEV, COLS), F32),
            jax.ShapeDtypeStruct((ROWS, LEV, COLS), F32),
        ),
        in_specs=[
            pl.BlockSpec(memory_space=pltpu.SMEM),
            pl.BlockSpec(
                (pl.Element(4), pl.Element(BLOCK + 2), pl.Element(LEV), pl.Element(PC)),
                lambda i: (0, i * BLOCK, 0, 0),
            ),
        ],
        out_specs=(
            pl.BlockSpec((2, BLOCK, LEV, COLS), lambda i: (0, i, 0, 0)),
            pl.BlockSpec((BLOCK, LEV, COLS), lambda i: (i, 0, 0)),
            pl.BlockSpec((BLOCK, LEV, COLS), lambda i: (i, 0, 0)),
        ),
        compiler_params=pltpu.CompilerParams(vmem_limit_bytes=60 * 2**20),
        name="stencil",
    )(jnp.asarray(trig_table()), state)
    return new_winds.transpose(0, 2, 1, 3), new_t.transpose(1, 0, 2), new_h.transpose(1, 0, 2)


def solution(mesh):
    in_specs = (P(None, None, "lat", "lon"), P(None, "lat", "lon"), P(None, "lat", "lon"), P(), P())
    out_specs = (P(None, None, "lat", "lon"), P(None, "lat", "lon"), P(None, "lat", "lon"))
    return jax.shard_map(body, mesh=mesh, in_specs=in_specs, out_specs=out_specs, check_vma=False)
```

```python
import functools

import jax
import jax.numpy as jnp
import numpy as np
from jax import lax
from jax.experimental import pallas as pl
from jax.experimental.pallas import tpu as pltpu
from jax.sharding import PartitionSpec as P

NLON = 2880
NLAT = 1440
LEV = 16
ROWS = 90
COLS = 360
HALF = ROWS // 2
PC = 384
NP = 8
SUB = 8
NCH = 15
CR = ROWS // NCH
OFF1 = 10
OFF2 = 7
NSUB = 3
SR = HALF // NSUB
NG = 4
BLOCK = 18
MESH = pl.DeviceIdType.MESH
F32 = jnp.float32
BF16 = jnp.bfloat16


def split(table):
    hi = table.astype(np.float32).astype(BF16)
    lo = (table - hi.astype(np.float64)).astype(np.float32).astype(BF16)
    return np.asarray(hi), np.asarray(lo)


@functools.lru_cache(maxsize=None)
def value_tables():
    q = np.arange(PC)
    q = np.where(q == PC - 1, -1, q)
    forward = np.zeros((4, 2 * PC, PC))
    inverse = np.zeros((4, PC, 2 * PC))
    waves = np.full((4, PC), 1e9)
    m = np.arange(90)
    for g in range(4):
        parts = [(0, 0, 0), (4, 1, 0)] if g == 0 else [(g, 0, 1), (8 - g, 0, -1)]
        for slot, (r, half, sign) in enumerate(parts):
            k = 8 * m + r
            angle = 2.0 * np.pi * ((k[:, None] * q[None, :]) % NLON) / NLON
            cos, sin = np.cos(angle), np.sin(angle)
            re = slice(slot * 180, slot * 180 + 90)
            im = slice(slot * 180 + 90, slot * 180 + 180)
            waves[g, re] = k
            waves[g, im] = k
            weight = np.where(k == 0, 1.0, 2.0)[:, None] / NLON
            own = np.zeros((PC, 2 * PC))
            if sign == 0:
                own[re, half * PC : (half + 1) * PC] = cos
                own[im, half * PC : (half + 1) * PC] = -sin
            else:
                own[re, :PC] = cos
                own[im, :PC] = -sin
                own[re, PC:] = sign * sin
                own[im, PC:] = sign * cos
            scaled = own.copy()
            scaled[re] *= weight
            scaled[im] *= weight
            inverse[g] += scaled
            keep = np.concatenate([np.arange(PC) < COLS] * 2)
            forward[g] += (own * keep[None, :]).T
    used = np.concatenate([(np.arange(PC) <= COLS) | (np.arange(PC) == PC - 1)] * 2)
    inverse = inverse * used[None, None, :]
    return split(forward) + split(inverse) + (waves.astype(np.float32),)


@functools.lru_cache(maxsize=None)
def packed_tables():
    lane = np.arange(PC)
    wave = (lane + 1) // 2
    is_cos = (lane == 0) | (lane % 2 == 1)
    q = np.arange(PC)
    q = np.where(q == PC - 1, -1, q)
    used = (np.arange(PC) <= COLS) | (np.arange(PC) == PC - 1)
    forward = np.zeros((NP, 2, PC, PC))
    inverse = np.zeros((NP, 2, PC, PC))
    for p in range(NP):
        n = COLS * p + q
        angle = 2.0 * np.pi * ((wave[:, None] * n[None, :]) % NLON) / NLON
        base = np.where(is_cos[:, None], np.cos(angle), np.sin(angle))
        weight = np.where(wave == 0, 1.0, 2.0)[:, None] / NLON
        back = base * weight * used[None, :]
        ahead = (base * (np.arange(PC) < COLS)[None, :]).T
        forward[p, 0], forward[p, 1] = ahead, ahead[:, ::-1]
        inverse[p, 0], inverse[p, 1] = back, back[::-1]
    waves = np.stack([wave, wave[::-1]]).astype(np.float32)
    return split(forward) + split(inverse) + (waves,)


def dot3(x, hi, lo):
    x_hi = x.astype(BF16)
    x_lo = (x - x_hi.astype(F32)).astype(BF16)
    count = x.shape[0]
    both = jnp.dot(jnp.concatenate([x_lo, x_hi], axis=0), hi, preferred_element_type=F32)
    return jnp.dot(x_hi, lo, preferred_element_type=F32) + both[:count] + both[count:]


def wide(lim):
    return jnp.concatenate([lim, lim, lim], axis=-1)


def filter_kernel(
    w_ref, t_ref, h_ref, cut_ref, wv_ref, wp_ref,
    thi_ref, tlo_ref, uhi_ref, ulo_ref, fhi_ref, flo_ref, ghi_ref, glo_ref,
    state_ref,
    lim_ref, thi, tlo, uhi, ulo, fhi, flo, ghi, glo,
    recv, ret, srecv, stage, obuf, pbuf, xs, yb, zb, rawp, cols, side, zero, home,
    tab_sem, stage_sem, fsend, frecv, rsend, rrecv, ssend, srecv_sem, asend, arecv_sem,
    hsend, hrecv, lsend, lrecv, osem, zsem, xsend, xrecv, part_sem, psem,
):
    lat = lax.axis_index("lat")
    lon = lax.axis_index("lon")
    north = lat < 8
    depth = jnp.where(north, lat, 15 - lat)
    partner = jnp.where(north, jnp.where(lat < 4, lat + 4, lat - 4), jnp.where(lat >= 12, lat - 4, lat + 4))
    is_packed = depth == 0
    is_value = (depth >= 1) & (depth <= 3)
    is_off = (depth == 5) | (depth == 6)
    served = jnp.where(is_off, partner, lat)
    served_depth = jnp.where(is_off, depth - 4, depth)
    n_off = jnp.where(served_depth == 1, OFF1, jnp.where(served_depth == 2, OFF2, 0))
    begin = jnp.where(served == 12, 2 * NCH // 3, 0)
    end = jnp.where(served == 3, NCH // 3, NCH)
    first = jnp.where(is_off, 0, jnp.maximum(begin, n_off))
    last = jnp.where(is_off, n_off, end)
    sources = (w_ref.at[0], w_ref.at[1], t_ref, h_ref)

    bar = pltpu.get_barrier_semaphore()
    for i in range(1, NP):
        pl.semaphore_signal(bar, inc=1, device_id=(lat, lax.rem(lon + i, NP)), device_id_type=MESH)
    for i in (1, 15):
        pl.semaphore_signal(bar, inc=1, device_id=(lax.rem(lat + i, 16), lon), device_id_type=MESH)
    n_signals = 9
    if OFF1 or OFF2:
        for i in range(NP):
            pl.semaphore_signal(bar, inc=1, device_id=(partner, lax.rem(lon + i, NP)), device_id_type=MESH)
        n_signals += NP

    tables = ((thi_ref, thi), (tlo_ref, tlo), (uhi_ref, uhi), (ulo_ref, ulo))
    packs = ((fhi_ref, fhi), (flo_ref, flo), (ghi_ref, ghi), (glo_ref, glo))

    @pl.when(is_packed)
    def _():
        for i, (src, dst) in enumerate(packs):
            pltpu.make_async_copy(src.at[lon], dst, tab_sem.at[i]).start()

    @pl.when(is_value | is_off)
    def _():
        for i, (src, dst) in enumerate(tables):
            pltpu.make_async_copy(src, dst, tab_sem.at[i]).start()
        yb[...] = jnp.zeros_like(yb)

    def part(g, rows):
        return sources[g // 2].at[rows, 8 * (g % 2) : 8 * (g % 2) + 8]

    def whole_part(g):
        return pltpu.make_async_copy(part(g, slice(0, ROWS)), recv.at[g], part_sem.at[g])

    @pl.when(is_packed)
    def _():
        for g in range(NP):
            whole_part(g).start()

    def stage_copy(g, slot):
        return pltpu.make_async_copy(part(g, slice(0, ROWS)), stage.at[slot], stage_sem.at[slot])

    def state_part(p, start, count):
        return state_ref.at[p // 2, pl.ds(start, count), pl.ds(pl.multiple_of(lax.rem(p, 2) * 8, 8), 8)]

    @pl.when(depth >= 3)
    def _():
        stage_copy(0, 0).start()

    def spread(j, carry):
        lim_ref[j] = jnp.full((SUB, 128), cut_ref[j], F32)
        return carry

    lax.fori_loop(0, ROWS, spread, 0, unroll=6)
    pl.semaphore_wait(bar, n_signals)

    def relay(c, k):
        return pltpu.make_async_remote_copy(
            src_ref=sources[k].at[pl.ds(c * CR, CR)], dst_ref=home.at[c, k],
            send_sem=xsend.at[c, k], recv_sem=xrecv.at[c, k],
            device_id=(partner, lon), device_id_type=MESH,
        )

    def relay_all(c, act):
        for k in range(4):
            act(relay(c, k))

    def stay(c):
        def per_owner(i, carry):
            p = lax.rem(lon + i, NP)
            dst = recv.at[lon, pl.ds(c * CR, CR)]
            half = pl.ds(pl.multiple_of(lax.rem(p, 2) * 8, 8), 8)
            for k in range(4):
                src = sources[k].at[pl.ds(c * CR, CR), half]

                @pl.when((p // 2 == k) & (p != lon))
                def _(src=src):
                    pltpu.make_async_remote_copy(
                        src_ref=src, dst_ref=dst, send_sem=fsend.at[c, p],
                        recv_sem=frecv.at[c, lon], device_id=(lat, p), device_id_type=MESH,
                    ).start()

                @pl.when((p // 2 == k) & (p == lon))
                def _(src=src):
                    pltpu.make_async_copy(src, dst, frecv.at[c, lon]).start()

            return carry

        lax.fori_loop(0, NP, per_owner, 0)

    def edge_copy(i):
        row, there, step = ((1, ROWS + 1, 15), (ROWS, 0, 1))[i]
        return pltpu.make_async_remote_copy(
            src_ref=state_ref.at[:, row], dst_ref=state_ref.at[:, there],
            send_sem=lsend.at[i], recv_sem=lrecv.at[i],
            device_id=(lax.rem(lat + step, 16), lon), device_id_type=MESH,
        )

    inner = (lat > 0, lat < 15)

    def edges_out():
        for i in range(2):
            @pl.when(inner[i])
            def _(i=i):
                edge_copy(i).start()

    def strip_copy(p, sub):
        rows = pl.ds(sub * SR, SR)
        return pltpu.make_async_remote_copy(
            src_ref=ret.at[p, rows], dst_ref=srecv.at[lon, rows], send_sem=ssend.at[sub, p],
            recv_sem=srecv_sem.at[sub, lon], device_id=(lat, p), device_id_type=MESH,
        )

    @pl.when(is_packed)
    def _():
        xs[...] = jnp.zeros_like(xs)
        for i, (src, dst) in enumerate(packs):
            pltpu.make_async_copy(src.at[lon], dst, tab_sem.at[i]).wait()
        for g in range(NP):
            whole_part(g).wait()

        def keep(sub):
            near = wp_ref[0:1, :] <= wide(lim_ref[pl.ds(sub * SR, SR)])
            far = wp_ref[1:2, :] <= wide(lim_ref[pl.ds(ROWS - SR - sub * SR, SR)])
            return near[None], far[None]

        def ahead(n, carry):
            sub = n // (NP // NG)
            base = lon + 1 + lax.rem(n, NP // NG) * NG
            for i in range(NG):
                g = lax.rem(base + i, NP)
                near = recv[g, pl.ds(sub * SR, SR)].reshape(SR * SUB, COLS)
                far = recv[g, pl.ds(ROWS - SR - sub * SR, SR)].reshape(SR * SUB, COLS)
                xs[0, i * SR * SUB : (i + 1) * SR * SUB, 0:COLS] = near
                xs[1, i * SR * SUB : (i + 1) * SR * SUB, 0:COLS] = far
            keep_near, keep_far = keep(sub)
            shape = (NG, SR, SUB, PC)
            pbuf[0, :, 0] = jnp.where(keep_near, dot3(xs[0], fhi[0], flo[0]).reshape(shape), 0.0)
            pbuf[0, :, 1] = jnp.where(keep_far, dot3(xs[1], fhi[1], flo[1]).reshape(shape), 0.0)
            for i in range(NG):
                g = lax.rem(base + i, NP)
                for j in range(SR):
                    ret[g, sub * SR + j] = pbuf[0, i, 0, j] + pbuf[0, i, 1, SR - 1 - j]

                @pl.when(lon != g)
                def _(g=g):
                    strip_copy(g, sub).start()

                @pl.when(lon == g)
                def _(g=g):
                    rows = pl.ds(sub * SR, SR)
                    pltpu.make_async_copy(ret.at[g, rows], srecv.at[g, rows], srecv_sem.at[sub, g]).start()

            return carry

        lax.fori_loop(0, NSUB * (NP // NG), ahead, 0)

        def sum_rows(p, sub):
            return ret.at[p, pl.ds(HALF + sub * SR, SR)]

        def sum_to(p, sub):
            return pltpu.make_async_remote_copy(
                src_ref=sum_rows(lon, sub), dst_ref=sum_rows(lon, sub), send_sem=asend.at[sub, p],
                recv_sem=arecv_sem.at[sub, lon], device_id=(lat, p), device_id_type=MESH,
            )

        def add_up(sub, carry):
            def wait_part(p, carry):
                ref = srecv.at[p, pl.ds(sub * SR, SR)]
                pltpu.make_async_copy(ref, ref, srecv_sem.at[sub, p]).wait()
                return carry

            lax.fori_loop(0, NP, wait_part, 0)

            def add(j, carry):
                total = srecv[0, sub * SR + j]
                for p in range(1, NP):
                    total = total + srecv[p, sub * SR + j]
                ret[lon, HALF + sub * SR + j] = total
                return carry

            lax.fori_loop(0, SR, add, 0, unroll=5)

            def send(i, carry):
                sum_to(lax.rem(lon + i, NP), sub).start()
                return carry

            lax.fori_loop(1, NP, send, 0)
            return carry

        lax.fori_loop(0, NSUB, add_up, 0)

        def out_copies(n, act):
            slot = lax.rem(n, 2)
            sub = n // (NP // NG)
            base = lon + lax.rem(n, NP // NG) * NG
            for i in range(NG):
                g = lax.rem(base + i, NP)
                for far in range(2):
                    start = ROWS - SR - sub * SR if far else sub * SR
                    act(pltpu.make_async_copy(
                        pbuf.at[slot, i, far], state_part(g, 1 + start, SR), psem.at[slot, i, far]
                    ))

        def back(n, carry):
            slot = lax.rem(n, 2)
            sub = n // (NP // NG)
            base = lon + lax.rem(n, NP // NG) * NG
            for i in range(NG):
                g = lax.rem(base + i, NP)

                @pl.when(g != lon)
                def _(g=g):
                    pltpu.make_async_copy(sum_rows(g, sub), sum_rows(g, sub), arecv_sem.at[sub, g]).wait()

                for j in range(SR):
                    spec = ret[g, HALF + sub * SR + j]
                    xs[0, (i * SR + j) * SUB : (i * SR + j + 1) * SUB, :] = spec
                    xs[1, (i * SR + SR - 1 - j) * SUB : (i * SR + SR - j) * SUB, :] = spec

            @pl.when(n >= 2)
            def _():
                out_copies(n - 2, lambda copy: copy.wait())

            @pl.when(n == 4)
            def _():
                edges_out()

            shape = (NG, SR, SUB, PC)
            for far, keep_it in enumerate(keep(sub)):
                spec = jnp.where(keep_it, xs[far].reshape(shape), 0.0).reshape(NG * SR * SUB, PC)
                pbuf[slot, :, far] = dot3(spec, ghi[far], glo[far]).reshape(shape)
            out_copies(n, lambda copy: copy.start())
            return carry

        steps = NSUB * (NP // NG)
        lax.fori_loop(0, steps, back, 0)
        for n in (steps - 2, steps - 1):
            out_copies(n, lambda copy: copy.wait())

        def sent(n, carry):
            sub = n // (NP - 1)
            p = lax.rem(lon + 1 + lax.rem(n, NP - 1), NP)
            sum_to(p, sub).wait_send()
            strip_copy(p, sub).wait_send()
            return carry

        lax.fori_loop(0, NSUB * (NP - 1), sent, 0)

    def side_copy(i):
        step = NP - 1 if i == 0 else 1
        return pltpu.make_async_remote_copy(
            src_ref=cols.at[i], dst_ref=side.at[i], send_sem=hsend.at[i], recv_sem=hrecv.at[i],
            device_id=(lat, lax.rem(lon + step, NP)), device_id_type=MESH,
        )

    own_start = jnp.where(lat == 3, ROWS // 3, 0)

    def raw_copy(g, slot, act):
        full = pltpu.make_async_copy(obuf.at[slot], state_part(g, 1, ROWS), osem.at[slot])
        some = pltpu.make_async_copy(
            obuf.at[slot, pl.ds(own_start, 2 * ROWS // 3)],
            state_part(g, 1 + own_start, 2 * ROWS // 3), osem.at[slot],
        )

        @pl.when(depth > 3)
        def _():
            act(full)

        @pl.when(depth == 3)
        def _():
            act(some)

    def raw_out(g, carry):
        slot = lax.rem(g, 2)
        half = pl.ds(pl.multiple_of(slot * 8, 8), 8)
        for k in range(4):
            @pl.when(g // 2 == k)
            def _(k=k):
                pltpu.make_async_copy(sources[k].at[:, half], stage.at[slot], stage_sem.at[slot]).start()

        @pl.when(g >= 2)
        def _():
            raw_copy(g - 2, slot, lambda copy: copy.wait())

        pltpu.make_async_copy(stage.at[slot], stage.at[slot], stage_sem.at[slot]).wait()
        lane = lax.broadcasted_iota(jnp.int32, (SUB, 128), 1)

        def insert(j, carry):
            obuf[slot, j, :, 0:COLS] = stage[slot, j]
            east = pltpu.roll(side[0, g], lax.rem(COLS - 256 + 128 - j, 128), 1)
            west = pltpu.roll(side[1, g], 127 - j, 1)
            tail = obuf[slot, j, :, 256:PC]
            tail = jnp.where(lane == COLS - 256, east, tail)
            obuf[slot, j, :, 256:PC] = jnp.where(lane == 127, west, tail)
            return carry

        lax.fori_loop(0, ROWS, insert, 0, unroll=9)
        raw_copy(g, slot, lambda copy: copy.start())
        return carry

    @pl.when(depth >= 3)
    def _():
        lane = lax.broadcasted_iota(jnp.int32, (SUB, 128), 1)
        for g in range(NP):
            slot = g % 2
            if g + 1 < NP:
                stage_copy(g + 1, 1 - slot).start()
            stage_copy(g, slot).wait()

            def gather(j, carry, slot=slot):
                head, tail = carry
                head = jnp.where(lane == j, stage[slot, j, :, 0:1], head)
                tail = jnp.where(lane == j, stage[slot, j, :, COLS - 1 : COLS], tail)
                return head, tail

            zeros = jnp.zeros((SUB, 128), F32)
            head, tail = lax.fori_loop(0, ROWS, gather, (zeros, zeros), unroll=18)
            cols[0, g] = head
            cols[1, g] = tail

        for i in range(2):
            side_copy(i).start()

        @pl.when(jnp.logical_not(is_off))
        def _():
            for i in range(2):
                side_copy(i).wait()
            lax.fori_loop(0, NP, raw_out, 0)

    @pl.when(is_value | is_off)
    def _():
        half = np.float32(np.sqrt(0.5))

        def chunk(c, carry):
            def arrived(s, carry):
                ref = recv.at[s, pl.ds(c * CR, CR)]
                pltpu.make_async_copy(ref, ref, frecv.at[c, s]).wait()
                return carry

            lax.fori_loop(0, NP, arrived, 0)

            def fold(r, carry):
                rows = pl.ds(pl.multiple_of(r * SUB, SUB), SUB)
                x = [recv[s, c * CR + r] for s in range(NP)]
                s0, s1, s2, s3 = [x[j] + x[j + 4] for j in range(4)]
                d0, d1, d2, d3 = [x[j] - x[j + 4] for j in range(4)]
                plus, minus = half * (d1 + d3), half * (d1 - d3)
                out = (
                    (s0 + s2) + (s1 + s3), (s0 + s2) - (s1 + s3),
                    d0 + minus, -(d2 + plus),
                    s0 - s2, s3 - s1,
                    d0 - minus, d2 - plus,
                )
                for i in range(8):
                    yb[i, rows, 0:COLS] = out[i]
                return carry

            lax.fori_loop(0, CR, fold, 0, unroll=3)
            limit = wide(lim_ref[pl.ds(c * CR, CR)])

            def group(g, carry):
                spec = dot3(yb[2 * g], thi[g, 0:PC, :], tlo[g, 0:PC, :])
                spec += dot3(yb[2 * g + 1], thi[g, PC:, :], tlo[g, PC:, :])
                spec = jnp.where(wv_ref[g] <= limit, spec.reshape(CR, SUB, PC), 0.0).reshape(CR * SUB, PC)
                zb[2 * g] = dot3(spec, uhi[g, :, 0:PC], ulo[g, :, 0:PC])
                zb[2 * g + 1] = dot3(spec, uhi[g, :, PC:], ulo[g, :, PC:])
                return carry

            lax.fori_loop(0, 4, group, 0)

            def unfold(r, carry):
                rows = pl.ds(pl.multiple_of(r * SUB, SUB), SUB)
                a0, b0, a1, b1, a2, b2, a3, b3 = [zb[i, rows, :] for i in range(8)]
                even = (a0 + b0 + a2, a0 - b0 - b2, a0 + b0 - a2, a0 - b0 + b2)
                odd = (a1 + a3, half * ((a1 - a3) - (b1 + b3)), b3 - b1, half * ((a3 - a1) - (b1 + b3)))
                for j in range(4):
                    ret[j, c * CR + r] = even[j] + odd[j]
                    ret[j + 4, c * CR + r] = even[j] - odd[j]
                return carry

            lax.fori_loop(0, CR, unfold, 0, unroll=3)

            @pl.when(served_depth >= 2)
            def _():
                lane = lax.broadcasted_iota(jnp.int32, (SUB, 128), 1)

                def select(r, carry):
                    listed = wide(lim_ref[c * CR + r]) >= 0.0
                    for p in range(NP):
                        rawp[p, :, 0:COLS] = recv[p, c * CR + r]
                    for p in range(NP):
                        east = recv[(p + 1) % NP, c * CR + r, :, 0:1]
                        west = recv[(p + 7) % NP, c * CR + r, :, COLS - 1 : COLS]
                        tail = jnp.where(lane == COLS - 256, east, rawp[p, :, 256:PC])
                        tail = jnp.where(lane == 127, west, tail)
                        raw = jnp.concatenate([rawp[p, :, 0:256], tail], axis=-1)
                        ret[p, c * CR + r] = jnp.where(listed, ret[p, c * CR + r], raw)
                    return carry

                lax.fori_loop(0, CR, select, 0, unroll=2)

            def give_back(i, carry):
                p = lax.rem(lon + i, NP)
                src = ret.at[p, pl.ds(c * CR, CR)]
                dst = state_part(lon, 1 + c * CR, CR)
                local = is_value & (p == lon)

                @pl.when(jnp.logical_not(local))
                def _():
                    pltpu.make_async_remote_copy(
                        src_ref=src, dst_ref=dst, send_sem=rsend.at[c, p],
                        recv_sem=rrecv.at[c, lon], device_id=(served, p), device_id_type=MESH,
                    ).start()

                @pl.when(local)
                def _():
                    pltpu.make_async_copy(src, dst, rrecv.at[c, lon]).start()

                return carry

            lax.fori_loop(0, NP, give_back, 0)
            return carry

        def pass_on(c):
            relay_all(c, lambda copy: copy.wait_recv())
            dst = recv.at[lon, pl.ds(c * CR, CR)]

            def home_part(p):
                return home.at[c, p // 2, :, pl.ds(pl.multiple_of(lax.rem(p, 2) * 8, 8), 8)]

            def to_owner(i, carry):
                p = lax.rem(lon + i, NP)
                pltpu.make_async_remote_copy(
                    src_ref=home_part(p), dst_ref=dst, send_sem=fsend.at[c, p],
                    recv_sem=frecv.at[c, lon], device_id=(lat, p), device_id_type=MESH,
                ).start()
                return carry

            lax.fori_loop(1, NP, to_owner, 0)
            pltpu.make_async_copy(home_part(lon), dst, frecv.at[c, lon]).start()

        n_loc = last - first

        def step(n, carry):
            @pl.when(is_value & (n < n_off))
            def _():
                @pl.when(n >= 2)
                def _():
                    relay_all(n - 2, lambda copy: copy.wait_send())

                relay_all(n, lambda copy: copy.start())

            @pl.when(is_value & (n < n_loc))
            def _():
                stay(first + n)

            @pl.when(is_off & (n < n_off))
            def _():
                pass_on(n)

            @pl.when(n == 1)
            def _():
                for i, (src, dst) in enumerate(tables):
                    pltpu.make_async_copy(src, dst, tab_sem.at[i]).wait()

            lag = jnp.where(is_off, 1, 2)

            @pl.when((n >= lag) & (n < n_loc + lag))
            def _():
                chunk(first + n - lag, 0)

            @pl.when(is_off & (n >= 1))
            def _():
                @pl.when(n == 1)
                def _():
                    for i in range(2):
                        side_copy(i).wait()

                lax.fori_loop(jnp.minimum(n - 1, NP), jnp.where(n == n_off, NP, jnp.minimum(n, NP)), raw_out, 0)

            return carry

        lax.fori_loop(0, jnp.where(is_off, n_off + 1, jnp.maximum(n_off, n_loc + 2)), step, 0)

        def returned(n, carry):
            c = first + n // NP
            p = lax.rem(n, NP)

            @pl.when(is_off | (p != lon))
            def _():
                ref = ret.at[p, pl.ds(c * CR, CR)]
                pltpu.make_async_copy(ref, ref, rsend.at[c, p]).wait()

            @pl.when(p != lon)
            def _():
                ref = recv.at[p, pl.ds(c * CR, CR)]
                pltpu.make_async_copy(ref, ref, fsend.at[c, p]).wait()

            return carry

        lax.fori_loop(0, (last - first) * NP, returned, 0)

    @pl.when(depth >= 3)
    def _():
        for slot in range(2):
            raw_copy(slot, slot, lambda copy: copy.wait())

    @pl.when(is_value)
    def _():
        def drain(m, carry):
            c = jnp.where(m == 0, begin, jnp.where(m == 1, end - 1, begin + m - 1))

            def one(p, carry):
                dst = state_part(p, 1 + c * CR, CR)
                pltpu.make_async_copy(dst, dst, rrecv.at[c, p]).wait()
                return carry

            lax.fori_loop(0, NP, one, 0)

            @pl.when(m == 1)
            def _():
                edges_out()

            return carry

        lax.fori_loop(0, end - begin, drain, 0)

        def relayed(c, carry):
            relay_all(c, lambda copy: copy.wait_send())
            return carry

        lax.fori_loop(jnp.maximum(n_off - 2, 0), n_off, relayed, 0)

    def blank(row):
        return pltpu.make_async_copy(zero, state_ref.at[:, row], zsem)

    @pl.when(depth >= 4)
    def _():
        edges_out()

    for i, row in ((0, 0), (1, ROWS + 1)):
        @pl.when(jnp.logical_not(inner[i]))
        def _(row=row):
            zero[...] = jnp.zeros_like(zero)
            blank(row).start()
            blank(row).wait()

    for i in range(2):
        @pl.when(inner[i])
        def _(i=i):
            edge_copy(i).wait_send()

        @pl.when(inner[1 - i])
        def _(i=i):
            edge_copy(i).wait_recv()


def stencil_kernel(trig_ref, state_ref, wind_out, t_out, h_out):
    base = lax.axis_index("lat") * ROWS + pl.program_id(0) * BLOCK

    def dx(a):
        return pltpu.roll(a, PC - 1, 1) - pltpu.roll(a, 1, 1)

    def one(r, carry):
        at = base + r
        cos_n, cos_s = trig_ref[0, at], trig_ref[0, at + 2]
        inv = trig_ref[1, at + 1]
        turn = 0.3 * trig_ref[2, at + 1]
        u, v, t, h = [state_ref[k, r + 1] for k in range(4)]
        un, vn, tn, hn = [state_ref[k, r] for k in range(4)]
        us, vs, ts, hs = [state_ref[k, r + 2] for k in range(4)]
        cu = (0.025 * inv) * u
        cv = 0.1 * v
        new_h = h - (0.025 * inv) * dx(u * h) - (0.1 * inv) * (vs * hs * cos_s - vn * hn * cos_n)
        new_t = t - cu * dx(t) - cv * (ts - tn)
        new_u = u - cu * dx(u) - cv * (us - un) - (0.05 * inv) * dx(h) + turn * v
        new_v = v - cu * dx(v) - cv * (vs - vn) - 0.15 * (hs - hn) - turn * u
        wind_out[0, r] = new_u[:, 0:COLS]
        wind_out[1, r] = new_v[:, 0:COLS]
        t_out[r] = new_t[:, 0:COLS]
        h_out[r] = new_h[:, 0:COLS]
        return carry

    lax.fori_loop(0, BLOCK, one, 0, unroll=True)


@functools.lru_cache(maxsize=None)
def trig_table():
    row = np.arange(-1, NLAT + 1).astype(np.float32) + np.float32(0.5)
    angle = (row * np.float32(np.pi / NLAT)).astype(np.float64)
    cos = np.sin(angle).astype(np.float32)
    sin = -np.cos(angle).astype(np.float32)
    return np.stack([cos, (1.0 / cos.astype(np.float64)).astype(np.float32), sin])


def body(winds, theta, thick, polar_rows, cutoffs):
    lat = lax.axis_index("lat")
    served = jnp.where((lat >= 4) & (lat < 8), lat - 4, jnp.where((lat >= 8) & (lat < 12), lat + 4, lat))
    rows = served * ROWS + jnp.arange(ROWS, dtype=jnp.int32)
    hits = polar_rows[None, :] == rows[:, None]
    limit = jnp.max(jnp.where(hits, cutoffs[None, :], -1), axis=1).astype(F32)
    thi, tlo, uhi, ulo, wv = value_tables()
    fhi, flo, ghi, glo, wp = packed_tables()
    vm = pl.BlockSpec(memory_space=pltpu.VMEM)
    hbm = pl.BlockSpec(memory_space=pl.ANY)
    dma = pltpu.SemaphoreType.DMA
    state = pl.pallas_call(
        filter_kernel,
        out_shape=jax.ShapeDtypeStruct((4, ROWS + 2, LEV, PC), F32),
        in_specs=[hbm, hbm, hbm, pl.BlockSpec(memory_space=pltpu.SMEM), vm, vm] + [hbm] * 8,
        out_specs=hbm,
        scratch_shapes=[
            pltpu.VMEM((ROWS, SUB, 128), F32),
            pltpu.VMEM((4, 2 * PC, PC), BF16), pltpu.VMEM((4, 2 * PC, PC), BF16),
            pltpu.VMEM((4, PC, 2 * PC), BF16), pltpu.VMEM((4, PC, 2 * PC), BF16),
            pltpu.VMEM((2, PC, PC), BF16), pltpu.VMEM((2, PC, PC), BF16),
            pltpu.VMEM((2, PC, PC), BF16), pltpu.VMEM((2, PC, PC), BF16),
            pltpu.VMEM((NP, ROWS, SUB, COLS), F32),
            pltpu.VMEM((NP, ROWS, SUB, PC), F32),
            pltpu.VMEM((NP, HALF, SUB, PC), F32),
            pltpu.VMEM((2, ROWS, SUB, COLS), F32),
            pltpu.VMEM((2, ROWS, SUB, PC), F32),
            pltpu.VMEM((2, NG, 2, SR, SUB, PC), F32),
            pltpu.VMEM((2, NG * SR * SUB, PC), F32),
            pltpu.VMEM((8, CR * SUB, PC), F32),
            pltpu.VMEM((8, CR * SUB, PC), F32),
            pltpu.VMEM((NP, SUB, PC), F32),
            pltpu.VMEM((2, NP, SUB, 128), F32),
            pltpu.VMEM((2, NP, SUB, 128), F32),
            pltpu.VMEM((4, LEV, PC), F32),
            pltpu.VMEM((max(OFF1, OFF2), 4, CR, LEV, COLS), F32),
            dma((4,)), dma((2,)),
            dma((NCH, NP)), dma((NCH, NP)), dma((NCH, NP)), dma((NCH, NP)),
            dma((NSUB, NP)), dma((NSUB, NP)), dma((NSUB, NP)), dma((NSUB, NP)),
            dma((2,)), dma((2,)), dma((2,)), dma((2,)), dma((2,)), dma,
            dma((NCH, 4)), dma((NCH, 4)), dma((NP,)), dma((2, NG, 2)),
        ],
        compiler_params=pltpu.CompilerParams(
            collective_id=1, has_side_effects=True, vmem_limit_bytes=60 * 2**20
        ),
        name="polar_filter",
    )(
        winds.transpose(0, 2, 1, 3), theta.transpose(1, 0, 2), thick.transpose(1, 0, 2), limit,
        jnp.asarray(wv)[:, None, :], jnp.asarray(wp), thi, tlo, uhi, ulo, fhi, flo, ghi, glo,
    )
    new_winds, new_t, new_h = pl.pallas_call(
        stencil_kernel,
        grid=(ROWS // BLOCK,),
        out_shape=(
            jax.ShapeDtypeStruct((2, ROWS, LEV, COLS), F32),
            jax.ShapeDtypeStruct((ROWS, LEV, COLS), F32),
            jax.ShapeDtypeStruct((ROWS, LEV, COLS), F32),
        ),
        in_specs=[
            pl.BlockSpec(memory_space=pltpu.SMEM),
            pl.BlockSpec(
                (pl.Element(4), pl.Element(BLOCK + 2), pl.Element(LEV), pl.Element(PC)),
                lambda i: (0, i * BLOCK, 0, 0),
            ),
        ],
        out_specs=(
            pl.BlockSpec((2, BLOCK, LEV, COLS), lambda i: (0, i, 0, 0)),
            pl.BlockSpec((BLOCK, LEV, COLS), lambda i: (i, 0, 0)),
            pl.BlockSpec((BLOCK, LEV, COLS), lambda i: (i, 0, 0)),
        ),
        compiler_params=pltpu.CompilerParams(vmem_limit_bytes=60 * 2**20),
        name="stencil",
    )(jnp.asarray(trig_table()), state)
    return new_winds.transpose(0, 2, 1, 3), new_t.transpose(1, 0, 2), new_h.transpose(1, 0, 2)


def solution(mesh):
    in_specs = (P(None, None, "lat", "lon"), P(None, "lat", "lon"), P(None, "lat", "lon"), P(), P())
    out_specs = (P(None, None, "lat", "lon"), P(None, "lat", "lon"), P(None, "lat", "lon"))
    return jax.shard_map(body, mesh=mesh, in_specs=in_specs, out_specs=out_specs, check_vma=False)
```
